32 devices in a mesh: seq: 8 (over z, x), tp: 4 (over y, core).
Axes of the slice: x: 2, y: 2, z: 4, core: 2. Of those that a mesh axis runs over, the one named last changes fastest.
Arguments:
- panels: bfloat16 [256, 8, 5120], P('seq', None, 'tp'), may hold values from -60 to 60
- w_merge: bfloat16 [5120, 8192], P('seq', 'tp'), may hold values from -2 to 2
- ln_gain: bfloat16 [8192], P('tp'), may hold values from 0.099609375 to 1.8984375
- w_kv: bfloat16 [8192, 1024], P('tp'), may hold values from -0.0625 to 0.0625
- page_src: int32 [256, 1], P('seq'), may hold values from 0 to 7; in each aligned block of 32 rows (0 to 31, 32 to 63, ...) at most 8 rows name the same one
- page_tile: int32 [256], P('seq'), may hold values from 0 to 31
- doc_pages: int32 [8, 4], P('seq'), may hold values from 1 to 16, 32 in all within a row
- prefix_id: int32 [32], P('seq'), may hold values from 0 to 7
- prefix_cache: bfloat16 [8, 32, 1024], P('seq', None, 'tp'), may hold values from -4 to 4
- queries: bfloat16 [32, 128, 4096], P('seq', None, 'tp'), may hold values from -9 to 9
- text_kv: bfloat16 [32, 128, 1024], P('seq', None, 'tp'), may hold values from -4 to 4
Outputs:
- attended: bfloat16 [32, 128, 4096], P('seq', None, 'tp')
- vision_kv: bfloat16 [2048, 1024], P('seq', 'tp')
The draws below stay inside these ranges and needn't reach their ends.
Inputs may be any that keep to these rules, and one draw needn't show every extreme that they name: `page_src`: in the 32 rows of one owner index (aligned blocks), no encoder index is named more than 8 times, and some encoder index is named exactly 8 times in some block.
All inputs are finite; a program needn't handle non-finite values.
Results may differ from the reference program's by a relative error of at most 0.015.
Values may be sent and summed in bfloat16 or wider, within the bound.
No kernel may reach another device: no remote copies, remote signals or barrier semaphores. Data moves between devices by JAX's collectives and lax.ppermute only.
A program may use at most 128 MiB of HBM per device.

```python
import math
import jax
import jax.numpy as jnp
import numpy as np
from jax import lax

D = 8192
VW = 5120
HD = 128
KVW = 4
GROUP = 8
PROWS = 8
PAN_DEV = 32
TILE_DEV = 32
DOC_DEV = 4
QR = 128
PR = 32
TILES = 256
PAGES = 256
VROWS = 2048
DOCS = 32
NPREF = 8
CAP = 8
MOSTP = 16
N_SEQ = 8


def draw_panels(key, part):
    base_key, row_key = jax.random.split(jax.random.fold_in(key, 3))
    row_scale = jnp.exp(jax.random.uniform(row_key, (TILES, PROWS, 1), jnp.float32) * math.log(10.0))
    base = jnp.clip(jax.random.normal(base_key, (TILES, PROWS, VW), jnp.float32), -6.0, 6.0)
    return (base * row_scale).astype(jnp.bfloat16)


def draw_w_merge(key, part):
    base_key, col_key = jax.random.split(jax.random.fold_in(key, 5))
    column = jnp.arange(D, dtype=jnp.float32) / D
    noise = jnp.exp(jax.random.uniform(col_key, (D,), jnp.float32) * math.log(10.0))
    ramp = jnp.exp(column * math.log(2.0))
    base = jnp.clip(jax.random.normal(base_key, (VW, D), jnp.float32), -4.0, 4.0) * VW ** (-0.5)
    return (base * noise[None, :] * ramp[None, :] / 3.0).astype(jnp.bfloat16)


def text_pair(key):
    query_key, kv_key = jax.random.split(jax.random.fold_in(key, 17), 2)
    query_shape = (DOCS, QR, KVW, GROUP, HD)
    kv_shape = (DOCS, QR, KVW, 2, HD)
    query = jnp.clip(jax.random.normal(query_key, query_shape, jnp.float32), -4.0, 4.0)
    pairs = jnp.clip(jax.random.normal(kv_key, kv_shape, jnp.float32), -4.0, 4.0)
    return (query.reshape(DOCS, QR, KVW * GROUP * HD), pairs.reshape(DOCS, QR, KVW * 2 * HD))


def draw_queries(key, part):
    return text_pair(key)[0].astype(jnp.bfloat16)


def draw_text_kv(key, part):
    return text_pair(key)[1].astype(jnp.bfloat16)


def set_ends(values, own_key, smallest, top_value):
    shape = values.shape
    index_at = [jax.random.randint(jax.random.fold_in(own_key, axis), (), 0, shape[axis]) for axis in range(len(shape))]
    values = values.at[tuple(index_at)].set(smallest)
    longest = shape.index(max(shape))
    index_at[longest] = (index_at[longest] + 1) % shape[longest]
    return values.at[tuple(index_at)].set(top_value)


def levels(rng, shape, shards, least, high):
    factor_of, own = 1.0, jax.random.fold_in(rng, 6)
    for axis_at, blocks in shards:
        draws = jnp.exp(jax.random.uniform(jax.random.fold_in(own, axis_at), (blocks,), jnp.float32, least / len(shards), high / len(shards)))
        factor_of = factor_of * jnp.repeat(draws, shape[axis_at] // blocks).reshape([-1 if axis == axis_at else 1 for axis in range(len(shape))])
    return factor_of


def rank_bounds(count, lean):
    portions = [(1 << 20) // math.isqrt(standing ** lean) + 1 for standing in range(1, count + 1)]
    spread = 1 + sum(portions) // (1 << 30)
    return np.cumsum(np.array([max(1, weight // spread) for weight in portions]))


def skewed_ids(stream_key, extent, number_of, slope):
    listing = rank_bounds(number_of, slope)
    pick = jax.random.randint(jax.random.fold_in(stream_key, 1), extent, 0, int(listing[number_of - 1]))
    rank = jnp.searchsorted(jnp.asarray(listing, jnp.int32), pick, side="right")
    return jax.random.permutation(jax.random.fold_in(stream_key, 2), number_of)[rank].astype(jnp.int32)


def split_up(number_of, total, most, skew):
    weights = [(1 << 20) // math.isqrt(standing ** skew) + 1 for standing in range(2, number_of + 1)]
    spare, given = total - most - (number_of - 1), [1] * (number_of - 1)
    while spare > 0:
        candidates = [i for i in range(number_of - 1) if given[i] < most]
        mass, remaining = sum([weights[i] for i in candidates]), spare
        for i in candidates:
            extra = min(most - given[i], max(1, remaining * weights[i] // mass), spare)
            given[i] = given[i] + extra
            spare = spare - extra
    return np.array([most] + given)


def uneven(rng, number_of, total, most, lean):
    if number_of == 2:
        one = jax.random.randint(rng, (), max(1, total - most), min(most, total - 1) + 1)
        return jnp.stack([one, total - one])
    lengths = jnp.asarray(split_up(number_of, total, most, lean), jnp.int32)
    twos = (number_of - 1) // 2
    source_of, sink = lengths[1:1 + 2 * twos:2], lengths[2:2 + 2 * twos:2]
    room = jnp.minimum(source_of - 1, most - sink)
    shifted = jax.random.randint(jax.random.fold_in(rng, 1), (twos,), 0, 1 << 20) % (room + 1)
    lengths = lengths.at[1:1 + 2 * twos:2].set(source_of - shifted).at[2:2 + 2 * twos:2].set(sink + shifted)
    return lengths[jax.random.permutation(jax.random.fold_in(rng, 2), number_of)]


def deal_out(stream_key, own, number, rows, number_of, top, most, slope):
    ranking = jax.random.permutation(stream_key, number_of)
    heavy_load, common = shares(number_of, rows * top, most, slope, True), shares(number_of, rows * top, most, slope, False)
    places = jnp.arange(number_of)

    def named(lengths, offset_by):
        used = int((lengths > 0).sum())
        fixed = max(1, used // 4)
        moved = fixed + (places - fixed + offset_by * (used - fixed)) % max(1, number_of - fixed)
        return jnp.zeros((number_of,), jnp.int32).at[ranking[jnp.where(places < fixed, places, moved)]].set(jnp.asarray(lengths, jnp.int32))

    lengths = jnp.where(number % 4 == 0, named(heavy_load, number // 4), named(common, number - number // 4 - 1))
    mixed = jax.random.permutation(jax.random.fold_in(own, 3), number_of)
    giver, sink = mixed[0:number_of // 2 * 2:2], mixed[1:number_of // 2 * 2:2]
    slack = jnp.minimum(lengths[giver] - 1, most - lengths[sink]) // 2
    slack = jnp.where((giver == ranking[0]) | (sink == ranking[0]) | (lengths[sink] == 0), 0, jnp.maximum(slack, 0))
    moved = jax.random.randint(jax.random.fold_in(own, 4), (number_of // 2,), 0, 1 << 20) % (slack + 1)
    lengths = lengths.at[giver].add(-moved).at[sink].add(moved)
    items = jnp.searchsorted(jnp.cumsum(lengths), jnp.arange(rows * top), side="right").astype(jnp.int32)
    table = items.reshape(top, rows).T
    table = table[jax.random.permutation(jax.random.fold_in(own, 1), rows)]
    offset_by = jax.random.randint(jax.random.fold_in(own, 2), (rows, 1), 0, top)
    return jnp.take_along_axis(table, (jnp.arange(top)[None, :] + offset_by) % top, axis=1)


def shares(amount, total, bound, lean, full):
    loads = [(1 << 20) // math.isqrt(rank ** lean) + 1 for rank in range(1, amount + 1)]
    largest = bound if full else min(bound, max(-(-total // amount), total * loads[0] // sum(loads)))
    least = 1 if total - largest >= amount - 1 else 0
    counts, rest = [largest] + [least] * (amount - 1), total - largest - least * (amount - 1)
    while rest > 0:
        candidates = [i for i in range(1, amount) if counts[i] < largest] or [i for i in range(1, amount) if counts[i] < bound]
        mass, remaining = sum([loads[i] for i in candidates]), rest
        for i in candidates:
            addition = min(bound - counts[i], max(1, remaining * loads[i] // mass), rest)
            counts[i] = counts[i] + addition
            rest = rest - addition
    return np.array(counts)


def centred(stream_key, dims, scale, reach, cuts=(), kind=jnp.bfloat16):
    level = levels(stream_key, dims, cuts, -0.22, 0.18) if cuts else 1.0
    values = jax.random.normal(stream_key, dims, jnp.float32) * scale * level
    return jnp.minimum(jnp.maximum(values, -reach), reach).astype(kind)


def setup_inputs(seed: int = 0) -> dict:
    key_list = jax.random.split(jax.random.key(seed), 12)
    panels = draw_panels(jax.random.fold_in(key_list[11], 71), 0)
    w_merge = draw_w_merge(jax.random.fold_in(key_list[11], 71), 0)
    ln_gain = jnp.clip(1.0 + 0.18 * jax.random.normal(key_list[2], (D,), jnp.float32), 0.099609375, 1.8984375).astype(jnp.bfloat16)
    w_kv = centred(key_list[3], (D, KVW * 2 * HD), D ** -0.5, 0.0625, ((0, 4),))
    page_src_keys = jax.random.split(jax.random.fold_in(key_list[4], 1), PAGES // PAN_DEV)
    page_src_turns = jax.random.permutation(jax.random.fold_in(key_list[4], 3), PAGES // PAN_DEV)
    page_src = jax.vmap(lambda own, number: deal_out(jax.random.fold_in(key_list[4], 2), own, number, PAN_DEV, N_SEQ, 1, CAP, 2))(page_src_keys, page_src_turns).reshape((PAGES, 1))
    page_tile = set_ends(jax.random.randint(key_list[5], (PAGES,), 0, TILE_DEV), jax.random.fold_in(key_list[5], 1), 0, TILE_DEV - 1).astype(jnp.int32)
    doc_pages = jax.vmap(lambda own: uneven(own, DOC_DEV, PAN_DEV, MOSTP, 2))(jax.random.split(key_list[6], N_SEQ)).reshape((N_SEQ, DOC_DEV)).astype(jnp.int32)
    prefix_id = set_ends(skewed_ids(key_list[7], (DOCS,), NPREF, 2), jax.random.fold_in(key_list[7], 3), 0, NPREF - 1).astype(jnp.int32)
    prefix_cache = centred(key_list[8], (NPREF, PR, KVW * 2 * HD), 1.0, 4.0, ((0, 8), (2, 4)))
    queries = draw_queries(jax.random.fold_in(key_list[11], 71), 0)
    text_kv = draw_text_kv(jax.random.fold_in(key_list[11], 71), 0)
    return dict(panels=panels, w_merge=w_merge, ln_gain=ln_gain, w_kv=w_kv, page_src=page_src, page_tile=page_tile, doc_pages=doc_pages, prefix_id=prefix_id, prefix_cache=prefix_cache, queries=queries, text_kv=text_kv)


def reference(panels, w_merge, ln_gain, w_kv, page_src, page_tile, doc_pages, prefix_id, prefix_cache, queries, text_kv):
    tile_rows = panels.reshape(TILES * PROWS, VW)
    merged_tiles = jnp.dot(tile_rows, w_merge, preferred_element_type=jnp.float32).astype(jnp.bfloat16)
    merged_tiles = merged_tiles.reshape(TILES, PROWS, D)
    chosen = (page_src[:, 0] * TILE_DEV + page_tile).astype(jnp.int32)
    merged = merged_tiles[chosen].reshape(VROWS, D).astype(jnp.float32)
    mean_square = lax.optimization_barrier(jnp.mean(merged * merged, axis=1, keepdims=True))
    normed = (merged * ln_gain.astype(jnp.float32)[None, :] * lax.rsqrt(mean_square + 1e-06)).astype(jnp.bfloat16)
    vision_kv = jnp.dot(normed, w_kv, preferred_element_type=jnp.float32).astype(jnp.bfloat16)
    vision_all = vision_kv.reshape(N_SEQ, PAN_DEV * PROWS, KVW, 2, HD)
    scale = HD ** (-0.5)
    page_of_row = jnp.arange(PAN_DEV * PROWS, dtype=jnp.int32) // PROWS
    text_rows = jnp.arange(QR, dtype=jnp.int32)
    causal = text_rows[None, :] <= text_rows[:, None]

    def one_doc(doc):
        holder = doc // DOC_DEV
        within = doc % DOC_DEV
        vision = vision_all[holder]
        ends = jnp.cumsum(doc_pages[holder])
        row_doc = lax.optimization_barrier(jnp.sum((page_of_row[:, None] >= ends[None, :]).astype(jnp.int32), axis=1))
        prefix = prefix_cache[prefix_id[doc]].reshape(PR, KVW, 2, HD)
        own = text_kv[doc].reshape(QR, KVW, 2, HD)
        keys = jnp.concatenate([prefix, vision, own], axis=0).astype(jnp.float32)
        mask = jnp.concatenate([jnp.ones((QR, PR), dtype=bool), jnp.broadcast_to((row_doc == within)[None, :], (QR, PAN_DEV * PROWS)), causal], axis=1)
        query = queries[doc].reshape(QR, KVW, GROUP, HD).astype(jnp.float32)
        scores = jnp.einsum('qhgc,khc->hgqk', query, keys[:, :, 0]) * scale
        scores = jnp.where(mask[None, None], scores, -jnp.inf)
        best = lax.optimization_barrier(jnp.max(scores, axis=-1, keepdims=True))
        weights = jnp.exp(scores - best)
        total = lax.optimization_barrier(jnp.sum(weights, axis=-1, keepdims=True))
        rounded = lax.optimization_barrier(weights.astype(jnp.bfloat16)).astype(jnp.float32)
        accum = jnp.einsum('hgqk,khc->hgqc', rounded, keys[:, :, 1])
        result = accum / total
        return result.transpose(2, 0, 1, 3).reshape(QR, KVW * GROUP * HD).astype(jnp.bfloat16)
    attended = lax.map(one_doc, jnp.arange(DOCS, dtype=jnp.int32))
    return (attended, vision_kv)
```

```python
import jax
import jax.numpy as jnp
from jax import lax
from jax.sharding import PartitionSpec as P

D = 8192
HD = 128
GROUP = 8
CHUNKS = 2


def slot(origin, block, count):
    half = count // 2
    return ((origin ^ block) & 1) * half + origin // 2


def absorb(state, scores, valid, values, form):
    best, total, accum = state
    masked = jnp.where(valid, scores, -1e30)
    new_best = jnp.maximum(best, jnp.max(masked, axis=-1))
    factor = jnp.exp(best - new_best)
    weights = jnp.where(valid, jnp.exp(masked - new_best[..., None]), 0.0)
    total = total * factor + jnp.sum(weights, axis=-1)
    update = jnp.einsum(
        form, weights.astype(jnp.bfloat16), values, preferred_element_type=jnp.float32
    )
    accum = accum * factor[..., None] + update
    return (new_best, total, accum)


def merge_tiles(panels, w_merge):
    seq_count, tp_count = lax.axis_size("seq"), lax.axis_size("tp")
    width = seq_count // tp_count
    member = lax.axis_index("seq") // width
    tiles, panel_rows, depth = panels.shape
    rows = tiles * panel_rows
    local = panels.reshape(rows, depth)
    pairs = []
    for origin in range(tp_count):
        for inner in range(width):
            for block in range(tp_count):
                source = (origin * width + inner) * tp_count + block
                target = (block * width + inner) * tp_count + slot(origin, block, tp_count)
                pairs.append((source, target))
    moved = lax.ppermute(local, ("seq", "tp"), pairs)
    gathered = lax.all_gather(moved, "tp", axis=0, tiled=True)
    swapped = jnp.roll(gathered, rows * tp_count // 2, axis=0)
    ordered = jnp.where(member % 2 == 1, swapped, gathered)
    ordered = ordered.reshape(2, tp_count // 2, rows, depth).swapaxes(0, 1)
    ordered = ordered.reshape(tp_count * rows, depth)
    inner_groups = [[g * width + i for i in range(width)] for g in range(tp_count)]
    outer_groups = [[g * width + i for g in range(tp_count)] for i in range(width)]
    pieces = []
    columns = w_merge.shape[1] // CHUNKS
    for chunk in range(CHUNKS):
        weights = lax.all_gather(
            w_merge[:, chunk * columns : (chunk + 1) * columns],
            "seq",
            axis=0,
            tiled=True,
            axis_index_groups=inner_groups,
        )
        partial = jnp.dot(ordered, weights, preferred_element_type=jnp.float32)
        pieces.append(
            lax.psum_scatter(
                partial.astype(jnp.bfloat16),
                "seq",
                scatter_dimension=0,
                tiled=True,
                axis_index_groups=outer_groups,
            )
        )
    return jnp.concatenate(pieces, axis=1)


def shards(
    panels,
    w_merge,
    ln_gain,
    w_kv,
    page_src,
    page_tile,
    doc_pages,
    prefix_id,
    prefix_cache,
    queries,
    text_kv,
):
    tile_count, panel_rows, _ = panels.shape
    merged = merge_tiles(panels, w_merge)
    merged_float = merged.astype(jnp.float32)
    squares = lax.psum(jnp.sum(merged_float * merged_float, axis=1), "tp")
    row_scale = lax.rsqrt(squares / D + 1e-06)
    normed = (merged_float * ln_gain.astype(jnp.float32)[None, :] * row_scale[:, None]).astype(
        jnp.bfloat16
    )
    partial_kv = jnp.dot(normed, w_kv, preferred_element_type=jnp.float32)
    tile_kv = lax.psum_scatter(
        partial_kv.astype(jnp.bfloat16), "tp", scatter_dimension=1, tiled=True
    )
    all_kv = lax.all_gather(tile_kv, "seq", axis=0, tiled=True)
    all_kv = all_kv.reshape(-1, panel_rows, all_kv.shape[1])
    chosen = page_src[:, 0] * tile_count + page_tile
    vision_kv = all_kv[chosen].reshape(-1, all_kv.shape[2])
    doc_count, query_rows, _ = queries.shape
    heads = vision_kv.shape[1] // (2 * HD)
    query_all = queries.reshape(doc_count, query_rows, heads, GROUP, HD)
    score_scale = HD ** (-0.5)
    vision = vision_kv.reshape(-1, heads, 2, HD)
    ends = jnp.cumsum(doc_pages[0])
    page_of_row = jnp.arange(vision.shape[0], dtype=jnp.int32) // panel_rows
    row_doc = jnp.sum((page_of_row[:, None] >= ends[None, :]).astype(jnp.int32), axis=1)
    doc_index = jnp.arange(doc_count, dtype=jnp.int32)
    state = (
        jnp.full((doc_count, heads, GROUP, query_rows), -1e30, jnp.float32),
        jnp.zeros((doc_count, heads, GROUP, query_rows), jnp.float32),
        jnp.zeros((doc_count, heads, GROUP, query_rows, HD), jnp.float32),
    )
    piece = lax.all_gather(prefix_cache, "seq", axis=0, tiled=True)
    picked_blocks = piece[prefix_id].reshape(doc_count, -1, heads, 2, HD)
    scores = (
        jnp.einsum(
            "dqhgc,dkhc->dhgqk",
            query_all,
            picked_blocks[:, :, :, 0],
            preferred_element_type=jnp.float32,
        )
        * score_scale
    )
    state = absorb(state, scores, True, picked_blocks[:, :, :, 1], "dhgqk,dkhc->dhgqc")
    own = text_kv.reshape(doc_count, query_rows, heads, 2, HD)
    scores = (
        jnp.einsum(
            "dqhgc,dkhc->dhgqk", query_all, own[:, :, :, 0], preferred_element_type=jnp.float32
        )
        * score_scale
    )
    text_rows = jnp.arange(query_rows, dtype=jnp.int32)
    causal = (text_rows[None, :] <= text_rows[:, None])[None, None, None]
    state = absorb(state, scores, causal, own[:, :, :, 1], "dhgqk,dkhc->dhgqc")
    scores = (
        jnp.einsum(
            "dqhgc,khc->dhgqk", query_all, vision[:, :, 0], preferred_element_type=jnp.float32
        )
        * score_scale
    )
    valid = (row_doc[None, :] == doc_index[:, None])[:, None, None, None, :]
    state = absorb(state, scores, valid, vision[:, :, 1], "dhgqk,khc->dhgqc")
    best, total, accum = state
    result = accum / total[..., None]
    attended = (
        result.transpose(0, 3, 1, 2, 4).reshape(doc_count, query_rows, -1).astype(jnp.bfloat16)
    )
    return (attended, vision_kv)


def solution(mesh):
    return jax.shard_map(
        shards,
        mesh=mesh,
        in_specs=(
            P("seq", None, "tp"),
            P("seq", "tp"),
            P("tp"),
            P("tp", None),
            P("seq", None),
            P("seq"),
            P("seq", None),
            P("seq"),
            P("seq", None, "tp"),
            P("seq", None, "tp"),
            P("seq", None, "tp"),
        ),
        out_specs=(P("seq", None, "tp"), P("seq", "tp")),
        check_vma=False,
    )
```

```python
import functools

import jax
import jax.numpy as jnp
from jax import lax
from jax.experimental import pallas as pl
from jax.experimental.pallas import tpu as pltpu
from jax.sharding import PartitionSpec as P

D = 8192
HD = 128
GROUP = 8
MOST_PAGES = 16
CHUNKS = 4
VMEM = 48 * 1024 * 1024


def bits_of(count):
    return [1 << bit for bit in range(count.bit_length() - 1)]


def flip(value, axis, bit):
    count = lax.axis_size(axis)
    return lax.ppermute(value, axis, [(i, i ^ bit) for i in range(count)])


def transpose_panels(local):
    seq_count, tp_count = lax.axis_size("seq"), lax.axis_size("tp")
    width = seq_count // tp_count
    half = tp_count // 2
    pairs = []
    for origin in range(tp_count):
        for inner in range(width):
            for block in range(tp_count):
                source = (origin * width + inner) * tp_count + block
                slot = ((origin ^ block) & 1) * half + origin // 2
                pairs.append((source, (block * width + inner) * tp_count + slot))
    held = lax.ppermute(local, ("seq", "tp"), pairs)[None]
    bits = bits_of(tp_count)
    for bit in bits[-1:] + bits[:-1]:
        held = jnp.concatenate([held, flip(held, "tp", bit)], axis=0)
    group = lax.axis_index("seq") // width
    place = lax.axis_index("tp")
    base = 2 * (place % half) + ((place // half) ^ (group & 1))
    return held, base


def partial_kernel(base_ref, rows_ref, weights_ref, out_ref):
    out_ref[0] = jnp.dot(rows_ref[0], weights_ref[...], preferred_element_type=jnp.float32)


def partial_products(base, held, weights):
    groups, rows, depth = held.shape
    columns = weights.shape[1]
    return pl.pallas_call(
        partial_kernel,
        grid_spec=pltpu.PrefetchScalarGridSpec(
            num_scalar_prefetch=1,
            grid=(groups,),
            in_specs=[
                pl.BlockSpec((1, rows, depth), lambda i, base: (base[0] ^ i, 0, 0)),
                pl.BlockSpec((depth, columns), lambda i, base: (0, 0)),
            ],
            out_specs=pl.BlockSpec((1, rows, columns), lambda i, base: (i, 0, 0)),
        ),
        out_shape=jax.ShapeDtypeStruct((groups, rows, columns), jnp.float32),
        compiler_params=pltpu.CompilerParams(vmem_limit_bytes=VMEM),
        cost_estimate=pl.CostEstimate(
            flops=2 * groups * rows * depth * columns,
            bytes_accessed=2 * (groups * rows * depth + depth * columns)
            + 4 * groups * rows * columns,
            transcendentals=0,
        ),
    )(base.reshape(1).astype(jnp.int32), held, weights)


def reduce_groups(parts):
    seq_count, tp_count = lax.axis_size("seq"), lax.axis_size("tp")
    width = seq_count // tp_count
    group = lax.axis_index("seq") // width
    total = lax.dynamic_index_in_dim(parts, group, 0, keepdims=False)
    for sign in (1, -1):
        carried = None
        for reach in range(tp_count - 1, 0, -1):
            target = jnp.clip(group + sign * reach, 0, tp_count - 1)
            block = lax.dynamic_index_in_dim(parts, target, 0, keepdims=False)
            if carried is not None:
                block = block + carried.astype(jnp.float32)
            pairs = []
            for origin in range(tp_count):
                if 0 <= origin + sign * reach < tp_count:
                    for inner in range(width):
                        source = origin * width + inner
                        pairs.append((source, source + sign * width))
            carried = lax.ppermute(block.astype(jnp.bfloat16), "seq", pairs)
        total = total + carried.astype(jnp.float32)
    return total.astype(jnp.bfloat16)


def merge_tiles(panels, w_merge, ln_gain, w_kv):
    seq_count, tp_count = lax.axis_size("seq"), lax.axis_size("tp")
    width = seq_count // tp_count
    tiles, panel_rows, depth = panels.shape
    share = w_merge.shape[0]
    inner = lax.axis_index("seq") % width
    local = panels.reshape(tiles * panel_rows, depth)
    turned = lax.dynamic_slice_in_dim(
        jnp.concatenate([local, local], axis=1), inner * share, depth, axis=1
    )
    held, base = transpose_panels(turned)
    columns = w_merge.shape[1] // CHUNKS
    kv = 0.0
    squares = 0.0
    for chunk in range(CHUNKS):
        own = w_merge[:, chunk * columns : (chunk + 1) * columns]
        pieces = [own]
        for offset in range(1, width):
            pairs = [
                (g * width + (i + offset) % width, g * width + i)
                for g in range(tp_count)
                for i in range(width)
            ]
            pieces.append(lax.ppermute(own, "seq", pairs))
        parts = partial_products(base, held, jnp.concatenate(pieces, axis=0))
        merged = reduce_groups(parts).astype(jnp.float32)
        squares = squares + jnp.sum(merged * merged, axis=1)
        gain = ln_gain[chunk * columns : (chunk + 1) * columns].astype(jnp.float32)
        kv = kv + jnp.dot(
            (merged * gain[None, :]).astype(jnp.bfloat16),
            w_kv[chunk * columns : (chunk + 1) * columns],
            preferred_element_type=jnp.float32,
        )
    return kv, squares


def scatter_heads(kv, squares):
    tp_count = lax.axis_size("tp")
    place = lax.axis_index("tp")
    rows = kv.shape[0]
    blocks = jnp.stack(jnp.split(kv, tp_count, axis=1))
    for bit in bits_of(tp_count):
        paired = blocks.reshape(blocks.shape[0] // 2, 2, rows, blocks.shape[2])
        mine = (place // bit) % 2
        keep = lax.dynamic_index_in_dim(paired, mine, 1, keepdims=False)
        give = lax.dynamic_index_in_dim(paired, 1 - mine, 1, keepdims=False)
        blocks = keep + flip(give.astype(jnp.bfloat16), "tp", bit).astype(jnp.float32)
        squares = squares + flip(squares, "tp", bit)
    return blocks[0], squares


def share_small(prefix_cache, sources, tiles):
    rows = prefix_cache.shape[1]
    width = prefix_cache.shape[2]
    asks = jnp.stack([sources, tiles]).astype(jnp.bfloat16)
    asks = jnp.pad(asks, ((0, 14), (0, width - asks.shape[1])))
    held = jnp.concatenate([prefix_cache[0], asks], axis=0)[None]
    for bit in bits_of(lax.axis_size("seq")):
        held = jnp.concatenate([held, flip(held, "seq", bit)], axis=0)
    count = sources.shape[0]
    prefixes = held[:, :rows]
    asked_sources = held[:, rows, :count].astype(jnp.int32)
    asked_tiles = held[:, rows + 1, :count].astype(jnp.int32)
    return prefixes, asked_sources, asked_tiles


def attend_kernel(
    place_ref, query_ref, prefix_ref, text_ref, pages_ref, pick_ref, seen_ref, all_ref, out_ref, vision_ref
):
    pages = pages_ref[...]
    count = pages.shape[0]

    def pick(index):
        one_hot = lax.broadcasted_iota(jnp.int32, (index.shape[0], count), 1) == index
        one_hot = jnp.where(one_hot, 1.0, 0.0).astype(jnp.bfloat16)
        return jnp.dot(one_hot, pages, preferred_element_type=jnp.float32).astype(jnp.bfloat16)

    @pl.when(pl.program_id(0) == 0)
    def _():
        vision_ref[...] = pick(all_ref[...])

    window = pick(pick_ref[0])
    keys_values = jnp.concatenate([prefix_ref[0], window, text_ref[0]], axis=0)
    text_rows = text_ref.shape[1]
    heads = keys_values.shape[1] // (2 * HD)
    query = query_ref[0]
    for head in range(heads):
        keys = keys_values[:, 2 * head * HD : (2 * head + 1) * HD]
        values = keys_values[:, (2 * head + 1) * HD : (2 * head + 2) * HD]
        stacked = jnp.concatenate(
            [
                query[:, (head * GROUP + a) * HD : (head * GROUP + a + 1) * HD]
                for a in range(GROUP)
            ],
            axis=0,
        )
        scores = lax.dot_general(
            stacked, keys, (((1,), (1,)), ((), ())), preferred_element_type=jnp.float32
        ) * (HD**-0.5)
        row = lax.broadcasted_iota(jnp.int32, scores.shape, 0) % text_rows
        column = lax.broadcasted_iota(jnp.int32, scores.shape, 1)
        text_column = column - (scores.shape[1] - text_rows)
        allowed = (text_column <= row) & (seen_ref[0] > 0)
        scores = jnp.where(allowed, scores, -1e30)
        best = jnp.max(scores, axis=1, keepdims=True)
        weights = jnp.exp(scores - best)
        total = jnp.sum(weights, axis=1, keepdims=True)
        result = jnp.dot(weights.astype(jnp.bfloat16), values, preferred_element_type=jnp.float32)
        result = (result / total).astype(jnp.bfloat16)
        for a in range(GROUP):
            out_ref[0, :, (head * GROUP + a) * HD : (head * GROUP + a + 1) * HD] = result[
                a * text_rows : (a + 1) * text_rows
            ]


def attend(place, queries, prefixes, text_kv, pages, picks, seen, all_rows):
    docs, rows, width = queries.shape
    kv_width = text_kv.shape[2]
    vision_rows = all_rows.shape[0]
    keys = seen.shape[2]
    return pl.pallas_call(
        attend_kernel,
        grid_spec=pltpu.PrefetchScalarGridSpec(
            num_scalar_prefetch=1,
            grid=(docs,),
            in_specs=[
                pl.BlockSpec((1, rows, width), lambda d, place: (d, 0, 0)),
                pl.BlockSpec((1,) + prefixes.shape[1:], lambda d, place: (place[d], 0, 0)),
                pl.BlockSpec((1, rows, kv_width), lambda d, place: (d, 0, 0)),
                pl.BlockSpec(pages.shape, lambda d, place: (0, 0)),
                pl.BlockSpec((1,) + picks.shape[1:], lambda d, place: (d, 0, 0)),
                pl.BlockSpec((1, 1, keys), lambda d, place: (d, 0, 0)),
                pl.BlockSpec(all_rows.shape, lambda d, place: (0, 0)),
            ],
            out_specs=[
                pl.BlockSpec((1, rows, width), lambda d, place: (d, 0, 0)),
                pl.BlockSpec((vision_rows, kv_width), lambda d, place: (0, 0)),
            ],
        ),
        out_shape=[
            jax.ShapeDtypeStruct(queries.shape, jnp.bfloat16),
            jax.ShapeDtypeStruct((vision_rows, kv_width), jnp.bfloat16),
        ],
        compiler_params=pltpu.CompilerParams(vmem_limit_bytes=VMEM),
        cost_estimate=pl.CostEstimate(
            flops=4 * docs * rows * width * keys,
            bytes_accessed=8 * docs * rows * width,
            transcendentals=docs * rows * keys * width // HD,
        ),
    )(place, queries, prefixes, text_kv, pages, picks, seen, all_rows)


def shards(
    panels,
    w_merge,
    ln_gain,
    w_kv,
    page_src,
    page_tile,
    doc_pages,
    prefix_id,
    prefix_cache,
    queries,
    text_kv,
):
    seq_count = lax.axis_size("seq")
    holder = lax.axis_index("seq")
    tile_count, panel_rows, _ = panels.shape
    page_count = page_src.shape[0]
    capacity = max(2, 2 * page_count // seq_count)
    sources = page_src[:, 0]

    prefixes, asked_sources, asked_tiles = share_small(prefix_cache, sources, page_tile)
    asked = (asked_sources == holder).astype(jnp.int32)
    order = jnp.cumsum(asked, axis=1) - 1
    slots = jnp.arange(capacity, dtype=jnp.int32)
    picked = asked[:, None, :] * (order[:, None, :] == slots[None, :, None]).astype(jnp.int32)
    wanted = jnp.sum(picked * asked_tiles[:, None, :], axis=2)
    wanted = wanted[jnp.arange(seq_count, dtype=jnp.int32) ^ holder]
    within = jnp.arange(panel_rows, dtype=jnp.int32)
    wanted_rows = (wanted.reshape(-1, 1) * panel_rows + within[None, :]).reshape(-1)
    chooser = wanted_rows[:, None] == jnp.arange(tile_count * panel_rows, dtype=jnp.int32)[None, :]
    chooser = chooser.astype(jnp.bfloat16)

    position = jnp.arange(page_count, dtype=jnp.int32)
    earlier = (sources[:, None] == sources[None, :]) & (position[None, :] < position[:, None])
    rank = jnp.sum(earlier.astype(jnp.int32), axis=1)
    arrival = sources * capacity + rank
    all_rows = (arrival[:, None] * panel_rows + within[None, :]).reshape(-1, 1)
    lengths = doc_pages[0]
    starts = jnp.cumsum(lengths) - lengths
    step = jnp.arange(MOST_PAGES, dtype=jnp.int32)
    inside = step[None, :] < lengths[:, None]
    page = jnp.minimum(starts[:, None] + step[None, :], page_count - 1)
    doc_rows = arrival[page][:, :, None] * panel_rows + within[None, None, :]
    doc_rows = jnp.where(inside[:, :, None], doc_rows, -1)
    doc_count, query_rows, _ = queries.shape
    picks = doc_rows.reshape(doc_count, -1, 1)
    seen = jnp.concatenate(
        [
            jnp.ones((doc_count, prefixes.shape[1]), jnp.int32),
            (doc_rows >= 0).reshape(doc_count, -1).astype(jnp.int32),
            jnp.ones((doc_count, query_rows), jnp.int32),
        ],
        axis=1,
    )[:, None, :]

    kv, squares = merge_tiles(panels, w_merge, ln_gain, w_kv)
    kv, squares = scatter_heads(kv, squares)
    row_scale = lax.rsqrt(squares / D + 1e-06)
    tile_kv = (kv * row_scale[:, None]).astype(jnp.bfloat16)
    outgoing = jnp.dot(chooser, tile_kv, preferred_element_type=jnp.float32).astype(jnp.bfloat16)
    pages = lax.all_to_all(outgoing, "seq", split_axis=0, concat_axis=0, tiled=True)
    attended, vision_kv = attend(
        prefix_id ^ holder, queries, prefixes, text_kv, pages, picks, seen, all_rows
    )
    return (attended, vision_kv)


def solution(mesh):
    return jax.shard_map(
        shards,
        mesh=mesh,
        in_specs=(
            P("seq", None, "tp"),
            P("seq", "tp"),
            P("tp"),
            P("tp", None),
            P("seq", None),
            P("seq"),
            P("seq", None),
            P("seq"),
            P("seq", None, "tp"),
            P("seq", None, "tp"),
            P("seq", None, "tp"),
        ),
        out_specs=(P("seq", None, "tp"), P("seq", "tp")),
        check_vma=False,
    )
```

```python
import functools

import jax
import jax.numpy as jnp
from jax import lax
from jax.experimental import pallas as pl
from jax.experimental.pallas import tpu as pltpu
from jax.sharding import PartitionSpec as P

D = 8192
HD = 128
GROUP = 8
MOST_PAGES = 16
CHUNKS = 4
VMEM = 48 * 1024 * 1024


def bits_of(count):
    return [1 << bit for bit in range(count.bit_length() - 1)]


def flip(value, axis, bit):
    count = lax.axis_size(axis)
    return lax.ppermute(value, axis, [(i, i ^ bit) for i in range(count)])


def transpose_panels(local):
    seq_count, tp_count = lax.axis_size("seq"), lax.axis_size("tp")
    width = seq_count // tp_count
    half = tp_count // 2
    pairs = []
    for origin in range(tp_count):
        for inner in range(width):
            for block in range(tp_count):
                source = (origin * width + inner) * tp_count + block
                slot = ((origin ^ block) & 1) * half + origin // 2
                pairs.append((source, (block * width + inner) * tp_count + slot))
    held = [lax.ppermute(local, ("seq", "tp"), pairs)]
    bits = bits_of(tp_count)
    for bit in bits[-1:] + bits[:-1]:
        held = held + [flip(piece, "tp", bit) for piece in held]
    return held


def panel_base():
    group = lax.axis_index("seq") // (lax.axis_size("seq") // lax.axis_size("tp"))
    place = lax.axis_index("tp")
    half = lax.axis_size("tp") // 2
    return 2 * (place % half) + ((place // half) ^ (group & 1))


ROLE_GROUPS = (3, 0, 2, 1)


def partial_kernel(pieces, blocks, roles_ref, *refs):
    rows_refs = refs[: 4 * pieces]
    weights_refs = refs[4 * pieces : 4 * pieces + blocks]
    far_end, near_end, far_mid, near_mid, first, second, held = refs[4 * pieces + blocks :]
    rows = rows_refs[0].shape[0]
    for place in range(4):
        for piece in range(pieces):
            total = None
            at = 0
            for weights in weights_refs:
                depth = weights.shape[0]
                term = jnp.dot(
                    rows_refs[place * pieces + piece][:, at : at + depth],
                    weights[...],
                    preferred_element_type=jnp.float32,
                )
                total = term if total is None else total + term
                at += depth
            held[roles_ref[place], piece * rows : (piece + 1) * rows] = total
    far_end[...] = held[0]
    near_end[...] = held[1]
    far_mid[...] = held[2]
    near_mid[...] = held[3]
    first[...] = held[0].astype(jnp.bfloat16)
    second[0] = held[2].astype(jnp.bfloat16)
    second[1] = held[3].astype(jnp.bfloat16)


def partial_products(roles, held, weights):
    pieces = len(held[0])
    rows, depth = held[0][0].shape
    columns = weights[0].shape[1]
    tile = min(columns, 256)
    block_rows = pieces * rows
    one = pl.BlockSpec((block_rows, tile), lambda i, roles: (0, i))
    return pl.pallas_call(
        functools.partial(partial_kernel, pieces, len(weights)),
        grid_spec=pltpu.PrefetchScalarGridSpec(
            num_scalar_prefetch=1,
            grid=(columns // tile,),
            in_specs=[pl.BlockSpec((rows, depth), lambda i, roles: (0, 0))] * (4 * pieces)
            + [pl.BlockSpec((w.shape[0], tile), lambda i, roles: (0, i)) for w in weights],
            out_specs=[one] * 5
            + [pl.BlockSpec((2, block_rows, tile), lambda i, roles: (0, 0, i))],
            scratch_shapes=[pltpu.VMEM((4, block_rows, tile), jnp.float32)],
        ),
        out_shape=[jax.ShapeDtypeStruct((block_rows, columns), jnp.float32)] * 4
        + [
            jax.ShapeDtypeStruct((block_rows, columns), jnp.bfloat16),
            jax.ShapeDtypeStruct((2, block_rows, columns), jnp.bfloat16),
        ],
        compiler_params=pltpu.CompilerParams(vmem_limit_bytes=VMEM),
        cost_estimate=pl.CostEstimate(
            flops=8 * block_rows * depth * columns,
            bytes_accessed=8 * block_rows * depth + 2 * depth * columns + 22 * block_rows * columns,
            transcendentals=0,
        ),
    )(roles, *[piece for place in held for piece in place], *weights)


def along(pairs):
    width = lax.axis_size("seq") // lax.axis_size("tp")
    return [(a * width + i, b * width + i) for a, b in pairs for i in range(width)]


ENDS_IN = ((0, 1), (3, 2))
MIDDLES = ((1, 2), (2, 1))
ENDS_OUT = ((2, 3), (1, 0))


def reduce_groups(parts, is_end):
    far_end, near_end, far_mid, near_mid, first, second = parts
    first = lax.ppermute(first, "seq", along(ENDS_IN))
    second = lax.ppermute(second, "seq", along(ENDS_IN))
    passed = lax.ppermute(
        (far_end + first.astype(jnp.float32)).astype(jnp.bfloat16), "seq", along(MIDDLES)
    )
    crossed = lax.ppermute(
        (far_mid + second[0].astype(jnp.float32)).astype(jnp.bfloat16), "seq", along(MIDDLES)
    )
    outer = lax.ppermute(
        (near_end + passed.astype(jnp.float32)).astype(jnp.bfloat16), "seq", along(ENDS_OUT)
    )
    end = near_end + outer.astype(jnp.float32)
    middle = near_mid + second[1].astype(jnp.float32) + crossed.astype(jnp.float32)
    return jnp.where(is_end, end, middle).astype(jnp.bfloat16)


def merge_tiles(panels, w_merge, ln_gain, w_kv, small):
    seq_count, tp_count = lax.axis_size("seq"), lax.axis_size("tp")
    assert tp_count == 4 and seq_count % 4 == 0
    width = seq_count // tp_count
    tiles, panel_rows, depth = panels.shape
    share = w_merge.shape[0]
    group = lax.axis_index("seq") // width
    inner = lax.axis_index("seq") % width
    local = panels.reshape(tiles * panel_rows, depth)
    turned = lax.dynamic_slice_in_dim(
        jnp.concatenate([local, local], axis=1), inner * share, depth, axis=1
    )
    half = turned.shape[0] // 2
    held_pieces = [transpose_panels(turned[:half]), transpose_panels(turned[half:])]
    held = list(zip(*held_pieces))
    columns = w_merge.shape[1] // CHUNKS
    own_chunks = [w_merge[:, c * columns : (c + 1) * columns] for c in range(CHUNKS)]
    small = jnp.concatenate([small, flip(small, "seq", 1)], axis=0)
    own_chunks, small = lax.optimization_barrier((own_chunks, small))
    shift = jnp.where(group < 2, 0, 3)
    groups = (panel_base() ^ jnp.arange(4, dtype=jnp.int32)) ^ shift
    roles = jnp.array([ROLE_GROUPS.index(g) for g in range(4)], jnp.int32)[groups]
    is_end = (group == 0) | (group == 3)
    received = []
    for own in own_chunks:
        pieces = []
        for offset in range(1, width):
            pairs = [
                (g * width + (i + offset) % width, g * width + i)
                for g in range(tp_count)
                for i in range(width)
            ]
            pieces.append(lax.ppermute(own, "seq", pairs))
        received.append(pieces)
    _, small = lax.optimization_barrier((held_pieces[1][0], small))
    for bit in bits_of(seq_count)[1:]:
        small = jnp.concatenate([small, flip(small, "seq", bit)], axis=0)
    kv = 0.0
    squares = 0.0
    for chunk in range(CHUNKS):
        weights = [own_chunks[chunk]] + received[chunk]
        if share % 128:
            weights = [jnp.concatenate(weights, axis=0)]
        parts = partial_products(roles, held, weights)
        merged = reduce_groups(parts, is_end).astype(jnp.float32)
        squares = squares + jnp.sum(merged * merged, axis=1)
        gain = ln_gain[chunk * columns : (chunk + 1) * columns].astype(jnp.float32)
        kv = kv + jnp.dot(
            (merged * gain[None, :]).astype(jnp.bfloat16),
            w_kv[chunk * columns : (chunk + 1) * columns],
            preferred_element_type=jnp.float32,
        )
    return kv, squares, small


def scatter_heads(kv, squares):
    tp_count = lax.axis_size("tp")
    place = lax.axis_index("tp")
    rows = kv.shape[0]
    blocks = jnp.stack(jnp.split(kv, tp_count, axis=1))
    for bit in bits_of(tp_count):
        paired = blocks.reshape(blocks.shape[0] // 2, 2, rows, blocks.shape[2])
        mine = (place // bit) % 2
        keep = lax.dynamic_index_in_dim(paired, mine, 1, keepdims=False)
        give = lax.dynamic_index_in_dim(paired, 1 - mine, 1, keepdims=False)
        blocks = keep + flip(give.astype(jnp.bfloat16), "tp", bit).astype(jnp.float32)
        squares = squares + flip(squares, "tp", bit)
    return blocks[0], squares


def pack_small(prefix_cache, sources, tiles):
    width = prefix_cache.shape[2]
    asks = jnp.stack([sources, tiles]).astype(jnp.bfloat16)
    asks = jnp.pad(asks, ((0, 14), (0, width - asks.shape[1])))
    return jnp.concatenate([prefix_cache[0], asks], axis=0)[None]


def attend_kernel(
    place_ref, query_ref, prefix_ref, text_ref, pages_ref, pick_ref, seen_ref, all_ref, out_ref, vision_ref
):
    pages = pages_ref[...]
    count = pages.shape[0]

    def pick(index):
        one_hot = lax.broadcasted_iota(jnp.int32, (index.shape[0], count), 1) == index
        one_hot = jnp.where(one_hot, 1.0, 0.0).astype(jnp.bfloat16)
        return jnp.dot(one_hot, pages, preferred_element_type=jnp.float32).astype(jnp.bfloat16)

    @pl.when(pl.program_id(0) == 0)
    def _():
        vision_ref[...] = pick(all_ref[...])

    window = pick(pick_ref[0])
    keys_values = jnp.concatenate([prefix_ref[0], window, text_ref[0]], axis=0)
    text_rows = text_ref.shape[1]
    heads = keys_values.shape[1] // (2 * HD)
    query = query_ref[0]
    for head in range(heads):
        keys = keys_values[:, 2 * head * HD : (2 * head + 1) * HD]
        values = keys_values[:, (2 * head + 1) * HD : (2 * head + 2) * HD]
        stacked = jnp.concatenate(
            [
                query[:, (head * GROUP + a) * HD : (head * GROUP + a + 1) * HD]
                for a in range(GROUP)
            ],
            axis=0,
        )
        scores = lax.dot_general(
            stacked, keys, (((1,), (1,)), ((), ())), preferred_element_type=jnp.float32
        ) * (HD**-0.5)
        row = lax.broadcasted_iota(jnp.int32, scores.shape, 0) % text_rows
        column = lax.broadcasted_iota(jnp.int32, scores.shape, 1)
        text_column = column - (scores.shape[1] - text_rows)
        allowed = (text_column <= row) & (seen_ref[0] > 0)
        scores = jnp.where(allowed, scores, -1e30)
        best = jnp.max(scores, axis=1, keepdims=True)
        weights = jnp.exp(scores - best)
        total = jnp.sum(weights, axis=1, keepdims=True)
        result = jnp.dot(weights.astype(jnp.bfloat16), values, preferred_element_type=jnp.float32)
        result = (result / total).astype(jnp.bfloat16)
        for a in range(GROUP):
            out_ref[0, :, (head * GROUP + a) * HD : (head * GROUP + a + 1) * HD] = result[
                a * text_rows : (a + 1) * text_rows
            ]


def attend(place, queries, prefixes, text_kv, pages, picks, seen, all_rows):
    docs, rows, width = queries.shape
    kv_width = text_kv.shape[2]
    vision_rows = all_rows.shape[0]
    keys = seen.shape[2]
    return pl.pallas_call(
        attend_kernel,
        grid_spec=pltpu.PrefetchScalarGridSpec(
            num_scalar_prefetch=1,
            grid=(docs,),
            in_specs=[
                pl.BlockSpec((1, rows, width), lambda d, place: (d, 0, 0)),
                pl.BlockSpec((1,) + prefixes.shape[1:], lambda d, place: (place[d], 0, 0)),
                pl.BlockSpec((1, rows, kv_width), lambda d, place: (d, 0, 0)),
                pl.BlockSpec(pages.shape, lambda d, place: (0, 0)),
                pl.BlockSpec((1,) + picks.shape[1:], lambda d, place: (d, 0, 0)),
                pl.BlockSpec((1, 1, keys), lambda d, place: (d, 0, 0)),
                pl.BlockSpec(all_rows.shape, lambda d, place: (0, 0)),
            ],
            out_specs=[
                pl.BlockSpec((1, rows, width), lambda d, place: (d, 0, 0)),
                pl.BlockSpec((vision_rows, kv_width), lambda d, place: (0, 0)),
            ],
        ),
        out_shape=[
            jax.ShapeDtypeStruct(queries.shape, jnp.bfloat16),
            jax.ShapeDtypeStruct((vision_rows, kv_width), jnp.bfloat16),
        ],
        compiler_params=pltpu.CompilerParams(vmem_limit_bytes=VMEM),
        cost_estimate=pl.CostEstimate(
            flops=4 * docs * rows * width * keys,
            bytes_accessed=8 * docs * rows * width,
            transcendentals=docs * rows * keys * width // HD,
        ),
    )(place, queries, prefixes, text_kv, pages, picks, seen, all_rows)


def shards(
    panels,
    w_merge,
    ln_gain,
    w_kv,
    page_src,
    page_tile,
    doc_pages,
    prefix_id,
    prefix_cache,
    queries,
    text_kv,
):
    seq_count = lax.axis_size("seq")
    holder = lax.axis_index("seq")
    tile_count, panel_rows, _ = panels.shape
    page_count = page_src.shape[0]
    capacity = max(2, 2 * page_count // seq_count)
    sources = page_src[:, 0]

    kv, squares, small = merge_tiles(
        panels, w_merge, ln_gain, w_kv, pack_small(prefix_cache, sources, page_tile)
    )
    prefix_rows = prefix_cache.shape[1]
    prefixes = small[:, :prefix_rows]
    asked_sources = small[:, prefix_rows, :page_count].astype(jnp.int32)
    asked_tiles = small[:, prefix_rows + 1, :page_count].astype(jnp.int32)
    asked = (asked_sources == holder).astype(jnp.int32)
    order = jnp.cumsum(asked, axis=1) - 1
    slots = jnp.arange(capacity, dtype=jnp.int32)
    picked = asked[:, None, :] * (order[:, None, :] == slots[None, :, None]).astype(jnp.int32)
    wanted = jnp.sum(picked * asked_tiles[:, None, :], axis=2)
    wanted = wanted[jnp.arange(seq_count, dtype=jnp.int32) ^ holder]
    within = jnp.arange(panel_rows, dtype=jnp.int32)
    wanted_rows = (wanted.reshape(-1, 1) * panel_rows + within[None, :]).reshape(-1)
    chooser = wanted_rows[:, None] == jnp.arange(tile_count * panel_rows, dtype=jnp.int32)[None, :]
    chooser = chooser.astype(jnp.bfloat16)

    position = jnp.arange(page_count, dtype=jnp.int32)
    earlier = (sources[:, None] == sources[None, :]) & (position[None, :] < position[:, None])
    rank = jnp.sum(earlier.astype(jnp.int32), axis=1)
    arrival = sources * capacity + rank
    all_rows = (arrival[:, None] * panel_rows + within[None, :]).reshape(-1, 1)
    lengths = doc_pages[0]
    starts = jnp.cumsum(lengths) - lengths
    step = jnp.arange(MOST_PAGES, dtype=jnp.int32)
    inside = step[None, :] < lengths[:, None]
    page = jnp.minimum(starts[:, None] + step[None, :], page_count - 1)
    doc_rows = arrival[page][:, :, None] * panel_rows + within[None, None, :]
    doc_rows = jnp.where(inside[:, :, None], doc_rows, -1)
    doc_count, query_rows, _ = queries.shape
    picks = doc_rows.reshape(doc_count, -1, 1)
    seen = jnp.concatenate(
        [
            jnp.ones((doc_count, prefixes.shape[1]), jnp.int32),
            (doc_rows >= 0).reshape(doc_count, -1).astype(jnp.int32),
            jnp.ones((doc_count, query_rows), jnp.int32),
        ],
        axis=1,
    )[:, None, :]

    kv, squares = scatter_heads(kv, squares)
    row_scale = lax.rsqrt(squares / D + 1e-06)
    tile_kv = (kv * row_scale[:, None]).astype(jnp.bfloat16)
    outgoing = jnp.dot(chooser, tile_kv, preferred_element_type=jnp.float32).astype(jnp.bfloat16)
    pages = lax.all_to_all(outgoing, "seq", split_axis=0, concat_axis=0, tiled=True)
    attended, vision_kv = attend(
        prefix_id ^ holder, queries, prefixes, text_kv, pages, picks, seen, all_rows
    )
    return (attended, vision_kv)


def solution(mesh):
    return jax.shard_map(
        shards,
        mesh=mesh,
        in_specs=(
            P("seq", None, "tp"),
            P("seq", "tp"),
            P("tp"),
            P("tp", None),
            P("seq", None),
            P("seq"),
            P("seq", None),
            P("seq"),
            P("seq", None, "tp"),
            P("seq", None, "tp"),
            P("seq", None, "tp"),
        ),
        out_specs=(P("seq", None, "tp"), P("seq", "tp")),
        check_vma=False,
    )
```

```python
import functools

import jax
import jax.numpy as jnp
from jax import lax
from jax.experimental import pallas as pl
from jax.experimental.pallas import tpu as pltpu
from jax.sharding import PartitionSpec as P

D = 8192
HD = 128
GROUP = 8
MOST_PAGES = 16
CHUNKS = 4
VMEM = 48 * 1024 * 1024


def bits_of(count):
    return [1 << bit for bit in range(count.bit_length() - 1)]


def flip(value, axis, bit):
    count = lax.axis_size(axis)
    return lax.ppermute(value, axis, [(i, i ^ bit) for i in range(count)])


def transpose_panels(local, swap):
    seq_count, tp_count = lax.axis_size("seq"), lax.axis_size("tp")
    width = seq_count // tp_count
    half = tp_count // 2
    pairs = []
    for origin in range(tp_count):
        for inner in range(width):
            for block in range(tp_count):
                source = (origin * width + inner) * tp_count + (block ^ swap)
                slot = ((origin ^ block) & 1) * half + origin // 2
                pairs.append((source, (block * width + inner) * tp_count + slot))
    held = [lax.ppermute(local, ("seq", "tp"), pairs)]
    bits = bits_of(tp_count)
    for bit in bits[-1:] + bits[:-1]:
        held = held + [flip(piece, "tp", bit) for piece in held]
    return held


def panel_base():
    group = lax.axis_index("seq") // (lax.axis_size("seq") // lax.axis_size("tp"))
    place = lax.axis_index("tp")
    half = lax.axis_size("tp") // 2
    return 2 * (place % half) + ((place // half) ^ (group & 1))


ROLE_GROUPS = (3, 0, 2, 1)


def order_kernel(pieces, roles_ref, *refs):
    out_ref = refs[-1]
    for place in range(4):
        for piece in range(pieces):
            rows_ref = refs[place * pieces + piece]
            rows = rows_ref.shape[0]
            out_ref[roles_ref[place], piece * rows : (piece + 1) * rows] = rows_ref[...]


def order_rows(roles, held):
    pieces = len(held[0])
    rows, depth = held[0][0].shape
    return pl.pallas_call(
        functools.partial(order_kernel, pieces),
        grid_spec=pltpu.PrefetchScalarGridSpec(
            num_scalar_prefetch=1,
            grid=(1,),
            in_specs=[pl.BlockSpec((rows, depth), lambda i, roles: (0, 0))] * (4 * pieces),
            out_specs=pl.BlockSpec((4, pieces * rows, depth), lambda i, roles: (0, 0, 0)),
        ),
        out_shape=jax.ShapeDtypeStruct((4, pieces * rows, depth), jnp.bfloat16),
        compiler_params=pltpu.CompilerParams(vmem_limit_bytes=VMEM),
        cost_estimate=pl.CostEstimate(
            flops=0, bytes_accessed=16 * pieces * rows * depth, transcendentals=0
        ),
    )(roles, *[piece for place in held for piece in place])


def partial_kernel(rows_ref, weights_ref, far_end, near_end, middles):
    _, rows, depth = rows_ref.shape
    held = rows_ref[...].reshape(4 * rows, depth)
    total = jnp.dot(held, weights_ref[...], preferred_element_type=jnp.float32)
    total = total.astype(jnp.bfloat16)
    far_end[...] = total[:rows]
    near_end[...] = total[rows : 2 * rows]
    middles[0] = total[2 * rows : 3 * rows]
    middles[1] = total[3 * rows :]


def partial_products(held, weights):
    _, rows, depth = held.shape
    columns = weights.shape[1]
    tile = min(columns, 256)
    one = pl.BlockSpec((rows, tile), lambda i: (0, i))
    return pl.pallas_call(
        partial_kernel,
        grid=(columns // tile,),
        in_specs=[
            pl.BlockSpec(held.shape, lambda i: (0, 0, 0)),
            pl.BlockSpec((depth, tile), lambda i: (0, i)),
        ],
        out_specs=[one, one, pl.BlockSpec((2, rows, tile), lambda i: (0, 0, i))],
        out_shape=[jax.ShapeDtypeStruct((rows, columns), jnp.bfloat16)] * 2
        + [jax.ShapeDtypeStruct((2, rows, columns), jnp.bfloat16)],
        compiler_params=pltpu.CompilerParams(vmem_limit_bytes=VMEM),
        cost_estimate=pl.CostEstimate(
            flops=8 * rows * depth * columns,
            bytes_accessed=8 * rows * depth + 2 * depth * columns + 8 * rows * columns,
            transcendentals=0,
        ),
    )(held, weights)


def along(pairs):
    width = lax.axis_size("seq") // lax.axis_size("tp")
    return [(a * width + i, b * width + i) for a, b in pairs for i in range(width)]


ENDS_IN = ((0, 1), (3, 2))
MIDDLES = ((1, 2), (2, 1))
ENDS_OUT = ((2, 3), (1, 0))


def reduce_groups(parts, is_end):
    far_end, near_end, middles = parts

    def add(mine, other):
        return (mine.astype(jnp.float32) + other.astype(jnp.float32)).astype(jnp.bfloat16)

    first = lax.ppermute(far_end, "seq", along(ENDS_IN))
    second = lax.ppermute(middles, "seq", along(ENDS_IN))
    passed = lax.ppermute(add(far_end, first), "seq", along(MIDDLES))
    crossed = lax.ppermute(add(middles[0], second[0]), "seq", along(MIDDLES))
    outer = lax.ppermute(add(near_end, passed), "seq", along(ENDS_OUT))
    end = near_end.astype(jnp.float32) + outer.astype(jnp.float32)
    middle = (
        middles[1].astype(jnp.float32)
        + second[1].astype(jnp.float32)
        + crossed.astype(jnp.float32)
    )
    return jnp.where(is_end, end, middle).astype(jnp.bfloat16)


def merge_tiles(panels, w_merge, ln_gain, w_kv, small):
    seq_count, tp_count = lax.axis_size("seq"), lax.axis_size("tp")
    assert tp_count == 4 and seq_count % 4 == 0
    width = seq_count // tp_count
    tiles, panel_rows, depth = panels.shape
    group = lax.axis_index("seq") // width
    local = panels.reshape(tiles * panel_rows, depth)
    half = local.shape[0] // 2
    held = list(
        zip(
            transpose_panels(local[:half], 0),
            transpose_panels(flip(local[half:], "tp", 2), 2),
        )
    )
    inner_groups = [[g * width + i for i in range(width)] for g in range(tp_count)]
    columns = w_merge.shape[1] // CHUNKS
    weights = [
        lax.all_gather(
            w_merge[:, c * columns : (c + 1) * columns],
            "seq",
            axis=0,
            tiled=True,
            axis_index_groups=inner_groups,
        )
        for c in range(CHUNKS)
    ]
    for bit in bits_of(seq_count):
        small = jnp.concatenate([small, flip(small, "seq", bit)], axis=0)
    shift = jnp.where(group < 2, 0, 3)
    groups = (panel_base() ^ jnp.arange(4, dtype=jnp.int32)) ^ shift
    roles = jnp.array([ROLE_GROUPS.index(g) for g in range(4)], jnp.int32)[groups]
    is_end = (group == 0) | (group == 3)
    held = order_rows(roles, held)
    kv = 0.0
    squares = 0.0
    for chunk in range(CHUNKS):
        merged = reduce_groups(partial_products(held, weights[chunk]), is_end)
        merged = merged.astype(jnp.float32)
        squares = squares + jnp.sum(merged * merged, axis=1)
        gain = ln_gain[chunk * columns : (chunk + 1) * columns].astype(jnp.float32)
        kv = kv + jnp.dot(
            (merged * gain[None, :]).astype(jnp.bfloat16),
            w_kv[chunk * columns : (chunk + 1) * columns],
            preferred_element_type=jnp.float32,
        )
    return kv, squares, small


def scatter_heads(kv, squares):
    tp_count = lax.axis_size("tp")
    place = lax.axis_index("tp")
    rows = kv.shape[0]
    blocks = jnp.stack(jnp.split(kv, tp_count, axis=1))
    for bit in bits_of(tp_count):
        paired = blocks.reshape(blocks.shape[0] // 2, 2, rows, blocks.shape[2])
        mine = (place // bit) % 2
        keep = lax.dynamic_index_in_dim(paired, mine, 1, keepdims=False)
        give = lax.dynamic_index_in_dim(paired, 1 - mine, 1, keepdims=False)
        blocks = keep + flip(give.astype(jnp.bfloat16), "tp", bit).astype(jnp.float32)
        squares = squares + flip(squares, "tp", bit)
    return blocks[0], squares


def pack_small(prefix_cache, sources, tiles):
    width = prefix_cache.shape[2]
    asks = jnp.stack([sources, tiles]).astype(jnp.bfloat16)
    asks = jnp.pad(asks, ((0, 14), (0, width - asks.shape[1])))
    return jnp.concatenate([prefix_cache[0], asks], axis=0)[None]


def attend_kernel(
    place_ref, query_ref, prefix_ref, text_ref, pages_ref, pick_ref, seen_ref, all_ref, out_ref, vision_ref
):
    pages = pages_ref[...]
    count = pages.shape[0]

    def pick(index):
        one_hot = lax.broadcasted_iota(jnp.int32, (index.shape[0], count), 1) == index
        one_hot = jnp.where(one_hot, 1.0, 0.0).astype(jnp.bfloat16)
        return jnp.dot(one_hot, pages, preferred_element_type=jnp.float32).astype(jnp.bfloat16)

    @pl.when(pl.program_id(0) == 0)
    def _():
        vision_ref[...] = pick(all_ref[...])

    window = pick(pick_ref[0])
    keys_values = jnp.concatenate([prefix_ref[0], window, text_ref[0]], axis=0)
    text_rows = text_ref.shape[1]
    heads = keys_values.shape[1] // (2 * HD)
    query = query_ref[0]
    for head in range(heads):
        keys = keys_values[:, 2 * head * HD : (2 * head + 1) * HD]
        values = keys_values[:, (2 * head + 1) * HD : (2 * head + 2) * HD]
        stacked = jnp.concatenate(
            [
                query[:, (head * GROUP + a) * HD : (head * GROUP + a + 1) * HD]
                for a in range(GROUP)
            ],
            axis=0,
        )
        scores = lax.dot_general(
            stacked, keys, (((1,), (1,)), ((), ())), preferred_element_type=jnp.float32
        ) * (HD**-0.5)
        row = lax.broadcasted_iota(jnp.int32, scores.shape, 0) % text_rows
        column = lax.broadcasted_iota(jnp.int32, scores.shape, 1)
        text_column = column - (scores.shape[1] - text_rows)
        allowed = (text_column <= row) & (seen_ref[0] > 0)
        scores = jnp.where(allowed, scores, -1e30)
        best = jnp.max(scores, axis=1, keepdims=True)
        weights = jnp.exp(scores - best)
        total = jnp.sum(weights, axis=1, keepdims=True)
        result = jnp.dot(weights.astype(jnp.bfloat16), values, preferred_element_type=jnp.float32)
        result = (result / total).astype(jnp.bfloat16)
        for a in range(GROUP):
            out_ref[0, :, (head * GROUP + a) * HD : (head * GROUP + a + 1) * HD] = result[
                a * text_rows : (a + 1) * text_rows
            ]


def attend(place, queries, prefixes, text_kv, pages, picks, seen, all_rows):
    docs, rows, width = queries.shape
    kv_width = text_kv.shape[2]
    vision_rows = all_rows.shape[0]
    keys = seen.shape[2]
    return pl.pallas_call(
        attend_kernel,
        grid_spec=pltpu.PrefetchScalarGridSpec(
            num_scalar_prefetch=1,
            grid=(docs,),
            in_specs=[
                pl.BlockSpec((1, rows, width), lambda d, place: (d, 0, 0)),
                pl.BlockSpec((1,) + prefixes.shape[1:], lambda d, place: (place[d], 0, 0)),
                pl.BlockSpec((1, rows, kv_width), lambda d, place: (d, 0, 0)),
                pl.BlockSpec(pages.shape, lambda d, place: (0, 0)),
                pl.BlockSpec((1,) + picks.shape[1:], lambda d, place: (d, 0, 0)),
                pl.BlockSpec((1, 1, keys), lambda d, place: (d, 0, 0)),
                pl.BlockSpec(all_rows.shape, lambda d, place: (0, 0)),
            ],
            out_specs=[
                pl.BlockSpec((1, rows, width), lambda d, place: (d, 0, 0)),
                pl.BlockSpec((vision_rows, kv_width), lambda d, place: (0, 0)),
            ],
        ),
        out_shape=[
            jax.ShapeDtypeStruct(queries.shape, jnp.bfloat16),
            jax.ShapeDtypeStruct((vision_rows, kv_width), jnp.bfloat16),
        ],
        compiler_params=pltpu.CompilerParams(vmem_limit_bytes=VMEM),
        cost_estimate=pl.CostEstimate(
            flops=4 * docs * rows * width * keys,
            bytes_accessed=8 * docs * rows * width,
            transcendentals=docs * rows * keys * width // HD,
        ),
    )(place, queries, prefixes, text_kv, pages, picks, seen, all_rows)


def shards(
    panels,
    w_merge,
    ln_gain,
    w_kv,
    page_src,
    page_tile,
    doc_pages,
    prefix_id,
    prefix_cache,
    queries,
    text_kv,
):
    seq_count = lax.axis_size("seq")
    holder = lax.axis_index("seq")
    tile_count, panel_rows, _ = panels.shape
    page_count = page_src.shape[0]
    capacity = max(2, 2 * page_count // seq_count)
    sources = page_src[:, 0]

    kv, squares, small = merge_tiles(
        panels, w_merge, ln_gain, w_kv, pack_small(prefix_cache, sources, page_tile)
    )
    prefix_rows = prefix_cache.shape[1]
    prefixes = small[:, :prefix_rows]
    asked_sources = small[:, prefix_rows, :page_count].astype(jnp.int32)
    asked_tiles = small[:, prefix_rows + 1, :page_count].astype(jnp.int32)
    asked = (asked_sources == holder).astype(jnp.int32)
    order = jnp.cumsum(asked, axis=1) - 1
    slots = jnp.arange(capacity, dtype=jnp.int32)
    picked = asked[:, None, :] * (order[:, None, :] == slots[None, :, None]).astype(jnp.int32)
    wanted = jnp.sum(picked * asked_tiles[:, None, :], axis=2)
    wanted = wanted[jnp.arange(seq_count, dtype=jnp.int32) ^ holder]
    within = jnp.arange(panel_rows, dtype=jnp.int32)
    wanted_rows = (wanted.reshape(-1, 1) * panel_rows + within[None, :]).reshape(-1)
    chooser = wanted_rows[:, None] == jnp.arange(tile_count * panel_rows, dtype=jnp.int32)[None, :]
    chooser = chooser.astype(jnp.bfloat16)

    position = jnp.arange(page_count, dtype=jnp.int32)
    earlier = (sources[:, None] == sources[None, :]) & (position[None, :] < position[:, None])
    rank = jnp.sum(earlier.astype(jnp.int32), axis=1)
    arrival = sources * capacity + rank
    all_rows = (arrival[:, None] * panel_rows + within[None, :]).reshape(-1, 1)
    lengths = doc_pages[0]
    starts = jnp.cumsum(lengths) - lengths
    step = jnp.arange(MOST_PAGES, dtype=jnp.int32)
    inside = step[None, :] < lengths[:, None]
    page = jnp.minimum(starts[:, None] + step[None, :], page_count - 1)
    doc_rows = arrival[page][:, :, None] * panel_rows + within[None, None, :]
    doc_rows = jnp.where(inside[:, :, None], doc_rows, -1)
    doc_count, query_rows, _ = queries.shape
    picks = doc_rows.reshape(doc_count, -1, 1)
    seen = jnp.concatenate(
        [
            jnp.ones((doc_count, prefixes.shape[1]), jnp.int32),
            (doc_rows >= 0).reshape(doc_count, -1).astype(jnp.int32),
            jnp.ones((doc_count, query_rows), jnp.int32),
        ],
        axis=1,
    )[:, None, :]

    kv, squares = scatter_heads(kv, squares)
    row_scale = lax.rsqrt(squares / D + 1e-06)
    tile_kv = (kv * row_scale[:, None]).astype(jnp.bfloat16)
    outgoing = jnp.dot(chooser, tile_kv, preferred_element_type=jnp.float32).astype(jnp.bfloat16)
    pages = lax.all_to_all(outgoing, "seq", split_axis=0, concat_axis=0, tiled=True)
    attended, vision_kv = attend(
        prefix_id ^ holder, queries, prefixes, text_kv, pages, picks, seen, all_rows
    )
    return (attended, vision_kv)


def solution(mesh):
    return jax.shard_map(
        shards,
        mesh=mesh,
        in_specs=(
            P("seq", None, "tp"),
            P("seq", "tp"),
            P("tp"),
            P("tp", None),
            P("seq", None),
            P("seq"),
            P("seq", None),
            P("seq"),
            P("seq", None, "tp"),
            P("seq", None, "tp"),
            P("seq", None, "tp"),
        ),
        out_specs=(P("seq", None, "tp"), P("seq", "tp")),
        check_vma=False,
    )
```

```python
import functools

import jax
import jax.numpy as jnp
from jax import lax
from jax.experimental import pallas as pl
from jax.experimental.pallas import tpu as pltpu
from jax.sharding import PartitionSpec as P

D = 8192
HD = 128
GROUP = 8
MOST_PAGES = 16
CHUNKS = 4
VMEM = 48 * 1024 * 1024


def bits_of(count):
    return [1 << bit for bit in range(count.bit_length() - 1)]


def flip(value, axis, bit):
    count = lax.axis_size(axis)
    return lax.ppermute(value, axis, [(i, i ^ bit) for i in range(count)])


def transpose_panels(local, swap):
    seq_count, tp_count = lax.axis_size("seq"), lax.axis_size("tp")
    width = seq_count // tp_count
    half = tp_count // 2
    pairs = []
    for origin in range(tp_count):
        for inner in range(width):
            for block in range(tp_count):
                source = (origin * width + inner) * tp_count + (block ^ swap)
                slot = ((origin ^ block) & 1) * half + origin // 2
                pairs.append((source, (block * width + inner) * tp_count + slot))
    held = [lax.ppermute(local, ("seq", "tp"), pairs)]
    bits = bits_of(tp_count)
    for bit in bits[-1:] + bits[:-1]:
        held = held + [flip(piece, "tp", bit) for piece in held]
    return held


def panel_base():
    group = lax.axis_index("seq") // (lax.axis_size("seq") // lax.axis_size("tp"))
    place = lax.axis_index("tp")
    half = lax.axis_size("tp") // 2
    return 2 * (place % half) + ((place // half) ^ (group & 1))


ROLE_GROUPS = (3, 2, 0, 1)


def order_kernel(share, scalars_ref, *refs):
    out_ref = refs[-1]
    rows, depth = refs[0].shape
    members = depth // share
    for place in range(4):
        at = pl.ds(pl.multiple_of(scalars_ref[place] * rows, rows), rows)
        for member in range(members):
            if members == 1:
                out_ref[at, :] = refs[place][...]
            else:
                source = lax.rem(scalars_ref[4] + member, members)
                columns = pl.ds(pl.multiple_of(source * share, share), share)
                out_ref[at, member * share : (member + 1) * share] = refs[place][:, columns]


def order_rows(scalars, held, share):
    rows, depth = held[0].shape
    return pl.pallas_call(
        functools.partial(order_kernel, share),
        grid_spec=pltpu.PrefetchScalarGridSpec(
            num_scalar_prefetch=1,
            grid=(1,),
            in_specs=[pl.BlockSpec((rows, depth), lambda i, scalars: (0, 0))] * 4,
            out_specs=pl.BlockSpec((4 * rows, depth), lambda i, scalars: (0, 0)),
        ),
        out_shape=jax.ShapeDtypeStruct((4 * rows, depth), jnp.bfloat16),
        compiler_params=pltpu.CompilerParams(vmem_limit_bytes=VMEM),
        cost_estimate=pl.CostEstimate(
            flops=0, bytes_accessed=16 * rows * depth, transcendentals=0
        ),
    )(scalars, *held)


def partial_kernel(halves, *refs):
    rows_refs, weights_refs = refs[:halves], refs[halves:-2]
    far_ref, near_ref = refs[-2:]
    for half, rows_ref in enumerate(rows_refs):
        total = None
        at = 0
        for weights_ref in weights_refs:
            depth = weights_ref.shape[0]
            term = jnp.dot(
                rows_ref[:, at : at + depth],
                weights_ref[...],
                preferred_element_type=jnp.float32,
            )
            total = term if total is None else total + term
            at += depth
        total = total.astype(jnp.bfloat16)
        rows = total.shape[0] // 2
        far_ref[half * rows : (half + 1) * rows] = total[:rows]
        near_ref[half * rows : (half + 1) * rows] = total[rows:]


def partial_products(held, weights, first, count):
    rows, depth = held[0].shape
    out_rows = len(held) * rows // 2
    tile = min(count, 256)
    offset = first // tile
    out = pl.BlockSpec((out_rows, tile), lambda i: (0, i))
    return pl.pallas_call(
        functools.partial(partial_kernel, len(held)),
        grid=(count // tile,),
        in_specs=[pl.BlockSpec((rows, depth), lambda i: (0, 0))] * len(held)
        + [pl.BlockSpec((w.shape[0], tile), lambda i: (0, i + offset)) for w in weights],
        out_specs=[out, out],
        out_shape=[jax.ShapeDtypeStruct((out_rows, count), jnp.bfloat16)] * 2,
        compiler_params=pltpu.CompilerParams(vmem_limit_bytes=VMEM),
        cost_estimate=pl.CostEstimate(
            flops=4 * out_rows * depth * count,
            bytes_accessed=4 * out_rows * depth + 2 * depth * count + 4 * out_rows * count,
            transcendentals=0,
        ),
    )(*held, *weights)


def along(pairs):
    width = lax.axis_size("seq") // lax.axis_size("tp")
    return [(a * width + i, b * width + i) for a, b in pairs for i in range(width)]


ENDS_IN = ((0, 1), (3, 2))
MIDDLES = ((1, 2), (2, 1))
ENDS_OUT = ((2, 3), (1, 0))


def reduce_groups(parts):
    far, near = parts

    def add(mine, other):
        return (mine.astype(jnp.float32) + other.astype(jnp.float32)).astype(jnp.bfloat16)

    inward = lax.ppermute(far, "seq", along(ENDS_IN))
    across = lax.ppermute(add(far, inward), "seq", along(MIDDLES))
    outward = lax.ppermute(add(near, across), "seq", along(ENDS_OUT))
    return add(near, outward)


PLAN = (((0,), 0, 1), ((0,), 1, 1), ((1,), 0, 1), ((1,), 1, 1), ((0, 1), 2, 1), ((0,), 3, 1), ((1,), 3, 1))


def merge_tiles(panels, w_merge, ln_gain, w_kv, small):
    seq_count, tp_count = lax.axis_size("seq"), lax.axis_size("tp")
    assert tp_count == 4 and seq_count % 4 == 0
    width = seq_count // tp_count
    tiles, panel_rows, depth = panels.shape
    share = w_merge.shape[0]
    group = lax.axis_index("seq") // width
    inner = lax.axis_index("seq") % width
    local = panels.reshape(tiles * panel_rows, depth)
    half = local.shape[0] // 2
    pieces = [
        transpose_panels(local[:half], 0),
        transpose_panels(flip(local[half:], "tp", 2), 2),
    ]
    columns = w_merge.shape[1] // CHUNKS
    weights = []
    for chunk in range(CHUNKS):
        own = w_merge[:, chunk * columns : (chunk + 1) * columns]
        if chunk >= 2:
            own, _ = lax.optimization_barrier((own, weights[chunk - 2][1]))
        parts = [own]
        for offset in range(1, width):
            pairs = [
                (g * width + (i + offset) % width, g * width + i)
                for g in range(tp_count)
                for i in range(width)
            ]
            parts.append(lax.ppermute(own, "seq", pairs))
        weights.append(parts)
    turn = inner
    if share % 128:
        weights = [
            [parts[0], jnp.roll(jnp.concatenate(parts, axis=0), inner * share, axis=0)]
            for parts in weights
        ]
        weights = [parts[1:] for parts in weights]
        share = depth
    shift = jnp.where(group < 2, 0, 3)
    groups = (panel_base() ^ jnp.arange(4, dtype=jnp.int32)) ^ shift
    roles = jnp.array([ROLE_GROUPS.index(g) for g in range(4)], jnp.int32)[groups]
    scalars = jnp.concatenate([roles, jnp.full((4,), turn, jnp.int32)])
    held = [order_rows(scalars, piece, share) for piece in pieces]
    kv = [0.0, 0.0]
    squares = [0.0, 0.0]
    for step, (halves, first, count) in enumerate(PLAN):
        chunk_rows = [held[h] for h in halves]
        merged = reduce_groups(partial_products(chunk_rows, weights[first], 0, columns * count))
        merged = merged.astype(jnp.float32)
        at = slice(first * columns, (first + count) * columns)
        gained = (merged * ln_gain[at].astype(jnp.float32)[None, :]).astype(jnp.bfloat16)
        for i, h in enumerate(halves):
            rows = slice(i * 2 * half, (i + 1) * 2 * half)
            squares[h] = squares[h] + jnp.sum(merged[rows] * merged[rows], axis=1)
            kv[h] = kv[h] + jnp.dot(gained[rows], w_kv[at], preferred_element_type=jnp.float32)
        if step == len(PLAN) - 2:
            small, kv[0] = lax.optimization_barrier((small, kv[0]))
    for bit in bits_of(seq_count):
        small = jnp.concatenate([small, flip(small, "seq", bit)], axis=0)
    def arrange(parts):
        return jnp.concatenate([part[:half] for part in parts] + [part[half:] for part in parts])

    return arrange(kv), arrange(squares), small


def return_rows(tile_kv):
    width = lax.axis_size("seq") // lax.axis_size("tp")
    group = lax.axis_index("seq") // width
    rows = tile_kv.shape[0] // 2
    returned = lax.ppermute(tile_kv[rows:], "seq", along(ENDS_IN))
    return jnp.where((group == 0) | (group == 3), tile_kv[:rows], returned)


def scatter_heads(kv, squares):
    tp_count = lax.axis_size("tp")
    place = lax.axis_index("tp")
    rows = kv.shape[0]
    blocks = jnp.stack(jnp.split(kv, tp_count, axis=1))
    for bit in bits_of(tp_count):
        paired = blocks.reshape(blocks.shape[0] // 2, 2, rows, blocks.shape[2])
        mine = (place // bit) % 2
        keep = lax.dynamic_index_in_dim(paired, mine, 1, keepdims=False)
        give = lax.dynamic_index_in_dim(paired, 1 - mine, 1, keepdims=False)
        blocks = keep + flip(give.astype(jnp.bfloat16), "tp", bit).astype(jnp.float32)
        squares = squares + flip(squares, "tp", bit)
    return blocks[0], squares


def pack_small(prefix_cache, sources, tiles):
    width = prefix_cache.shape[2]
    asks = jnp.stack([sources, tiles]).astype(jnp.bfloat16)
    asks = jnp.pad(asks, ((0, 14), (0, width - asks.shape[1])))
    return jnp.concatenate([prefix_cache[0], asks], axis=0)[None]


def attend_kernel(
    place_ref, query_ref, prefix_ref, text_ref, pages_ref, pick_ref, seen_ref, all_ref, out_ref, vision_ref
):
    pages = pages_ref[...]
    count = pages.shape[0]

    def pick(index):
        one_hot = lax.broadcasted_iota(jnp.int32, (index.shape[0], count), 1) == index
        one_hot = jnp.where(one_hot, 1.0, 0.0).astype(jnp.bfloat16)
        return jnp.dot(one_hot, pages, preferred_element_type=jnp.float32).astype(jnp.bfloat16)

    @pl.when(pl.program_id(0) == 0)
    def _():
        vision_ref[...] = pick(all_ref[...])

    window = pick(pick_ref[0])
    keys_values = jnp.concatenate([prefix_ref[0], window, text_ref[0]], axis=0)
    text_rows = text_ref.shape[1]
    heads = keys_values.shape[1] // (2 * HD)
    query = query_ref[0]
    for head in range(heads):
        keys = keys_values[:, 2 * head * HD : (2 * head + 1) * HD]
        values = keys_values[:, (2 * head + 1) * HD : (2 * head + 2) * HD]
        stacked = jnp.concatenate(
            [
                query[:, (head * GROUP + a) * HD : (head * GROUP + a + 1) * HD]
                for a in range(GROUP)
            ],
            axis=0,
        )
        scores = lax.dot_general(
            stacked, keys, (((1,), (1,)), ((), ())), preferred_element_type=jnp.float32
        ) * (HD**-0.5)
        row = lax.broadcasted_iota(jnp.int32, scores.shape, 0) % text_rows
        column = lax.broadcasted_iota(jnp.int32, scores.shape, 1)
        text_column = column - (scores.shape[1] - text_rows)
        allowed = (text_column <= row) & (seen_ref[0] > 0)
        scores = jnp.where(allowed, scores, -1e30)
        best = jnp.max(scores, axis=1, keepdims=True)
        weights = jnp.exp(scores - best)
        total = jnp.sum(weights, axis=1, keepdims=True)
        result = jnp.dot(weights.astype(jnp.bfloat16), values, preferred_element_type=jnp.float32)
        result = (result / total).astype(jnp.bfloat16)
        for a in range(GROUP):
            out_ref[0, :, (head * GROUP + a) * HD : (head * GROUP + a + 1) * HD] = result[
                a * text_rows : (a + 1) * text_rows
            ]


def attend(place, queries, prefixes, text_kv, pages, picks, seen, all_rows):
    docs, rows, width = queries.shape
    kv_width = text_kv.shape[2]
    vision_rows = all_rows.shape[0]
    keys = seen.shape[2]
    return pl.pallas_call(
        attend_kernel,
        grid_spec=pltpu.PrefetchScalarGridSpec(
            num_scalar_prefetch=1,
            grid=(docs,),
            in_specs=[
                pl.BlockSpec((1, rows, width), lambda d, place: (d, 0, 0)),
                pl.BlockSpec((1,) + prefixes.shape[1:], lambda d, place: (place[d], 0, 0)),
                pl.BlockSpec((1, rows, kv_width), lambda d, place: (d, 0, 0)),
                pl.BlockSpec(pages.shape, lambda d, place: (0, 0)),
                pl.BlockSpec((1,) + picks.shape[1:], lambda d, place: (d, 0, 0)),
                pl.BlockSpec((1, 1, keys), lambda d, place: (d, 0, 0)),
                pl.BlockSpec(all_rows.shape, lambda d, place: (0, 0)),
            ],
            out_specs=[
                pl.BlockSpec((1, rows, width), lambda d, place: (d, 0, 0)),
                pl.BlockSpec((vision_rows, kv_width), lambda d, place: (0, 0)),
            ],
        ),
        out_shape=[
            jax.ShapeDtypeStruct(queries.shape, jnp.bfloat16),
            jax.ShapeDtypeStruct((vision_rows, kv_width), jnp.bfloat16),
        ],
        compiler_params=pltpu.CompilerParams(vmem_limit_bytes=VMEM),
        cost_estimate=pl.CostEstimate(
            flops=4 * docs * rows * width * keys,
            bytes_accessed=8 * docs * rows * width,
            transcendentals=docs * rows * keys * width // HD,
        ),
    )(place, queries, prefixes, text_kv, pages, picks, seen, all_rows)


def shards(
    panels,
    w_merge,
    ln_gain,
    w_kv,
    page_src,
    page_tile,
    doc_pages,
    prefix_id,
    prefix_cache,
    queries,
    text_kv,
):
    seq_count = lax.axis_size("seq")
    holder = lax.axis_index("seq")
    tile_count, panel_rows, _ = panels.shape
    page_count = page_src.shape[0]
    capacity = max(2, 2 * page_count // seq_count)
    sources = page_src[:, 0]

    kv, squares, small = merge_tiles(
        panels, w_merge, ln_gain, w_kv, pack_small(prefix_cache, sources, page_tile)
    )
    prefix_rows = prefix_cache.shape[1]
    prefixes = small[:, :prefix_rows]
    asked_sources = small[:, prefix_rows, :page_count].astype(jnp.int32)
    asked_tiles = small[:, prefix_rows + 1, :page_count].astype(jnp.int32)
    asked = (asked_sources == holder).astype(jnp.int32)
    order = jnp.cumsum(asked, axis=1) - 1
    slots = jnp.arange(capacity, dtype=jnp.int32)
    picked = asked[:, None, :] * (order[:, None, :] == slots[None, :, None]).astype(jnp.int32)
    wanted = jnp.sum(picked * asked_tiles[:, None, :], axis=2)
    wanted = wanted[jnp.arange(seq_count, dtype=jnp.int32) ^ holder]
    within = jnp.arange(panel_rows, dtype=jnp.int32)
    wanted_rows = (wanted.reshape(-1, 1) * panel_rows + within[None, :]).reshape(-1)
    chooser = wanted_rows[:, None] == jnp.arange(tile_count * panel_rows, dtype=jnp.int32)[None, :]
    chooser = chooser.astype(jnp.bfloat16)

    position = jnp.arange(page_count, dtype=jnp.int32)
    earlier = (sources[:, None] == sources[None, :]) & (position[None, :] < position[:, None])
    rank = jnp.sum(earlier.astype(jnp.int32), axis=1)
    arrival = sources * capacity + rank
    all_rows = (arrival[:, None] * panel_rows + within[None, :]).reshape(-1, 1)
    lengths = doc_pages[0]
    starts = jnp.cumsum(lengths) - lengths
    step = jnp.arange(MOST_PAGES, dtype=jnp.int32)
    inside = step[None, :] < lengths[:, None]
    page = jnp.minimum(starts[:, None] + step[None, :], page_count - 1)
    doc_rows = arrival[page][:, :, None] * panel_rows + within[None, None, :]
    doc_rows = jnp.where(inside[:, :, None], doc_rows, -1)
    doc_count, query_rows, _ = queries.shape
    picks = doc_rows.reshape(doc_count, -1, 1)
    seen = jnp.concatenate(
        [
            jnp.ones((doc_count, prefixes.shape[1]), jnp.int32),
            (doc_rows >= 0).reshape(doc_count, -1).astype(jnp.int32),
            jnp.ones((doc_count, query_rows), jnp.int32),
        ],
        axis=1,
    )[:, None, :]

    kv, squares = scatter_heads(kv, squares)
    row_scale = lax.rsqrt(squares / D + 1e-06)
    tile_kv = return_rows((kv * row_scale[:, None]).astype(jnp.bfloat16))
    outgoing = jnp.dot(chooser, tile_kv, preferred_element_type=jnp.float32).astype(jnp.bfloat16)
    pages = lax.all_to_all(outgoing, "seq", split_axis=0, concat_axis=0, tiled=True)
    attended, vision_kv = attend(
        prefix_id ^ holder, queries, prefixes, text_kv, pages, picks, seen, all_rows
    )
    return (attended, vision_kv)


def solution(mesh):
    return jax.shard_map(
        shards,
        mesh=mesh,
        in_specs=(
            P("seq", None, "tp"),
            P("seq", "tp"),
            P("tp"),
            P("tp", None),
            P("seq", None),
            P("seq"),
            P("seq", None),
            P("seq"),
            P("seq", None, "tp"),
            P("seq", None, "tp"),
            P("seq", None, "tp"),
        ),
        out_specs=(P("seq", None, "tp"), P("seq", "tp")),
        check_vma=False,
    )
```

```python
import functools

import jax
import jax.numpy as jnp
from jax import lax
from jax.experimental import pallas as pl
from jax.experimental.pallas import tpu as pltpu
from jax.sharding import PartitionSpec as P

D = 8192
HD = 128
GROUP = 8
MOST_PAGES = 16
VMEM = 48 * 1024 * 1024


def bits_of(count):
    return [1 << bit for bit in range(count.bit_length() - 1)]


def flip(value, axis, bit):
    count = lax.axis_size(axis)
    return lax.ppermute(value, axis, [(i, i ^ bit) for i in range(count)])


def transpose_panels(local, swap):
    seq_count, tp_count = lax.axis_size("seq"), lax.axis_size("tp")
    width = seq_count // tp_count
    half = tp_count // 2
    pairs = []
    for origin in range(tp_count):
        for inner in range(width):
            for block in range(tp_count):
                source = (origin * width + inner) * tp_count + (block ^ swap)
                slot = ((origin ^ block) & 1) * half + origin // 2
                pairs.append((source, (block * width + inner) * tp_count + slot))
    held = [lax.ppermute(local, ("seq", "tp"), pairs)]
    bits = bits_of(tp_count)
    for bit in bits[-1:] + bits[:-1]:
        held = held + [flip(piece, "tp", bit) for piece in held]
    return held


def panel_base():
    group = lax.axis_index("seq") // (lax.axis_size("seq") // lax.axis_size("tp"))
    place = lax.axis_index("tp")
    half = lax.axis_size("tp") // 2
    return 2 * (place % half) + ((place // half) ^ (group & 1))


ROLE_GROUPS = (3, 2, 0, 1)


def order_kernel(share, pieces, scalars_ref, *refs):
    out_ref = refs[-1]
    rows, depth = refs[0].shape
    members = depth // share
    for place in range(4):
        for piece in range(pieces):
            row = (scalars_ref[place] * pieces + piece) * rows
            at = pl.ds(pl.multiple_of(row, rows), rows)
            rows_ref = refs[place * pieces + piece]
            for member in range(members):
                if members == 1:
                    out_ref[at, :] = rows_ref[...]
                else:
                    source = lax.rem(scalars_ref[4] + member, members)
                    columns = pl.ds(pl.multiple_of(source * share, share), share)
                    out_ref[at, member * share : (member + 1) * share] = rows_ref[:, columns]


def order_rows(scalars, held, share):
    pieces = len(held[0])
    rows, depth = held[0][0].shape
    return pl.pallas_call(
        functools.partial(order_kernel, share, pieces),
        grid_spec=pltpu.PrefetchScalarGridSpec(
            num_scalar_prefetch=1,
            grid=(1,),
            in_specs=[pl.BlockSpec((rows, depth), lambda i, scalars: (0, 0))] * (4 * pieces),
            out_specs=pl.BlockSpec((4 * pieces * rows, depth), lambda i, scalars: (0, 0)),
        ),
        out_shape=jax.ShapeDtypeStruct((4 * pieces * rows, depth), jnp.bfloat16),
        compiler_params=pltpu.CompilerParams(vmem_limit_bytes=VMEM),
        cost_estimate=pl.CostEstimate(
            flops=0, bytes_accessed=16 * pieces * rows * depth, transcendentals=0
        ),
    )(scalars, *[piece for place in held for piece in place])


def partial_kernel(rows_ref, *refs):
    weights_refs = refs[:-2]
    far_ref, near_ref = refs[-2:]
    total = None
    at = 0
    for weights_ref in weights_refs:
        depth = weights_ref.shape[0]
        term = jnp.dot(
            rows_ref[:, at : at + depth], weights_ref[...], preferred_element_type=jnp.float32
        )
        total = term if total is None else total + term
        at += depth
    total = total.astype(jnp.bfloat16)
    rows = total.shape[0] // 2
    far_ref[...] = total[:rows]
    near_ref[...] = total[rows:]


def partial_products(held, weights, count):
    rows, depth = held.shape
    tile = min(count, 256)

    def block(used, first):
        return pl.BlockSpec((used, tile), lambda i: (0, i + first // tile))

    out = pl.BlockSpec((rows // 2, tile), lambda i: (0, i))
    return pl.pallas_call(
        partial_kernel,
        grid=(count // tile,),
        in_specs=[pl.BlockSpec((rows, depth), lambda i: (0, 0))]
        + [block(used, first) for _, used, first in weights],
        out_specs=[out, out],
        out_shape=[jax.ShapeDtypeStruct((rows // 2, count), jnp.bfloat16)] * 2,
        compiler_params=pltpu.CompilerParams(vmem_limit_bytes=VMEM),
        cost_estimate=pl.CostEstimate(
            flops=2 * rows * depth * count,
            bytes_accessed=2 * rows * depth + 2 * depth * count + 2 * rows * count,
            transcendentals=0,
        ),
    )(held, *[array for array, _, _ in weights])


def along(pairs):
    width = lax.axis_size("seq") // lax.axis_size("tp")
    return [(a * width + i, b * width + i) for a, b in pairs for i in range(width)]


ENDS_IN = ((0, 1), (3, 2))
MIDDLES = ((1, 2), (2, 1))
ENDS_OUT = ((2, 3), (1, 0))


def reduce_groups(parts, is_end, small):
    far, near = parts
    rows = far.shape[0]

    def add(mine, other):
        return (mine.astype(jnp.float32) + other[:rows].astype(jnp.float32)).astype(jnp.bfloat16)

    def send(value, extra, pairs):
        if small is not None:
            value = jnp.concatenate([value] + extra, axis=0)
        return lax.ppermute(value, "seq", along(pairs))

    def part(value, index):
        count = small.shape[0]
        return value[rows + index * count : rows + (index + 1) * count]

    message = far if small is None else jnp.concatenate([far, small], axis=0)
    inward = lax.ppermute(message, "seq", along(ENDS_IN))
    extra = [] if small is None else [part(inward, 0), small]
    across = send(add(far, inward), extra, MIDDLES)
    extra = [] if small is None else [small, part(across, 1), part(across, 0)]
    outward = send(add(near, across), extra, ENDS_OUT)
    shared = None
    if small is not None:
        at_end = [part(outward, 0), part(outward, 1), part(outward, 2)]
        at_middle = [part(inward, 0), part(across, 0), part(across, 1)]
        shared = [small] + [jnp.where(is_end, e, m) for e, m in zip(at_end, at_middle)]
    return add(near, outward), message, inward, shared


PLAN = (2, 2, 2, 1, 1)


def merge_tiles(panels, w_merge, ln_gain, w_kv, small):
    seq_count, tp_count = lax.axis_size("seq"), lax.axis_size("tp")
    assert tp_count == 4 and seq_count % 4 == 0
    width = seq_count // tp_count
    tiles, panel_rows, depth = panels.shape
    share = w_merge.shape[0]
    group = lax.axis_index("seq") // width
    inner = lax.axis_index("seq") % width
    is_end = (group == 0) | (group == 3)
    local = panels.reshape(tiles * panel_rows, depth)
    half = local.shape[0] // 2
    swapped = flip(local[half:], "tp", 2)
    pieces = [transpose_panels(local[:half], 0), transpose_panels(swapped, 2)]
    columns = w_merge.shape[1] // 2
    small = small.reshape(-1, columns)
    extra = small.shape[0]
    received = []
    for side in range(2):
        own = w_merge[:, side * columns : (side + 1) * columns]
        if side == 0:
            own = jnp.concatenate([own, small], axis=0)
        else:
            own, _ = lax.optimization_barrier((own, swapped))
        others = []
        for offset in range(1, width):
            pairs = [
                (g * width + (i + offset) % width, g * width + i)
                for g in range(tp_count)
                for i in range(width)
            ]
            others.append(lax.ppermute(own, "seq", pairs))
        received.append(others)
    small = jnp.stack([small] + [other[share : share + extra] for other in received[0]])
    small_shape = small.shape
    if width > 2 or share % 128:
        weights = []
        for side in range(2):
            own = w_merge[:, side * columns : (side + 1) * columns]
            parts = [own] + [other[:share] for other in received[side]]
            weights.append(jnp.roll(jnp.concatenate(parts, axis=0), inner * share, axis=0))
        share = depth
    shift = jnp.where(group < 2, 0, 3)
    groups = (panel_base() ^ jnp.arange(4, dtype=jnp.int32)) ^ shift
    roles = jnp.array([ROLE_GROUPS.index(g) for g in range(4)], jnp.int32)[groups]
    scalars = jnp.concatenate([roles, jnp.full((4,), inner, jnp.int32)])
    held = order_rows(scalars, list(zip(*pieces)), share)
    kv = 0.0
    squares = 0.0
    inwards = []
    first = 0
    for step, part in enumerate(PLAN):
        count = part * w_merge.shape[1] // sum(PLAN)
        side = first // columns
        inside = first - side * columns
        if share == depth:
            operands = [(weights[side], depth, inside)]
        else:
            operands = [(w_merge, share, first), (received[side][0], share, inside)]
        rows = held
        if step >= 1:
            before = (message,) + tuple(inwards[step - 2 : step - 1] if step >= 2 else ())
            rows, _ = lax.optimization_barrier((held, before))
        riding = small.reshape(-1, count) if step == 0 else None
        merged, message, inward, shared = reduce_groups(
            partial_products(rows, operands, count), is_end, riding
        )
        inwards.append(inward)
        if step == 0:
            everyone = jnp.stack(shared).reshape((4,) + small_shape)
        merged = merged.astype(jnp.float32)
        at = slice(first, first + count)
        gained = (merged * ln_gain[at].astype(jnp.float32)[None, :]).astype(jnp.bfloat16)
        squares = squares + jnp.sum(merged * merged, axis=1)
        kv = kv + jnp.dot(gained, w_kv[at], preferred_element_type=jnp.float32)
        first += count
    return kv, squares, everyone


def return_rows(tile_kv):
    width = lax.axis_size("seq") // lax.axis_size("tp")
    group = lax.axis_index("seq") // width
    rows = tile_kv.shape[0] // 2
    returned = lax.ppermute(tile_kv[rows:], "seq", along(ENDS_IN))
    return jnp.where((group == 0) | (group == 3), tile_kv[:rows], returned)


def scatter_heads(kv, squares):
    tp_count = lax.axis_size("tp")
    place = lax.axis_index("tp")
    rows = kv.shape[0]
    blocks = jnp.stack(jnp.split(kv, tp_count, axis=1))
    for bit in bits_of(tp_count):
        paired = blocks.reshape(blocks.shape[0] // 2, 2, rows, blocks.shape[2])
        mine = (place // bit) % 2
        keep = lax.dynamic_index_in_dim(paired, mine, 1, keepdims=False)
        give = lax.dynamic_index_in_dim(paired, 1 - mine, 1, keepdims=False)
        blocks = keep + flip(give.astype(jnp.bfloat16), "tp", bit).astype(jnp.float32)
        squares = squares + flip(squares, "tp", bit)
    return blocks[0], squares


SMALL_ROWS = 64


def pack_small(prefix_cache, sources, tiles):
    width = prefix_cache.shape[2]
    asks = jnp.stack([sources, tiles]).astype(jnp.bfloat16)
    rows = SMALL_ROWS - prefix_cache.shape[1]
    asks = jnp.pad(asks, ((0, rows - 2), (0, width - asks.shape[1])))
    return jnp.concatenate([prefix_cache[0], asks], axis=0)


def attend_kernel(
    place_ref, query_ref, prefix_ref, text_ref, pages_ref, pick_ref, seen_ref, all_ref, out_ref, vision_ref
):
    pages = pages_ref[...]
    count = pages.shape[0]

    def pick(index):
        one_hot = lax.broadcasted_iota(jnp.int32, (index.shape[0], count), 1) == index
        one_hot = jnp.where(one_hot, 1.0, 0.0).astype(jnp.bfloat16)
        return jnp.dot(one_hot, pages, preferred_element_type=jnp.float32).astype(jnp.bfloat16)

    @pl.when(pl.program_id(0) == 0)
    def _():
        vision_ref[...] = pick(all_ref[...])

    window = pick(pick_ref[0])
    keys_values = jnp.concatenate([prefix_ref[0], window, text_ref[0]], axis=0)
    text_rows = text_ref.shape[1]
    heads = keys_values.shape[1] // (2 * HD)
    query = query_ref[0]
    for head in range(heads):
        keys = keys_values[:, 2 * head * HD : (2 * head + 1) * HD]
        values = keys_values[:, (2 * head + 1) * HD : (2 * head + 2) * HD]
        stacked = jnp.concatenate(
            [
                query[:, (head * GROUP + a) * HD : (head * GROUP + a + 1) * HD]
                for a in range(GROUP)
            ],
            axis=0,
        )
        scores = lax.dot_general(
            stacked, keys, (((1,), (1,)), ((), ())), preferred_element_type=jnp.float32
        ) * (HD**-0.5)
        row = lax.broadcasted_iota(jnp.int32, scores.shape, 0) % text_rows
        column = lax.broadcasted_iota(jnp.int32, scores.shape, 1)
        text_column = column - (scores.shape[1] - text_rows)
        allowed = (text_column <= row) & (seen_ref[0] > 0)
        scores = jnp.where(allowed, scores, -1e30)
        best = jnp.max(scores, axis=1, keepdims=True)
        weights = jnp.exp(scores - best)
        total = jnp.sum(weights, axis=1, keepdims=True)
        result = jnp.dot(weights.astype(jnp.bfloat16), values, preferred_element_type=jnp.float32)
        result = (result / total).astype(jnp.bfloat16)
        for a in range(GROUP):
            out_ref[0, :, (head * GROUP + a) * HD : (head * GROUP + a + 1) * HD] = result[
                a * text_rows : (a + 1) * text_rows
            ]


def attend(place, queries, prefixes, text_kv, pages, picks, seen, all_rows):
    docs, rows, width = queries.shape
    kv_width = text_kv.shape[2]
    vision_rows = all_rows.shape[0]
    keys = seen.shape[2]
    return pl.pallas_call(
        attend_kernel,
        grid_spec=pltpu.PrefetchScalarGridSpec(
            num_scalar_prefetch=1,
            grid=(docs,),
            in_specs=[
                pl.BlockSpec((1, rows, width), lambda d, place: (d, 0, 0)),
                pl.BlockSpec((1,) + prefixes.shape[1:], lambda d, place: (place[d], 0, 0)),
                pl.BlockSpec((1, rows, kv_width), lambda d, place: (d, 0, 0)),
                pl.BlockSpec(pages.shape, lambda d, place: (0, 0)),
                pl.BlockSpec((1,) + picks.shape[1:], lambda d, place: (d, 0, 0)),
                pl.BlockSpec((1, 1, keys), lambda d, place: (d, 0, 0)),
                pl.BlockSpec(all_rows.shape, lambda d, place: (0, 0)),
            ],
            out_specs=[
                pl.BlockSpec((1, rows, width), lambda d, place: (d, 0, 0)),
                pl.BlockSpec((vision_rows, kv_width), lambda d, place: (0, 0)),
            ],
        ),
        out_shape=[
            jax.ShapeDtypeStruct(queries.shape, jnp.bfloat16),
            jax.ShapeDtypeStruct((vision_rows, kv_width), jnp.bfloat16),
        ],
        compiler_params=pltpu.CompilerParams(vmem_limit_bytes=VMEM),
        cost_estimate=pl.CostEstimate(
            flops=4 * docs * rows * width * keys,
            bytes_accessed=8 * docs * rows * width,
            transcendentals=docs * rows * keys * width // HD,
        ),
    )(place, queries, prefixes, text_kv, pages, picks, seen, all_rows)


def shards(
    panels,
    w_merge,
    ln_gain,
    w_kv,
    page_src,
    page_tile,
    doc_pages,
    prefix_id,
    prefix_cache,
    queries,
    text_kv,
):
    seq_count = lax.axis_size("seq")
    holder = lax.axis_index("seq")
    tile_count, panel_rows, _ = panels.shape
    page_count = page_src.shape[0]
    capacity = max(2, 2 * page_count // seq_count)
    sources = page_src[:, 0]

    kv, squares, small = merge_tiles(
        panels, w_merge, ln_gain, w_kv, pack_small(prefix_cache, sources, page_tile)
    )
    width = seq_count // lax.axis_size("tp")
    small = small.reshape(seq_count, SMALL_ROWS, -1)

    def place_of(index):
        group = (index // width) ^ (holder // width)
        return group * width + (index - holder) % width

    prefix_rows = prefix_cache.shape[1]
    prefixes = small[:, :prefix_rows]
    place = place_of(jnp.arange(seq_count, dtype=jnp.int32))
    asked_sources = small[:, prefix_rows, :page_count].astype(jnp.int32)[place]
    asked_tiles = small[:, prefix_rows + 1, :page_count].astype(jnp.int32)[place]
    asked = (asked_sources == holder).astype(jnp.int32)
    order = jnp.cumsum(asked, axis=1) - 1
    slots = jnp.arange(capacity, dtype=jnp.int32)
    picked = asked[:, None, :] * (order[:, None, :] == slots[None, :, None]).astype(jnp.int32)
    wanted = jnp.sum(picked * asked_tiles[:, None, :], axis=2)
    within = jnp.arange(panel_rows, dtype=jnp.int32)
    wanted_rows = (wanted.reshape(-1, 1) * panel_rows + within[None, :]).reshape(-1)
    chooser = wanted_rows[:, None] == jnp.arange(tile_count * panel_rows, dtype=jnp.int32)[None, :]
    chooser = chooser.astype(jnp.bfloat16)

    position = jnp.arange(page_count, dtype=jnp.int32)
    earlier = (sources[:, None] == sources[None, :]) & (position[None, :] < position[:, None])
    rank = jnp.sum(earlier.astype(jnp.int32), axis=1)
    arrival = sources * capacity + rank
    all_rows = (arrival[:, None] * panel_rows + within[None, :]).reshape(-1, 1)
    lengths = doc_pages[0]
    starts = jnp.cumsum(lengths) - lengths
    step = jnp.arange(MOST_PAGES, dtype=jnp.int32)
    inside = step[None, :] < lengths[:, None]
    page = jnp.minimum(starts[:, None] + step[None, :], page_count - 1)
    doc_rows = arrival[page][:, :, None] * panel_rows + within[None, None, :]
    doc_rows = jnp.where(inside[:, :, None], doc_rows, -1)
    doc_count, query_rows, _ = queries.shape
    picks = doc_rows.reshape(doc_count, -1, 1)
    seen = jnp.concatenate(
        [
            jnp.ones((doc_count, prefixes.shape[1]), jnp.int32),
            (doc_rows >= 0).reshape(doc_count, -1).astype(jnp.int32),
            jnp.ones((doc_count, query_rows), jnp.int32),
        ],
        axis=1,
    )[:, None, :]

    kv, squares = scatter_heads(kv, squares)
    row_scale = lax.rsqrt(squares / D + 1e-06)
    tile_kv = return_rows((kv * row_scale[:, None]).astype(jnp.bfloat16))
    outgoing = jnp.dot(chooser, tile_kv, preferred_element_type=jnp.float32).astype(jnp.bfloat16)
    pages = lax.all_to_all(outgoing, "seq", split_axis=0, concat_axis=0, tiled=True)
    attended, vision_kv = attend(
        place_of(prefix_id), queries, prefixes, text_kv, pages, picks, seen, all_rows
    )
    return (attended, vision_kv)


def solution(mesh):
    return jax.shard_map(
        shards,
        mesh=mesh,
        in_specs=(
            P("seq", None, "tp"),
            P("seq", "tp"),
            P("tp"),
            P("tp", None),
            P("seq", None),
            P("seq"),
            P("seq", None),
            P("seq"),
            P("seq", None, "tp"),
            P("seq", None, "tp"),
            P("seq", None, "tp"),
        ),
        out_specs=(P("seq", None, "tp"), P("seq", "tp")),
        check_vma=False,
    )
```

```python
import functools

import jax
import jax.numpy as jnp
from jax import lax
from jax.experimental import pallas as pl
from jax.experimental.pallas import tpu as pltpu
from jax.sharding import PartitionSpec as P

D = 8192
HD = 128
GROUP = 8
MOST_PAGES = 16
VMEM = 16 * 1024 * 1024


def bits_of(count):
    return [1 << bit for bit in range(count.bit_length() - 1)]


def flip(value, axis, bit):
    count = lax.axis_size(axis)
    return lax.ppermute(value, axis, [(i, i ^ bit) for i in range(count)])


def transpose_panels(local, swap):
    seq_count, tp_count = lax.axis_size("seq"), lax.axis_size("tp")
    width = seq_count // tp_count
    half = tp_count // 2
    pairs = []
    for origin in range(tp_count):
        for inner in range(width):
            for block in range(tp_count):
                source = (origin * width + inner) * tp_count + (block ^ swap)
                slot = ((origin ^ block) & 1) * half + origin // 2
                pairs.append((source, (block * width + inner) * tp_count + slot))
    held = [lax.ppermute(local, ("seq", "tp"), pairs)]
    bits = bits_of(tp_count)
    for bit in bits[-1:] + bits[:-1]:
        held = held + [flip(piece, "tp", bit) for piece in held]
    return held


def panel_base():
    group = lax.axis_index("seq") // (lax.axis_size("seq") // lax.axis_size("tp"))
    place = lax.axis_index("tp")
    half = lax.axis_size("tp") // 2
    return 2 * (place % half) + ((place // half) ^ (group & 1))


ROLE_GROUPS = (3, 2, 0, 1)


def order_kernel(share, pieces, scalars_ref, *refs):
    out_ref = refs[-1]
    rows, depth = refs[0].shape
    members = depth // share
    for place in range(4):
        for piece in range(pieces):
            row = (scalars_ref[place] * pieces + piece) * rows
            at = pl.ds(pl.multiple_of(row, rows), rows)
            rows_ref = refs[place * pieces + piece]
            for member in range(members):
                if members == 1:
                    out_ref[at, :] = rows_ref[...]
                else:
                    source = lax.rem(scalars_ref[4] + member, members)
                    columns = pl.ds(pl.multiple_of(source * share, share), share)
                    out_ref[at, member * share : (member + 1) * share] = rows_ref[:, columns]


def order_rows(scalars, held, share):
    pieces = len(held[0])
    rows, depth = held[0][0].shape
    return pl.pallas_call(
        functools.partial(order_kernel, share, pieces),
        grid_spec=pltpu.PrefetchScalarGridSpec(
            num_scalar_prefetch=1,
            grid=(1,),
            in_specs=[pl.BlockSpec((rows, depth), lambda i, scalars: (0, 0))] * (4 * pieces),
            out_specs=pl.BlockSpec((4 * pieces * rows, depth), lambda i, scalars: (0, 0)),
        ),
        out_shape=jax.ShapeDtypeStruct((4 * pieces * rows, depth), jnp.bfloat16),
        compiler_params=pltpu.CompilerParams(vmem_limit_bytes=VMEM),
        cost_estimate=pl.CostEstimate(
            flops=0, bytes_accessed=16 * pieces * rows * depth, transcendentals=0
        ),
    )(scalars, *[piece for place in held for piece in place])


def partial_kernel(rows_ref, *refs):
    weights_refs = refs[:-2]
    far_ref, near_ref = refs[-2:]
    total = None
    at = 0
    for weights_ref in weights_refs:
        depth = weights_ref.shape[0]
        term = jnp.dot(
            rows_ref[:, at : at + depth], weights_ref[...], preferred_element_type=jnp.float32
        )
        total = term if total is None else total + term
        at += depth
    total = total.astype(jnp.bfloat16)
    rows = total.shape[0] // 2
    far_ref[...] = total[:rows]
    near_ref[...] = total[rows:]


def partial_products(held, weights, count):
    rows, depth = held.shape
    tile = min(count, 256)

    def block(used, first):
        return pl.BlockSpec((used, tile), lambda i: (0, i + first // tile))

    out = pl.BlockSpec((rows // 2, tile), lambda i: (0, i))
    return pl.pallas_call(
        partial_kernel,
        grid=(count // tile,),
        in_specs=[pl.BlockSpec((rows, depth), lambda i: (0, 0))]
        + [block(used, first) for _, used, first in weights],
        out_specs=[out, out],
        out_shape=[jax.ShapeDtypeStruct((rows // 2, count), jnp.bfloat16)] * 2,
        compiler_params=pltpu.CompilerParams(vmem_limit_bytes=VMEM),
        cost_estimate=pl.CostEstimate(
            flops=2 * rows * depth * count,
            bytes_accessed=2 * rows * depth + 2 * depth * count + 2 * rows * count,
            transcendentals=0,
        ),
    )(held, *[array for array, _, _ in weights])


def along(pairs):
    width = lax.axis_size("seq") // lax.axis_size("tp")
    return [(a * width + i, b * width + i) for a, b in pairs for i in range(width)]


ENDS_IN = ((0, 1), (3, 2))
MIDDLES = ((1, 2), (2, 1))
ENDS_OUT = ((2, 3), (1, 0))


def reduce_groups(parts, is_end, small):
    far, near = parts
    rows = far.shape[0]

    def add(mine, other):
        return (mine.astype(jnp.float32) + other[:rows].astype(jnp.float32)).astype(jnp.bfloat16)

    def send(value, extra, pairs):
        if small is not None:
            value = jnp.concatenate([value] + extra, axis=0)
        return lax.ppermute(value, "seq", along(pairs))

    def part(value, index):
        count = small.shape[0]
        return value[rows + index * count : rows + (index + 1) * count]

    message = far if small is None else jnp.concatenate([far, small], axis=0)
    inward = lax.ppermute(message, "seq", along(ENDS_IN))
    extra = [] if small is None else [part(inward, 0), small]
    across = send(add(far, inward), extra, MIDDLES)
    extra = [] if small is None else [small, part(across, 1), part(across, 0)]
    outward = send(add(near, across), extra, ENDS_OUT)
    shared = None
    if small is not None:
        at_end = [part(outward, 0), part(outward, 1), part(outward, 2)]
        at_middle = [part(inward, 0), part(across, 0), part(across, 1)]
        shared = [small] + [jnp.where(is_end, e, m) for e, m in zip(at_end, at_middle)]
    return add(near, outward), message, inward, shared


PLAN = (2, 2, 2, 1, 1)


def merge_tiles(panels, w_merge, ln_gain, w_kv, small):
    seq_count, tp_count = lax.axis_size("seq"), lax.axis_size("tp")
    assert tp_count == 4 and seq_count % 4 == 0
    width = seq_count // tp_count
    tiles, panel_rows, depth = panels.shape
    share = w_merge.shape[0]
    group = lax.axis_index("seq") // width
    inner = lax.axis_index("seq") % width
    is_end = (group == 0) | (group == 3)
    local = panels.reshape(tiles * panel_rows, depth)
    half = local.shape[0] // 2
    swapped = flip(local[half:], "tp", 2)
    pieces = [transpose_panels(local[:half], 0), transpose_panels(swapped, 2)]
    columns = w_merge.shape[1] // 2
    small = small.reshape(-1, columns)
    extra = small.shape[0]
    received = []
    for side in range(2):
        own = w_merge[:, side * columns : (side + 1) * columns]
        if side == 0:
            own = jnp.concatenate([own, small], axis=0)
        else:
            own, _ = lax.optimization_barrier((own, swapped))
        others = []
        for offset in range(1, width):
            pairs = [
                (g * width + (i + offset) % width, g * width + i)
                for g in range(tp_count)
                for i in range(width)
            ]
            others.append(lax.ppermute(own, "seq", pairs))
        received.append(others)
    small = jnp.stack([small] + [other[share : share + extra] for other in received[0]])
    small_shape = small.shape
    if width > 2 or share % 128:
        weights = []
        for side in range(2):
            own = w_merge[:, side * columns : (side + 1) * columns]
            parts = [own] + [other[:share] for other in received[side]]
            weights.append(jnp.roll(jnp.concatenate(parts, axis=0), inner * share, axis=0))
        share = depth
    shift = jnp.where(group < 2, 0, 3)
    groups = (panel_base() ^ jnp.arange(4, dtype=jnp.int32)) ^ shift
    roles = jnp.array([ROLE_GROUPS.index(g) for g in range(4)], jnp.int32)[groups]
    scalars = jnp.concatenate([roles, jnp.full((4,), inner, jnp.int32)])
    held = order_rows(scalars, list(zip(*pieces)), share)
    kv = 0.0
    squares = 0.0
    inwards = []
    first = 0
    for step, part in enumerate(PLAN):
        count = part * w_merge.shape[1] // sum(PLAN)
        side = first // columns
        inside = first - side * columns
        if share == depth:
            operands = [(weights[side], depth, inside)]
        else:
            operands = [(w_merge, share, first), (received[side][0], share, inside)]
        rows = held
        if step >= 1:
            before = inwards[step - 2] if step >= 2 else message
            rows, _ = lax.optimization_barrier((held, before))
        riding = small.reshape(-1, count) if step == 2 else None
        merged, message, inward, shared = reduce_groups(
            partial_products(rows, operands, count), is_end, riding
        )
        inwards.append(inward)
        if step == 2:
            everyone = jnp.stack(shared).reshape((4,) + small_shape)
        merged = merged.astype(jnp.float32)
        at = slice(first, first + count)
        gained = (merged * ln_gain[at].astype(jnp.float32)[None, :]).astype(jnp.bfloat16)
        squares = squares + jnp.sum(merged * merged, axis=1)
        kv = kv + jnp.dot(gained, w_kv[at], preferred_element_type=jnp.float32)
        first += count
    return kv, squares, everyone


def return_rows(tile_kv):
    width = lax.axis_size("seq") // lax.axis_size("tp")
    group = lax.axis_index("seq") // width
    rows = tile_kv.shape[0] // 2
    returned = lax.ppermute(tile_kv[rows:], "seq", along(ENDS_IN))
    return jnp.where((group == 0) | (group == 3), tile_kv[:rows], returned)


def scatter_heads(kv, squares):
    tp_count = lax.axis_size("tp")
    place = lax.axis_index("tp")
    rows = kv.shape[0]
    blocks = jnp.stack(jnp.split(kv, tp_count, axis=1))
    for bit in bits_of(tp_count):
        paired = blocks.reshape(blocks.shape[0] // 2, 2, rows, blocks.shape[2])
        mine = (place // bit) % 2
        keep = lax.dynamic_index_in_dim(paired, mine, 1, keepdims=False)
        give = lax.dynamic_index_in_dim(paired, 1 - mine, 1, keepdims=False)
        blocks = keep + flip(give.astype(jnp.bfloat16), "tp", bit).astype(jnp.float32)
        squares = squares + flip(squares, "tp", bit)
    return blocks[0], squares


SMALL_ROWS = 64


def pack_small(prefix_cache, sources, tiles):
    width = prefix_cache.shape[2]
    asks = jnp.stack([sources, tiles]).astype(jnp.bfloat16)
    rows = SMALL_ROWS - prefix_cache.shape[1]
    asks = jnp.pad(asks, ((0, rows - 2), (0, width - asks.shape[1])))
    return jnp.concatenate([prefix_cache[0], asks], axis=0)


def attend_kernel(
    place_ref, query_ref, prefix_ref, text_ref, pages_ref, pick_ref, seen_ref, all_ref, out_ref, vision_ref
):
    pages = pages_ref[...]
    count = pages.shape[0]

    def pick(index):
        one_hot = lax.broadcasted_iota(jnp.int32, (index.shape[0], count), 1) == index
        one_hot = jnp.where(one_hot, 1.0, 0.0).astype(jnp.bfloat16)
        return jnp.dot(one_hot, pages, preferred_element_type=jnp.float32).astype(jnp.bfloat16)

    @pl.when(pl.program_id(0) == 0)
    def _():
        vision_ref[...] = pick(all_ref[...])

    window = pick(pick_ref[0])
    keys_values = jnp.concatenate([prefix_ref[0], window, text_ref[0]], axis=0)
    text_rows = text_ref.shape[1]
    heads = keys_values.shape[1] // (2 * HD)
    query = query_ref[0]
    for head in range(heads):
        keys = keys_values[:, 2 * head * HD : (2 * head + 1) * HD]
        values = keys_values[:, (2 * head + 1) * HD : (2 * head + 2) * HD]
        stacked = jnp.concatenate(
            [
                query[:, (head * GROUP + a) * HD : (head * GROUP + a + 1) * HD]
                for a in range(GROUP)
            ],
            axis=0,
        )
        scores = lax.dot_general(
            stacked, keys, (((1,), (1,)), ((), ())), preferred_element_type=jnp.float32
        ) * (HD**-0.5)
        row = lax.broadcasted_iota(jnp.int32, scores.shape, 0) % text_rows
        column = lax.broadcasted_iota(jnp.int32, scores.shape, 1)
        text_column = column - (scores.shape[1] - text_rows)
        allowed = (text_column <= row) & (seen_ref[0] > 0)
        scores = jnp.where(allowed, scores, -1e30)
        best = jnp.max(scores, axis=1, keepdims=True)
        weights = jnp.exp(scores - best)
        total = jnp.sum(weights, axis=1, keepdims=True)
        result = jnp.dot(weights.astype(jnp.bfloat16), values, preferred_element_type=jnp.float32)
        result = (result / total).astype(jnp.bfloat16)
        for a in range(GROUP):
            out_ref[0, :, (head * GROUP + a) * HD : (head * GROUP + a + 1) * HD] = result[
                a * text_rows : (a + 1) * text_rows
            ]


def attend(place, queries, prefixes, text_kv, pages, picks, seen, all_rows):
    docs, rows, width = queries.shape
    kv_width = text_kv.shape[2]
    vision_rows = all_rows.shape[0]
    keys = seen.shape[2]
    return pl.pallas_call(
        attend_kernel,
        grid_spec=pltpu.PrefetchScalarGridSpec(
            num_scalar_prefetch=1,
            grid=(docs,),
            in_specs=[
                pl.BlockSpec((1, rows, width), lambda d, place: (d, 0, 0)),
                pl.BlockSpec((1,) + prefixes.shape[1:], lambda d, place: (place[d], 0, 0)),
                pl.BlockSpec((1, rows, kv_width), lambda d, place: (d, 0, 0)),
                pl.BlockSpec(pages.shape, lambda d, place: (0, 0)),
                pl.BlockSpec((1,) + picks.shape[1:], lambda d, place: (d, 0, 0)),
                pl.BlockSpec((1, 1, keys), lambda d, place: (d, 0, 0)),
                pl.BlockSpec(all_rows.shape, lambda d, place: (0, 0)),
            ],
            out_specs=[
                pl.BlockSpec((1, rows, width), lambda d, place: (d, 0, 0)),
                pl.BlockSpec((vision_rows, kv_width), lambda d, place: (0, 0)),
            ],
        ),
        out_shape=[
            jax.ShapeDtypeStruct(queries.shape, jnp.bfloat16),
            jax.ShapeDtypeStruct((vision_rows, kv_width), jnp.bfloat16),
        ],
        compiler_params=pltpu.CompilerParams(vmem_limit_bytes=VMEM),
        cost_estimate=pl.CostEstimate(
            flops=4 * docs * rows * width * keys,
            bytes_accessed=8 * docs * rows * width,
            transcendentals=docs * rows * keys * width // HD,
        ),
    )(place, queries, prefixes, text_kv, pages, picks, seen, all_rows)


def shards(
    panels,
    w_merge,
    ln_gain,
    w_kv,
    page_src,
    page_tile,
    doc_pages,
    prefix_id,
    prefix_cache,
    queries,
    text_kv,
):
    seq_count = lax.axis_size("seq")
    holder = lax.axis_index("seq")
    tile_count, panel_rows, _ = panels.shape
    page_count = page_src.shape[0]
    capacity = max(2, 2 * page_count // seq_count)
    sources = page_src[:, 0]

    kv, squares, small = merge_tiles(
        panels, w_merge, ln_gain, w_kv, pack_small(prefix_cache, sources, page_tile)
    )
    width = seq_count // lax.axis_size("tp")
    small = small.reshape(seq_count, SMALL_ROWS, -1)

    def place_of(index):
        group = (index // width) ^ (holder // width)
        return group * width + (index - holder) % width

    prefix_rows = prefix_cache.shape[1]
    prefixes = small[:, :prefix_rows]
    place = place_of(jnp.arange(seq_count, dtype=jnp.int32))
    asked_sources = small[:, prefix_rows, :page_count].astype(jnp.int32)[place]
    asked_tiles = small[:, prefix_rows + 1, :page_count].astype(jnp.int32)[place]
    asked = (asked_sources == holder).astype(jnp.int32)
    order = jnp.cumsum(asked, axis=1) - 1
    slots = jnp.arange(capacity, dtype=jnp.int32)
    picked = asked[:, None, :] * (order[:, None, :] == slots[None, :, None]).astype(jnp.int32)
    wanted = jnp.sum(picked * asked_tiles[:, None, :], axis=2)
    within = jnp.arange(panel_rows, dtype=jnp.int32)
    wanted_rows = (wanted.reshape(-1, 1) * panel_rows + within[None, :]).reshape(-1)
    chooser = wanted_rows[:, None] == jnp.arange(tile_count * panel_rows, dtype=jnp.int32)[None, :]
    chooser = chooser.astype(jnp.bfloat16)

    position = jnp.arange(page_count, dtype=jnp.int32)
    earlier = (sources[:, None] == sources[None, :]) & (position[None, :] < position[:, None])
    rank = jnp.sum(earlier.astype(jnp.int32), axis=1)
    arrival = sources * capacity + rank
    all_rows = (arrival[:, None] * panel_rows + within[None, :]).reshape(-1, 1)
    lengths = doc_pages[0]
    starts = jnp.cumsum(lengths) - lengths
    step = jnp.arange(MOST_PAGES, dtype=jnp.int32)
    inside = step[None, :] < lengths[:, None]
    page = jnp.minimum(starts[:, None] + step[None, :], page_count - 1)
    doc_rows = arrival[page][:, :, None] * panel_rows + within[None, None, :]
    doc_rows = jnp.where(inside[:, :, None], doc_rows, -1)
    doc_count, query_rows, _ = queries.shape
    picks = doc_rows.reshape(doc_count, -1, 1)
    seen = jnp.concatenate(
        [
            jnp.ones((doc_count, prefixes.shape[1]), jnp.int32),
            (doc_rows >= 0).reshape(doc_count, -1).astype(jnp.int32),
            jnp.ones((doc_count, query_rows), jnp.int32),
        ],
        axis=1,
    )[:, None, :]

    kv, squares = scatter_heads(kv, squares)
    row_scale = lax.rsqrt(squares / D + 1e-06)
    tile_kv = return_rows((kv * row_scale[:, None]).astype(jnp.bfloat16))
    outgoing = jnp.dot(chooser, tile_kv, preferred_element_type=jnp.float32).astype(jnp.bfloat16)
    pages = lax.all_to_all(outgoing, "seq", split_axis=0, concat_axis=0, tiled=True)
    attended, vision_kv = attend(
        place_of(prefix_id), queries, prefixes, text_kv, pages, picks, seen, all_rows
    )
    return (attended, vision_kv)


def solution(mesh):
    return jax.shard_map(
        shards,
        mesh=mesh,
        in_specs=(
            P("seq", None, "tp"),
            P("seq", "tp"),
            P("tp"),
            P("tp", None),
            P("seq", None),
            P("seq"),
            P("seq", None),
            P("seq"),
            P("seq", None, "tp"),
            P("seq", None, "tp"),
            P("seq", None, "tp"),
        ),
        out_specs=(P("seq", None, "tp"), P("seq", "tp")),
        check_vma=False,
    )
```

```python
import functools

import jax
import jax.numpy as jnp
from jax import lax
from jax.experimental import pallas as pl
from jax.experimental.pallas import tpu as pltpu
from jax.sharding import PartitionSpec as P

D = 8192
HD = 128
GROUP = 8
MOST_PAGES = 16
VMEM = 16 * 1024 * 1024


def bits_of(count):
    return [1 << bit for bit in range(count.bit_length() - 1)]


def flip(value, axis, bit):
    count = lax.axis_size(axis)
    return lax.ppermute(value, axis, [(i, i ^ bit) for i in range(count)])


def transpose_panels(local, swap):
    seq_count, tp_count = lax.axis_size("seq"), lax.axis_size("tp")
    width = seq_count // tp_count
    half = tp_count // 2
    pairs = []
    for origin in range(tp_count):
        for inner in range(width):
            for block in range(tp_count):
                source = (origin * width + inner) * tp_count + (block ^ swap)
                slot = ((origin ^ block) & 1) * half + origin // 2
                pairs.append((source, (block * width + inner) * tp_count + slot))
    held = [lax.ppermute(local, ("seq", "tp"), pairs)]
    bits = bits_of(tp_count)
    for bit in bits[-1:] + bits[:-1]:
        held = held + [flip(piece, "tp", bit) for piece in held]
    return held


def panel_base():
    group = lax.axis_index("seq") // (lax.axis_size("seq") // lax.axis_size("tp"))
    place = lax.axis_index("tp")
    half = lax.axis_size("tp") // 2
    return 2 * (place % half) + ((place // half) ^ (group & 1))


ROLE_GROUPS = (3, 2, 1, 0)


def order_kernel(share, pieces, scalars_ref, *refs):
    out_ref = refs[-1]
    rows, depth = refs[0].shape
    members = depth // share
    for place in range(4):
        for piece in range(pieces):
            row = (scalars_ref[place] * pieces + piece) * rows
            at = pl.ds(pl.multiple_of(row, rows), rows)
            rows_ref = refs[place * pieces + piece]
            for member in range(members):
                if members == 1:
                    out_ref[at, :] = rows_ref[...]
                else:
                    source = lax.rem(scalars_ref[4] + member, members)
                    columns = pl.ds(pl.multiple_of(source * share, share), share)
                    out_ref[at, member * share : (member + 1) * share] = rows_ref[:, columns]


def order_rows(scalars, held, share):
    pieces = len(held[0])
    rows, depth = held[0][0].shape
    return pl.pallas_call(
        functools.partial(order_kernel, share, pieces),
        grid_spec=pltpu.PrefetchScalarGridSpec(
            num_scalar_prefetch=1,
            grid=(1,),
            in_specs=[pl.BlockSpec((rows, depth), lambda i, scalars: (0, 0))] * (4 * pieces),
            out_specs=pl.BlockSpec((4 * pieces * rows, depth), lambda i, scalars: (0, 0)),
        ),
        out_shape=jax.ShapeDtypeStruct((4 * pieces * rows, depth), jnp.bfloat16),
        compiler_params=pltpu.CompilerParams(vmem_limit_bytes=VMEM),
        cost_estimate=pl.CostEstimate(flops=0, bytes_accessed=2 * depth, transcendentals=0),
    )(scalars, *[piece for place in held for piece in place])


def partial_kernel(rows_ref, *refs):
    weights_refs = refs[:-2]
    inner_ref, end_ref = refs[-2:]
    total = None
    at = 0
    for weights_ref in weights_refs:
        depth = weights_ref.shape[0]
        term = jnp.dot(
            rows_ref[:, at : at + depth], weights_ref[...], preferred_element_type=jnp.float32
        )
        total = term if total is None else total + term
        at += depth
    total = total.astype(jnp.bfloat16)
    rows = inner_ref.shape[0]
    inner_ref[...] = total[:rows]
    end_ref[...] = total[rows:]


def partial_products(held, weights, count):
    rows, depth = held.shape
    tile = min(count, 256)

    def block(used, first):
        return pl.BlockSpec((used, tile), lambda i: (0, i + first // tile))

    outs = (3 * rows // 4, rows // 4)
    return pl.pallas_call(
        partial_kernel,
        grid=(count // tile,),
        in_specs=[pl.BlockSpec((rows, depth), lambda i: (0, 0))]
        + [block(used, first) for _, used, first in weights],
        out_specs=[pl.BlockSpec((out, tile), lambda i: (0, i)) for out in outs],
        out_shape=[jax.ShapeDtypeStruct((out, count), jnp.bfloat16) for out in outs],
        compiler_params=pltpu.CompilerParams(vmem_limit_bytes=VMEM),
        cost_estimate=pl.CostEstimate(flops=0, bytes_accessed=2 * count, transcendentals=0),
    )(held, *[array for array, _, _ in weights])


def along(pairs):
    width = lax.axis_size("seq") // lax.axis_size("tp")
    return [(a * width + i, b * width + i) for a, b in pairs for i in range(width)]


INWARD = ((0, 1), (3, 2))
OUTWARD = ((1, 0), (2, 3))
ACROSS = ((1, 2), (2, 1))
BEYOND = ((1, 3), (2, 0))


def reduce_groups(parts, is_end, small):
    inner, end = parts
    rows = end.shape[0]

    def add(mine, other):
        return (mine.astype(jnp.float32) + other.astype(jnp.float32)).astype(jnp.bfloat16)

    def ride(value, extra):
        return value if small is None else jnp.concatenate([value] + extra, axis=0)

    def part(value, first, index=0):
        count = small.shape[0]
        return value[first + index * count : first + (index + 1) * count]

    message = ride(inner, [small])
    inward = lax.ppermute(message, "seq", along(INWARD))
    outward = lax.ppermute(ride(end, [small]), "seq", along(OUTWARD))
    extra = [] if small is None else [part(inward, 3 * rows), small]
    beyond = lax.ppermute(ride(add(inner[:rows], inward[:rows]), extra), "seq", along(BEYOND))
    across = lax.ppermute(
        ride(add(inner[rows : 2 * rows], inward[rows : 2 * rows]), extra), "seq", along(ACROSS)
    )
    at_end = end.astype(jnp.float32) + outward[:rows] + beyond[:rows]
    at_middle = inner[2 * rows :].astype(jnp.float32) + inward[2 * rows : 3 * rows] + across[:rows]
    shared = None
    if small is not None:
        ends = [part(outward, rows), part(beyond, rows, 1), part(beyond, rows, 0)]
        middles = [part(inward, 3 * rows), part(across, rows, 0), part(across, rows, 1)]
        shared = [small] + [jnp.where(is_end, e, m) for e, m in zip(ends, middles)]
    return jnp.where(is_end, at_end, at_middle).astype(jnp.bfloat16), inward, shared


PLAN = (2, 2, 2, 1, 1)


def merge_tiles(panels, w_merge, ln_gain, w_kv, small):
    seq_count, tp_count = lax.axis_size("seq"), lax.axis_size("tp")
    assert tp_count == 4 and seq_count % 4 == 0
    width = seq_count // tp_count
    tiles, panel_rows, depth = panels.shape
    share = w_merge.shape[0]
    group = lax.axis_index("seq") // width
    inner = lax.axis_index("seq") % width
    is_end = (group == 0) | (group == 3)
    local = panels.reshape(tiles * panel_rows, depth)
    half = local.shape[0] // 2
    swapped = flip(local[half:], "tp", 2)
    pieces = [transpose_panels(local[:half], 0), transpose_panels(swapped, 2)]
    columns = w_merge.shape[1] // 2
    small = small.reshape(-1, columns)
    extra = small.shape[0]
    received = []
    for side in range(2):
        own = w_merge[:, side * columns : (side + 1) * columns]
        if side == 1:
            own = jnp.concatenate([own, small], axis=0)
            own, _ = lax.optimization_barrier((own, swapped))
        others = []
        for offset in range(1, width):
            pairs = [
                (g * width + (i + offset) % width, g * width + i)
                for g in range(tp_count)
                for i in range(width)
            ]
            others.append(lax.ppermute(own, "seq", pairs))
        received.append(others)
    small = jnp.stack([small] + [other[share : share + extra] for other in received[1]])
    small_shape = small.shape
    if width > 2 or share % 128:
        weights = []
        for side in range(2):
            own = w_merge[:, side * columns : (side + 1) * columns]
            parts = [own] + [other[:share] for other in received[side]]
            weights.append(jnp.roll(jnp.concatenate(parts, axis=0), inner * share, axis=0))
        share = depth
    shift = jnp.where(group < 2, 0, 3)
    groups = (panel_base() ^ jnp.arange(4, dtype=jnp.int32)) ^ shift
    roles = jnp.array([ROLE_GROUPS.index(g) for g in range(4)], jnp.int32)[groups]
    scalars = jnp.concatenate([roles, jnp.full((4,), inner, jnp.int32)])
    held = order_rows(scalars, list(zip(*pieces)), share)
    kv = 0.0
    squares = 0.0
    inwards = []
    first = 0
    for step, part in enumerate(PLAN):
        count = part * w_merge.shape[1] // sum(PLAN)
        side = first // columns
        inside = first - side * columns
        if share == depth:
            operands = [(weights[side], depth, inside)]
        else:
            operands = [(w_merge, share, first), (received[side][0], share, inside)]
        rows = held
        if step >= 2:
            rows, _ = lax.optimization_barrier((held, inwards[step - 2]))
        riding = small.reshape(-1, count) if step == 2 else None
        merged, inward, shared = reduce_groups(
            partial_products(rows, operands, count), is_end, riding
        )
        inwards.append(inward)
        if step == 2:
            everyone = jnp.stack(shared).reshape((4,) + small_shape)
        merged = merged.astype(jnp.float32)
        at = slice(first, first + count)
        gained = (merged * ln_gain[at].astype(jnp.float32)[None, :]).astype(jnp.bfloat16)
        squares = squares + jnp.sum(merged * merged, axis=1)
        kv = kv + jnp.dot(gained, w_kv[at], preferred_element_type=jnp.float32)
        first += count
    return kv, squares, everyone


def scatter_heads(kv, squares):
    tp_count = lax.axis_size("tp")
    place = lax.axis_index("tp")
    rows = kv.shape[0]
    blocks = jnp.stack(jnp.split(kv, tp_count, axis=1))
    for bit in bits_of(tp_count):
        paired = blocks.reshape(blocks.shape[0] // 2, 2, rows, blocks.shape[2])
        mine = (place // bit) % 2
        keep = lax.dynamic_index_in_dim(paired, mine, 1, keepdims=False)
        give = lax.dynamic_index_in_dim(paired, 1 - mine, 1, keepdims=False)
        blocks = keep + flip(give.astype(jnp.bfloat16), "tp", bit).astype(jnp.float32)
        squares = squares + flip(squares, "tp", bit)
    return blocks[0], squares


SMALL_ROWS = 64


def pack_small(prefix_cache, sources, tiles):
    width = prefix_cache.shape[2]
    asks = jnp.stack([sources, tiles]).astype(jnp.bfloat16)
    rows = SMALL_ROWS - prefix_cache.shape[1]
    asks = jnp.pad(asks, ((0, rows - 2), (0, width - asks.shape[1])))
    return jnp.concatenate([prefix_cache[0], asks], axis=0)


def attend_kernel(
    place_ref, query_ref, prefix_ref, text_ref, pages_ref, pick_ref, seen_ref, all_ref, out_ref, vision_ref
):
    pages = pages_ref[...]
    count = pages.shape[0]

    def pick(index):
        one_hot = lax.broadcasted_iota(jnp.int32, (index.shape[0], count), 1) == index
        one_hot = jnp.where(one_hot, 1.0, 0.0).astype(jnp.bfloat16)
        return jnp.dot(one_hot, pages, preferred_element_type=jnp.float32).astype(jnp.bfloat16)

    @pl.when(pl.program_id(0) == 0)
    def _():
        vision_ref[...] = pick(all_ref[...])

    window = pick(pick_ref[0])
    keys_values = jnp.concatenate([prefix_ref[0], window, text_ref[0]], axis=0)
    text_rows = text_ref.shape[1]
    heads = keys_values.shape[1] // (2 * HD)
    query = query_ref[0]
    for head in range(heads):
        keys = keys_values[:, 2 * head * HD : (2 * head + 1) * HD]
        values = keys_values[:, (2 * head + 1) * HD : (2 * head + 2) * HD]
        stacked = jnp.concatenate(
            [
                query[:, (head * GROUP + a) * HD : (head * GROUP + a + 1) * HD]
                for a in range(GROUP)
            ],
            axis=0,
        )
        scores = lax.dot_general(
            stacked, keys, (((1,), (1,)), ((), ())), preferred_element_type=jnp.float32
        ) * (HD**-0.5)
        row = lax.broadcasted_iota(jnp.int32, scores.shape, 0) % text_rows
        column = lax.broadcasted_iota(jnp.int32, scores.shape, 1)
        text_column = column - (scores.shape[1] - text_rows)
        allowed = (text_column <= row) & (seen_ref[0] > 0)
        scores = jnp.where(allowed, scores, -1e30)
        best = jnp.max(scores, axis=1, keepdims=True)
        weights = jnp.exp(scores - best)
        total = jnp.sum(weights, axis=1, keepdims=True)
        result = jnp.dot(weights.astype(jnp.bfloat16), values, preferred_element_type=jnp.float32)
        result = (result / total).astype(jnp.bfloat16)
        for a in range(GROUP):
            out_ref[0, :, (head * GROUP + a) * HD : (head * GROUP + a + 1) * HD] = result[
                a * text_rows : (a + 1) * text_rows
            ]


def attend(place, queries, prefixes, text_kv, pages, picks, seen, all_rows):
    docs, rows, width = queries.shape
    kv_width = text_kv.shape[2]
    vision_rows = all_rows.shape[0]
    keys = seen.shape[2]
    return pl.pallas_call(
        attend_kernel,
        grid_spec=pltpu.PrefetchScalarGridSpec(
            num_scalar_prefetch=1,
            grid=(docs,),
            in_specs=[
                pl.BlockSpec((1, rows, width), lambda d, place: (d, 0, 0)),
                pl.BlockSpec((1,) + prefixes.shape[1:], lambda d, place: (place[d], 0, 0)),
                pl.BlockSpec((1, rows, kv_width), lambda d, place: (d, 0, 0)),
                pl.BlockSpec(pages.shape, lambda d, place: (0, 0)),
                pl.BlockSpec((1,) + picks.shape[1:], lambda d, place: (d, 0, 0)),
                pl.BlockSpec((1, 1, keys), lambda d, place: (d, 0, 0)),
                pl.BlockSpec(all_rows.shape, lambda d, place: (0, 0)),
            ],
            out_specs=[
                pl.BlockSpec((1, rows, width), lambda d, place: (d, 0, 0)),
                pl.BlockSpec((vision_rows, kv_width), lambda d, place: (0, 0)),
            ],
        ),
        out_shape=[
            jax.ShapeDtypeStruct(queries.shape, jnp.bfloat16),
            jax.ShapeDtypeStruct((vision_rows, kv_width), jnp.bfloat16),
        ],
        compiler_params=pltpu.CompilerParams(vmem_limit_bytes=VMEM),
        cost_estimate=pl.CostEstimate(
            flops=4 * docs * rows * width * keys,
            bytes_accessed=8 * docs * rows * width,
            transcendentals=docs * rows * keys * width // HD,
        ),
    )(place, queries, prefixes, text_kv, pages, picks, seen, all_rows)


def shards(
    panels,
    w_merge,
    ln_gain,
    w_kv,
    page_src,
    page_tile,
    doc_pages,
    prefix_id,
    prefix_cache,
    queries,
    text_kv,
):
    seq_count = lax.axis_size("seq")
    holder = lax.axis_index("seq")
    tile_count, panel_rows, _ = panels.shape
    page_count = page_src.shape[0]
    capacity = max(2, 2 * page_count // seq_count)
    sources = page_src[:, 0]

    kv, squares, small = merge_tiles(
        panels, w_merge, ln_gain, w_kv, pack_small(prefix_cache, sources, page_tile)
    )
    width = seq_count // lax.axis_size("tp")
    small = small.reshape(seq_count, SMALL_ROWS, -1)

    def place_of(index):
        group = (index // width) ^ (holder // width)
        return group * width + (index - holder) % width

    prefix_rows = prefix_cache.shape[1]
    prefixes = small[:, :prefix_rows]
    place = place_of(jnp.arange(seq_count, dtype=jnp.int32))
    asked_sources = small[:, prefix_rows, :page_count].astype(jnp.int32)[place]
    asked_tiles = small[:, prefix_rows + 1, :page_count].astype(jnp.int32)[place]
    asked = (asked_sources == holder).astype(jnp.int32)
    order = jnp.cumsum(asked, axis=1) - 1
    slots = jnp.arange(capacity, dtype=jnp.int32)
    picked = asked[:, None, :] * (order[:, None, :] == slots[None, :, None]).astype(jnp.int32)
    wanted = jnp.sum(picked * asked_tiles[:, None, :], axis=2)
    within = jnp.arange(panel_rows, dtype=jnp.int32)
    wanted_rows = (wanted.reshape(-1, 1) * panel_rows + within[None, :]).reshape(-1)
    chooser = wanted_rows[:, None] == jnp.arange(tile_count * panel_rows, dtype=jnp.int32)[None, :]
    chooser = chooser.astype(jnp.bfloat16)

    position = jnp.arange(page_count, dtype=jnp.int32)
    earlier = (sources[:, None] == sources[None, :]) & (position[None, :] < position[:, None])
    rank = jnp.sum(earlier.astype(jnp.int32), axis=1)
    arrival = sources * capacity + rank
    all_rows = (arrival[:, None] * panel_rows + within[None, :]).reshape(-1, 1)
    lengths = doc_pages[0]
    starts = jnp.cumsum(lengths) - lengths
    step = jnp.arange(MOST_PAGES, dtype=jnp.int32)
    inside = step[None, :] < lengths[:, None]
    page = jnp.minimum(starts[:, None] + step[None, :], page_count - 1)
    doc_rows = arrival[page][:, :, None] * panel_rows + within[None, None, :]
    doc_rows = jnp.where(inside[:, :, None], doc_rows, -1)
    doc_count, query_rows, _ = queries.shape
    picks = doc_rows.reshape(doc_count, -1, 1)
    seen = jnp.concatenate(
        [
            jnp.ones((doc_count, prefixes.shape[1]), jnp.int32),
            (doc_rows >= 0).reshape(doc_count, -1).astype(jnp.int32),
            jnp.ones((doc_count, query_rows), jnp.int32),
        ],
        axis=1,
    )[:, None, :]

    kv, squares = scatter_heads(kv, squares)
    row_scale = lax.rsqrt(squares / D + 1e-06)
    tile_kv = (kv * row_scale[:, None]).astype(jnp.bfloat16)
    outgoing = jnp.dot(chooser, tile_kv, preferred_element_type=jnp.float32).astype(jnp.bfloat16)
    pages = lax.all_to_all(outgoing, "seq", split_axis=0, concat_axis=0, tiled=True)
    attended, vision_kv = attend(
        place_of(prefix_id), queries, prefixes, text_kv, pages, picks, seen, all_rows
    )
    return (attended, vision_kv)


def solution(mesh):
    return jax.shard_map(
        shards,
        mesh=mesh,
        in_specs=(
            P("seq", None, "tp"),
            P("seq", "tp"),
            P("tp"),
            P("tp", None),
            P("seq", None),
            P("seq"),
            P("seq", None),
            P("seq"),
            P("seq", None, "tp"),
            P("seq", None, "tp"),
            P("seq", None, "tp"),
        ),
        out_specs=(P("seq", None, "tp"), P("seq", "tp")),
        check_vma=False,
    )
```

```python
import functools

import jax
import jax.numpy as jnp
from jax import lax
from jax.experimental import pallas as pl
from jax.experimental.pallas import tpu as pltpu
from jax.sharding import PartitionSpec as P

D = 8192
HD = 128
GROUP = 8
MOST_PAGES = 16
VMEM = 16 * 1024 * 1024


def bits_of(count):
    return [1 << bit for bit in range(count.bit_length() - 1)]


def flip(value, axis, bit):
    count = lax.axis_size(axis)
    return lax.ppermute(value, axis, [(i, i ^ bit) for i in range(count)])


def transpose_panels(local, swap):
    seq_count, tp_count = lax.axis_size("seq"), lax.axis_size("tp")
    width = seq_count // tp_count
    half = tp_count // 2
    pairs = []
    for origin in range(tp_count):
        for inner in range(width):
            for block in range(tp_count):
                source = (origin * width + inner) * tp_count + (block ^ swap)
                slot = ((origin ^ block) & 1) * half + origin // 2
                pairs.append((source, (block * width + inner) * tp_count + slot))
    return lax.ppermute(local, ("seq", "tp"), pairs)


def share_panels(moved):
    held = [moved]
    bits = bits_of(lax.axis_size("tp"))
    for bit in bits[-1:] + bits[:-1]:
        held = held + [flip(piece, "tp", bit) for piece in held]
    return held


def panel_base():
    group = lax.axis_index("seq") // (lax.axis_size("seq") // lax.axis_size("tp"))
    place = lax.axis_index("tp")
    half = lax.axis_size("tp") // 2
    return 2 * (place % half) + ((place // half) ^ (group & 1))


ROLE_GROUPS = (3, 2, 1, 0)


def order_kernel(share, scalars_ref, *refs):
    out_ref = refs[-1]
    rows, depth = refs[0].shape
    members = depth // share
    for place in range(4):
        at = pl.ds(pl.multiple_of(scalars_ref[place] * rows, rows), rows)
        for member in range(members):
            if members == 1:
                out_ref[at, :] = refs[place][...]
            else:
                source = lax.rem(scalars_ref[4] + member, members)
                columns = pl.ds(pl.multiple_of(source * share, share), share)
                out_ref[at, member * share : (member + 1) * share] = refs[place][:, columns]


def order_rows(scalars, held, share):
    rows, depth = held[0].shape
    return pl.pallas_call(
        functools.partial(order_kernel, share),
        grid_spec=pltpu.PrefetchScalarGridSpec(
            num_scalar_prefetch=1,
            grid=(1,),
            in_specs=[pl.BlockSpec((rows, depth), lambda i, scalars: (0, 0))] * 4,
            out_specs=pl.BlockSpec((4 * rows, depth), lambda i, scalars: (0, 0)),
        ),
        out_shape=jax.ShapeDtypeStruct((4 * rows, depth), jnp.bfloat16),
        compiler_params=pltpu.CompilerParams(vmem_limit_bytes=VMEM),
        cost_estimate=pl.CostEstimate(flops=0, bytes_accessed=2 * depth, transcendentals=0),
    )(scalars, *held)


def partial_kernel(halves, *refs):
    rows_refs, weights_refs = refs[:halves], refs[halves:-2]
    inner_ref, end_ref = refs[-2:]
    for half, rows_ref in enumerate(rows_refs):
        total = None
        at = 0
        for weights_ref in weights_refs:
            depth = weights_ref.shape[0]
            term = jnp.dot(
                rows_ref[:, at : at + depth],
                weights_ref[...],
                preferred_element_type=jnp.float32,
            )
            total = term if total is None else total + term
            at += depth
        total = total.astype(jnp.bfloat16)
        rows = total.shape[0] // 4
        for role in range(3):
            to = (role * halves + half) * rows
            inner_ref[to : to + rows] = total[role * rows : (role + 1) * rows]
        end_ref[half * rows : (half + 1) * rows] = total[3 * rows :]


def partial_products(held, weights, count):
    halves = len(held)
    rows, depth = held[0].shape
    rows = rows * halves
    tile = min(count, 256)

    def block(used, first):
        return pl.BlockSpec((used, tile), lambda i: (0, i + first // tile))

    outs = (3 * rows // 4, rows // 4)
    return pl.pallas_call(
        functools.partial(partial_kernel, halves),
        grid=(count // tile,),
        in_specs=[pl.BlockSpec((rows // halves, depth), lambda i: (0, 0))] * halves
        + [block(used, first) for _, used, first in weights],
        out_specs=[pl.BlockSpec((out, tile), lambda i: (0, i)) for out in outs],
        out_shape=[jax.ShapeDtypeStruct((out, count), jnp.bfloat16) for out in outs],
        compiler_params=pltpu.CompilerParams(vmem_limit_bytes=VMEM),
        cost_estimate=pl.CostEstimate(flops=0, bytes_accessed=2 * count, transcendentals=0),
    )(*held, *[array for array, _, _ in weights])


def along(pairs):
    width = lax.axis_size("seq") // lax.axis_size("tp")
    return [(a * width + i, b * width + i) for a, b in pairs for i in range(width)]


INWARD = ((0, 1), (3, 2))
OUTWARD = ((1, 0), (2, 3))
ACROSS = ((1, 2), (2, 1))
BEYOND = ((1, 3), (2, 0))


def ride(value, extra):
    return jnp.concatenate([value] + extra, axis=0) if extra else value


def send_sums(parts, small):
    inner, end = parts
    inward = lax.ppermute(ride(inner, small), "seq", along(INWARD))
    outward = lax.ppermute(ride(end, small), "seq", along(OUTWARD))
    return inward, outward


def finish_sums(parts, arrived, is_end, small):
    inner, end = parts
    inward, outward = arrived
    rows = end.shape[0]

    def add(mine, other):
        return (mine.astype(jnp.float32) + other.astype(jnp.float32)).astype(jnp.bfloat16)

    def part(value, first, index=0):
        count = small[0].shape[0]
        return value[first + index * count : first + (index + 1) * count]

    extra = [part(inward, 3 * rows)] + small if small else []
    beyond = lax.ppermute(ride(add(inner[:rows], inward[:rows]), extra), "seq", along(BEYOND))
    across = lax.ppermute(
        ride(add(inner[rows : 2 * rows], inward[rows : 2 * rows]), extra), "seq", along(ACROSS)
    )
    at_end = end.astype(jnp.float32) + outward[:rows] + beyond[:rows]
    at_middle = inner[2 * rows :].astype(jnp.float32) + inward[2 * rows : 3 * rows] + across[:rows]
    shared = None
    if small:
        ends = [part(outward, rows), part(beyond, rows, 1), part(beyond, rows, 0)]
        middles = [part(inward, 3 * rows), part(across, rows, 0), part(across, rows, 1)]
        shared = small + [jnp.where(is_end, e, m) for e, m in zip(ends, middles)]
    return jnp.where(is_end, at_end, at_middle).astype(jnp.bfloat16), shared


PLAN = (((0,), 0, 4), ((1,), 0, 4), ((0, 1), 4, 2), ((0, 1), 6, 2))
RIDE = 2


def merge_tiles(panels, w_merge, ln_gain, w_kv, small):
    seq_count, tp_count = lax.axis_size("seq"), lax.axis_size("tp")
    assert tp_count == 4 and seq_count % 4 == 0
    width = seq_count // tp_count
    tiles, panel_rows, depth = panels.shape
    share = w_merge.shape[0]
    group = lax.axis_index("seq") // width
    member = lax.axis_index("seq") % width
    is_end = (group == 0) | (group == 3)
    local = panels.reshape(tiles * panel_rows, depth)
    half = local.shape[0] // 2
    swapped = flip(local[half:], "tp", 2)
    moved = [transpose_panels(local[:half], 0), transpose_panels(swapped, 2)]
    columns = w_merge.shape[1] // 2
    small = small.reshape(-1, columns)
    extra = small.shape[0]
    received = []
    for side in range(2):
        own = w_merge[:, side * columns : (side + 1) * columns]
        if side == 1:
            own = jnp.concatenate([own, small], axis=0)
            own, _ = lax.optimization_barrier((own, swapped))
        others = []
        for offset in range(1, width):
            pairs = [
                (g * width + (i + offset) % width, g * width + i)
                for g in range(tp_count)
                for i in range(width)
            ]
            others.append(lax.ppermute(own, "seq", pairs))
        received.append(others)
    aligned = width == 2 and share % 128 == 0
    if not aligned:
        share = depth
    shift = jnp.where(group < 2, 0, 3)
    groups = (panel_base() ^ jnp.arange(4, dtype=jnp.int32)) ^ shift
    roles = jnp.array([ROLE_GROUPS.index(g) for g in range(4)], jnp.int32)[groups]
    scalars = jnp.concatenate([roles, jnp.full((4,), member, jnp.int32)])
    early = share_panels(moved[0])
    early, moved[1] = lax.optimization_barrier((early, moved[1]))
    held = [order_rows(scalars, early, share)]
    kv = [0.0, 0.0]
    squares = [0.0, 0.0]
    everyone = None
    eighth = w_merge.shape[1] // 8
    sent = []
    for step in range(len(PLAN) + 1):
        if step < len(PLAN):
            halves, first, count = PLAN[step]
            first, count = first * eighth, count * eighth
            if step == 1:
                late, _ = lax.optimization_barrier((moved[1], sent[0][0][0]))
                held.append(order_rows(scalars, share_panels(late), share))
            if step == RIDE:
                received[1], _ = lax.optimization_barrier((received[1], sent[step - 1][0][0]))
                small = [small] + [other[-extra:] for other in received[1]]
                small_shape = (width,) + small[0].shape
                small = [jnp.stack(small).reshape(-1, count)]
            side = first // columns
            inside = first - side * columns
            if aligned:
                operands = [(w_merge, share, first), (received[side][0], share, inside)]
            else:
                parts = [w_merge[:, side * columns : (side + 1) * columns]]
                parts += [other[: w_merge.shape[0]] for other in received[side]]
                parts = jnp.concatenate(parts, axis=0)
                operands = [(jnp.roll(parts, member * w_merge.shape[0], axis=0), depth, inside)]
            rows = [held[h] for h in halves]
            if step >= 2:
                rows, _ = lax.optimization_barrier((rows, sent[step - 2][1][0]))
            parts = partial_products(rows, operands, count)
            riding = small if step == RIDE else []
            sent.append((parts, send_sums(parts, riding), riding))
        if step >= 1:
            parts, arrived, riding = sent[step - 1]
            if step < len(PLAN):
                arrived, _ = lax.optimization_barrier((arrived, sent[step][0][0]))
            halves, first, count = PLAN[step - 1]
            first, count = first * eighth, count * eighth
            merged, shared = finish_sums(parts, arrived, is_end, riding)
            if shared is not None:
                everyone = jnp.stack(shared).reshape((4,) + small_shape)
            merged = merged.astype(jnp.float32)
            at = slice(first, first + count)
            gained = (merged * ln_gain[at].astype(jnp.float32)[None, :]).astype(jnp.bfloat16)
            squared = jnp.sum(merged * merged, axis=1)
            product = jnp.dot(gained, w_kv[at], preferred_element_type=jnp.float32)
            for i, h in enumerate(halves):
                squares[h] = squares[h] + squared[i * half : (i + 1) * half]
                kv[h] = kv[h] + product[i * half : (i + 1) * half]
    return jnp.concatenate(kv), jnp.concatenate(squares), everyone


def scatter_heads(kv, squares):
    tp_count = lax.axis_size("tp")
    place = lax.axis_index("tp")
    rows = kv.shape[0]
    blocks = jnp.stack(jnp.split(kv, tp_count, axis=1))
    for bit in bits_of(tp_count):
        paired = blocks.reshape(blocks.shape[0] // 2, 2, rows, blocks.shape[2])
        mine = (place // bit) % 2
        keep = lax.dynamic_index_in_dim(paired, mine, 1, keepdims=False)
        give = lax.dynamic_index_in_dim(paired, 1 - mine, 1, keepdims=False)
        blocks = keep + flip(give.astype(jnp.bfloat16), "tp", bit).astype(jnp.float32)
        squares = squares + flip(squares, "tp", bit)
    return blocks[0], squares


SMALL_ROWS = 64


def pack_small(prefix_cache, sources, tiles):
    width = prefix_cache.shape[2]
    asks = jnp.stack([sources, tiles]).astype(jnp.bfloat16)
    rows = SMALL_ROWS - prefix_cache.shape[1]
    asks = jnp.pad(asks, ((0, rows - 2), (0, width - asks.shape[1])))
    return jnp.concatenate([prefix_cache[0], asks], axis=0)


def attend_kernel(
    place_ref, query_ref, prefix_ref, text_ref, pages_ref, pick_ref, seen_ref, all_ref, out_ref, vision_ref
):
    pages = pages_ref[...]
    count = pages.shape[0]

    def pick(index):
        one_hot = lax.broadcasted_iota(jnp.int32, (index.shape[0], count), 1) == index
        one_hot = jnp.where(one_hot, 1.0, 0.0).astype(jnp.bfloat16)
        return jnp.dot(one_hot, pages, preferred_element_type=jnp.float32).astype(jnp.bfloat16)

    @pl.when(pl.program_id(0) == 0)
    def _():
        vision_ref[...] = pick(all_ref[...])

    window = pick(pick_ref[0])
    keys_values = jnp.concatenate([prefix_ref[0], window, text_ref[0]], axis=0)
    text_rows = text_ref.shape[1]
    heads = keys_values.shape[1] // (2 * HD)
    query = query_ref[0]
    for head in range(heads):
        keys = keys_values[:, 2 * head * HD : (2 * head + 1) * HD]
        values = keys_values[:, (2 * head + 1) * HD : (2 * head + 2) * HD]
        stacked = jnp.concatenate(
            [
                query[:, (head * GROUP + a) * HD : (head * GROUP + a + 1) * HD]
                for a in range(GROUP)
            ],
            axis=0,
        )
        scores = lax.dot_general(
            stacked, keys, (((1,), (1,)), ((), ())), preferred_element_type=jnp.float32
        ) * (HD**-0.5)
        row = lax.broadcasted_iota(jnp.int32, scores.shape, 0) % text_rows
        column = lax.broadcasted_iota(jnp.int32, scores.shape, 1)
        text_column = column - (scores.shape[1] - text_rows)
        allowed = (text_column <= row) & (seen_ref[0] > 0)
        scores = jnp.where(allowed, scores, -1e30)
        best = jnp.max(scores, axis=1, keepdims=True)
        weights = jnp.exp(scores - best)
        total = jnp.sum(weights, axis=1, keepdims=True)
        result = jnp.dot(weights.astype(jnp.bfloat16), values, preferred_element_type=jnp.float32)
        result = (result / total).astype(jnp.bfloat16)
        for a in range(GROUP):
            out_ref[0, :, (head * GROUP + a) * HD : (head * GROUP + a + 1) * HD] = result[
                a * text_rows : (a + 1) * text_rows
            ]


def attend(place, queries, prefixes, text_kv, pages, picks, seen, all_rows):
    docs, rows, width = queries.shape
    kv_width = text_kv.shape[2]
    vision_rows = all_rows.shape[0]
    keys = seen.shape[2]
    return pl.pallas_call(
        attend_kernel,
        grid_spec=pltpu.PrefetchScalarGridSpec(
            num_scalar_prefetch=1,
            grid=(docs,),
            in_specs=[
                pl.BlockSpec((1, rows, width), lambda d, place: (d, 0, 0)),
                pl.BlockSpec((1,) + prefixes.shape[1:], lambda d, place: (place[d], 0, 0)),
                pl.BlockSpec((1, rows, kv_width), lambda d, place: (d, 0, 0)),
                pl.BlockSpec(pages.shape, lambda d, place: (0, 0)),
                pl.BlockSpec((1,) + picks.shape[1:], lambda d, place: (d, 0, 0)),
                pl.BlockSpec((1, 1, keys), lambda d, place: (d, 0, 0)),
                pl.BlockSpec(all_rows.shape, lambda d, place: (0, 0)),
            ],
            out_specs=[
                pl.BlockSpec((1, rows, width), lambda d, place: (d, 0, 0)),
                pl.BlockSpec((vision_rows, kv_width), lambda d, place: (0, 0)),
            ],
        ),
        out_shape=[
            jax.ShapeDtypeStruct(queries.shape, jnp.bfloat16),
            jax.ShapeDtypeStruct((vision_rows, kv_width), jnp.bfloat16),
        ],
        compiler_params=pltpu.CompilerParams(vmem_limit_bytes=VMEM),
        cost_estimate=pl.CostEstimate(
            flops=4 * docs * rows * width * keys,
            bytes_accessed=8 * docs * rows * width,
            transcendentals=docs * rows * keys * width // HD,
        ),
    )(place, queries, prefixes, text_kv, pages, picks, seen, all_rows)


def shards(
    panels,
    w_merge,
    ln_gain,
    w_kv,
    page_src,
    page_tile,
    doc_pages,
    prefix_id,
    prefix_cache,
    queries,
    text_kv,
):
    seq_count = lax.axis_size("seq")
    holder = lax.axis_index("seq")
    tile_count, panel_rows, _ = panels.shape
    page_count = page_src.shape[0]
    capacity = max(2, 2 * page_count // seq_count)
    sources = page_src[:, 0]

    kv, squares, small = merge_tiles(
        panels, w_merge, ln_gain, w_kv, pack_small(prefix_cache, sources, page_tile)
    )
    width = seq_count // lax.axis_size("tp")
    small = small.reshape(seq_count, SMALL_ROWS, -1)

    def place_of(index):
        group = (index // width) ^ (holder // width)
        return group * width + (index - holder) % width

    prefix_rows = prefix_cache.shape[1]
    prefixes = small[:, :prefix_rows]
    place = place_of(jnp.arange(seq_count, dtype=jnp.int32))
    asked_sources = small[:, prefix_rows, :page_count].astype(jnp.int32)[place]
    asked_tiles = small[:, prefix_rows + 1, :page_count].astype(jnp.int32)[place]
    asked = (asked_sources == holder).astype(jnp.int32)
    order = jnp.cumsum(asked, axis=1) - 1
    slots = jnp.arange(capacity, dtype=jnp.int32)
    picked = asked[:, None, :] * (order[:, None, :] == slots[None, :, None]).astype(jnp.int32)
    wanted = jnp.sum(picked * asked_tiles[:, None, :], axis=2)
    within = jnp.arange(panel_rows, dtype=jnp.int32)
    wanted_rows = (wanted.reshape(-1, 1) * panel_rows + within[None, :]).reshape(-1)
    chooser = wanted_rows[:, None] == jnp.arange(tile_count * panel_rows, dtype=jnp.int32)[None, :]
    chooser = chooser.astype(jnp.bfloat16)

    position = jnp.arange(page_count, dtype=jnp.int32)
    earlier = (sources[:, None] == sources[None, :]) & (position[None, :] < position[:, None])
    rank = jnp.sum(earlier.astype(jnp.int32), axis=1)
    arrival = sources * capacity + rank
    all_rows = (arrival[:, None] * panel_rows + within[None, :]).reshape(-1, 1)
    lengths = doc_pages[0]
    starts = jnp.cumsum(lengths) - lengths
    step = jnp.arange(MOST_PAGES, dtype=jnp.int32)
    inside = step[None, :] < lengths[:, None]
    page = jnp.minimum(starts[:, None] + step[None, :], page_count - 1)
    doc_rows = arrival[page][:, :, None] * panel_rows + within[None, None, :]
    doc_rows = jnp.where(inside[:, :, None], doc_rows, -1)
    doc_count, query_rows, _ = queries.shape
    picks = doc_rows.reshape(doc_count, -1, 1)
    seen = jnp.concatenate(
        [
            jnp.ones((doc_count, prefixes.shape[1]), jnp.int32),
            (doc_rows >= 0).reshape(doc_count, -1).astype(jnp.int32),
            jnp.ones((doc_count, query_rows), jnp.int32),
        ],
        axis=1,
    )[:, None, :]

    kv, squares = scatter_heads(kv, squares)
    row_scale = lax.rsqrt(squares / D + 1e-06)
    tile_kv = (kv * row_scale[:, None]).astype(jnp.bfloat16)
    outgoing = jnp.dot(chooser, tile_kv, preferred_element_type=jnp.float32).astype(jnp.bfloat16)
    pages = lax.all_to_all(outgoing, "seq", split_axis=0, concat_axis=0, tiled=True)
    attended, vision_kv = attend(
        place_of(prefix_id), queries, prefixes, text_kv, pages, picks, seen, all_rows
    )
    return (attended, vision_kv)


def solution(mesh):
    return jax.shard_map(
        shards,
        mesh=mesh,
        in_specs=(
            P("seq", None, "tp"),
            P("seq", "tp"),
            P("tp"),
            P("tp", None),
            P("seq", None),
            P("seq"),
            P("seq", None),
            P("seq"),
            P("seq", None, "tp"),
            P("seq", None, "tp"),
            P("seq", None, "tp"),
        ),
        out_specs=(P("seq", None, "tp"), P("seq", "tp")),
        check_vma=False,
    )
```

```python
import functools

import jax
import jax.numpy as jnp
from jax import lax
from jax.experimental import pallas as pl
from jax.experimental.pallas import tpu as pltpu
from jax.sharding import PartitionSpec as P

D = 8192
HD = 128
GROUP = 8
MOST_PAGES = 16
VMEM = 16 * 1024 * 1024


def bits_of(count):
    return [1 << bit for bit in range(count.bit_length() - 1)]


def flip(value, axis, bit):
    count = lax.axis_size(axis)
    return lax.ppermute(value, axis, [(i, i ^ bit) for i in range(count)])


def transpose_panels(local, swap):
    seq_count, tp_count = lax.axis_size("seq"), lax.axis_size("tp")
    width = seq_count // tp_count
    half = tp_count // 2
    pairs = []
    for origin in range(tp_count):
        for inner in range(width):
            for block in range(tp_count):
                source = (origin * width + inner) * tp_count + (block ^ swap)
                slot = ((origin ^ block) & 1) * half + origin // 2
                pairs.append((source, (block * width + inner) * tp_count + slot))
    return lax.ppermute(local, ("seq", "tp"), pairs)


def share_panels(moved):
    held = [moved]
    bits = bits_of(lax.axis_size("tp"))
    for bit in bits[-1:] + bits[:-1]:
        held = held + [flip(piece, "tp", bit) for piece in held]
    return held


def panel_base():
    group = lax.axis_index("seq") // (lax.axis_size("seq") // lax.axis_size("tp"))
    place = lax.axis_index("tp")
    half = lax.axis_size("tp") // 2
    return 2 * (place % half) + ((place // half) ^ (group & 1))


def order_kernel(share, scalars_ref, *refs):
    out_ref = refs[-1]
    rows, depth = refs[0].shape
    members = depth // share
    for place in range(4):
        at = pl.ds(pl.multiple_of(scalars_ref[place] * rows, rows), rows)
        for member in range(members):
            if members == 1:
                out_ref[at, :] = refs[place][...]
            else:
                source = lax.rem(scalars_ref[4] + member, members)
                columns = pl.ds(pl.multiple_of(source * share, share), share)
                out_ref[at, member * share : (member + 1) * share] = refs[place][:, columns]


def order_rows(scalars, held, share):
    rows, depth = held[0].shape
    return pl.pallas_call(
        functools.partial(order_kernel, share),
        grid_spec=pltpu.PrefetchScalarGridSpec(
            num_scalar_prefetch=1,
            grid=(1,),
            in_specs=[pl.BlockSpec((rows, depth), lambda i, scalars: (0, 0))] * 4,
            out_specs=pl.BlockSpec((4 * rows, depth), lambda i, scalars: (0, 0)),
        ),
        out_shape=jax.ShapeDtypeStruct((4 * rows, depth), jnp.bfloat16),
        compiler_params=pltpu.CompilerParams(vmem_limit_bytes=VMEM),
        cost_estimate=pl.CostEstimate(flops=0, bytes_accessed=2 * depth, transcendentals=0),
    )(scalars, *held)


def partial_kernel(halves, *refs):
    rows_refs, weights_refs, out_refs = refs[:halves], refs[halves:-4], refs[-4:]
    weights = jnp.concatenate([ref[...] for ref in weights_refs], axis=0)
    for half, rows_ref in enumerate(rows_refs):
        total = jnp.dot(rows_ref[...], weights, preferred_element_type=jnp.float32)
        total = total.astype(jnp.bfloat16)
        rows = total.shape[0] // 4
        for k, out_ref in enumerate(out_refs):
            out_ref[half * rows : (half + 1) * rows] = total[k * rows : (k + 1) * rows]


def partial_products(held, weights, count):
    halves = len(held)
    rows, depth = held[0].shape
    tile = min(count, 512)

    def block(used, first):
        return pl.BlockSpec((used, tile), lambda i: (0, i + first // tile))

    out = halves * rows // 4
    return pl.pallas_call(
        functools.partial(partial_kernel, halves),
        grid=(count // tile,),
        in_specs=[pl.BlockSpec((rows, depth), lambda i: (0, 0))] * halves
        + [block(used, first) for _, used, first in weights],
        out_specs=[pl.BlockSpec((out, tile), lambda i: (0, i))] * 4,
        out_shape=[jax.ShapeDtypeStruct((out, count), jnp.bfloat16)] * 4,
        compiler_params=pltpu.CompilerParams(vmem_limit_bytes=VMEM),
        cost_estimate=pl.CostEstimate(flops=0, bytes_accessed=2 * count, transcendentals=0),
    )(*held, *[array for array, _, _ in weights])


def along(pairs):
    width = lax.axis_size("seq") // lax.axis_size("tp")
    return [(a * width + i, b * width + i) for a, b in pairs for i in range(width)]


def ride(value, extra):
    return jnp.concatenate([value] + extra, axis=0) if extra else value


def send_direct(parts, small):
    return [
        lax.ppermute(ride(part, small), "seq", along([(a, a ^ k) for a in range(4)]))
        for k, part in enumerate(parts[1:], 1)
    ]


def sum_direct(parts, arrived):
    rows = parts[0].shape[0]
    total = parts[0].astype(jnp.float32)
    for other in arrived:
        total = total + other[:rows]
    return total.astype(jnp.bfloat16)


PLAN = (((0,), 0, 4), ((1,), 0, 4), ((0, 1), 4, 4))
RIDE = 2


def merge_tiles(panels, w_merge, ln_gain, w_kv, small):
    seq_count, tp_count = lax.axis_size("seq"), lax.axis_size("tp")
    assert tp_count == 4 and seq_count % 4 == 0
    width = seq_count // tp_count
    tiles, panel_rows, depth = panels.shape
    share = w_merge.shape[0]
    group = lax.axis_index("seq") // width
    member = lax.axis_index("seq") % width
    local = panels.reshape(tiles * panel_rows, depth)
    half = local.shape[0] // 2
    swapped = flip(local[half:], "tp", 2)
    moved = [transpose_panels(local[:half], 0), transpose_panels(swapped, 2)]
    columns = w_merge.shape[1] // 2
    small = small.reshape(-1, columns)
    extra = small.shape[0]
    received = []
    for side in range(2):
        own = w_merge[:, side * columns : (side + 1) * columns]
        if side == 1:
            own = jnp.concatenate([own, small], axis=0)
            own, _ = lax.optimization_barrier((own, swapped))
        others = []
        for offset in range(1, width):
            pairs = [
                (g * width + (i + offset) % width, g * width + i)
                for g in range(tp_count)
                for i in range(width)
            ]
            others.append(lax.ppermute(own, "seq", pairs))
        received.append(others)
    aligned = width == 2 and share % 128 == 0
    if not aligned:
        share = depth
    places = panel_base() ^ jnp.arange(4, dtype=jnp.int32) ^ group
    scalars = jnp.concatenate([places, jnp.full((4,), member, jnp.int32)])
    early, _ = lax.optimization_barrier((moved[0], swapped))
    held = [order_rows(scalars, share_panels(early), share)]
    kv = [0.0, 0.0]
    squares = [0.0, 0.0]
    everyone = None
    eighth = w_merge.shape[1] // 8
    sent = []

    def finish(step):
        halves, first, count = PLAN[step]
        merged = sum_direct(*sent[step]).astype(jnp.float32)
        at = slice(first * eighth, (first + count) * eighth)
        gained = (merged * ln_gain[at].astype(jnp.float32)[None, :]).astype(jnp.bfloat16)
        squared = jnp.sum(merged * merged, axis=1)
        product = jnp.dot(gained, w_kv[at], preferred_element_type=jnp.float32)
        for i, h in enumerate(halves):
            squares[h] = squares[h] + squared[i * half : (i + 1) * half]
            kv[h] = kv[h] + product[i * half : (i + 1) * half]

    for step, (halves, first, count) in enumerate(PLAN):
        first, count = first * eighth, count * eighth
        if step == 1:
            late, _ = lax.optimization_barrier((moved[1], sent[0][0][0]))
            held.append(order_rows(scalars, share_panels(late), share))
        riding = []
        if step == RIDE:
            received[1], _ = lax.optimization_barrier((received[1], sent[step - 1][0][0]))
            small = [small] + [other[-extra:] for other in received[1]]
            small_shape = (width,) + small[0].shape
            riding = [jnp.stack(small).reshape(-1, count)]
        side = first // columns
        inside = first - side * columns
        if aligned:
            operands = [(w_merge, share, first), (received[side][0], share, inside)]
        else:
            parts = [w_merge[:, side * columns : (side + 1) * columns]]
            parts += [other[: w_merge.shape[0]] for other in received[side]]
            parts = jnp.concatenate(parts, axis=0)
            operands = [(jnp.roll(parts, member * w_merge.shape[0], axis=0), depth, inside)]
        parts = partial_products([held[h] for h in halves], operands, count)
        if step:
            before = [sent[step - 1][1][1]] + ([sent[step - 2][1][2]] if step >= 2 else [])
            parts, _ = lax.optimization_barrier((parts, before))
        sent.append((parts, send_direct(parts, riding)))
    for step in range(len(PLAN)):
        finish(step)
    rows = sent[RIDE][0][0].shape[0]
    everyone = riding + [other[rows:] for other in sent[RIDE][1]]
    everyone = jnp.stack(everyone).reshape((4,) + small_shape)
    return jnp.concatenate(kv), jnp.concatenate(squares), everyone


def scatter_heads(kv, squares):
    tp_count = lax.axis_size("tp")
    place = lax.axis_index("tp")
    rows = kv.shape[0]
    blocks = jnp.stack(jnp.split(kv, tp_count, axis=1))
    for bit in bits_of(tp_count):
        paired = blocks.reshape(blocks.shape[0] // 2, 2, rows, blocks.shape[2])
        mine = (place // bit) % 2
        keep = lax.dynamic_index_in_dim(paired, mine, 1, keepdims=False)
        give = lax.dynamic_index_in_dim(paired, 1 - mine, 1, keepdims=False)
        blocks = keep + flip(give.astype(jnp.bfloat16), "tp", bit).astype(jnp.float32)
        squares = squares + flip(squares, "tp", bit)
    return blocks[0], squares


SMALL_ROWS = 64


def pack_small(prefix_cache, sources, tiles):
    width = prefix_cache.shape[2]
    asks = jnp.stack([sources, tiles]).astype(jnp.bfloat16)
    rows = SMALL_ROWS - prefix_cache.shape[1]
    asks = jnp.pad(asks, ((0, rows - 2), (0, width - asks.shape[1])))
    return jnp.concatenate([prefix_cache[0], asks], axis=0)


def attend_kernel(
    place_ref, query_ref, prefix_ref, text_ref, pages_ref, pick_ref, seen_ref, all_ref, out_ref, vision_ref
):
    pages = pages_ref[...]
    count = pages.shape[0]

    def pick(index):
        one_hot = lax.broadcasted_iota(jnp.int32, (index.shape[0], count), 1) == index
        one_hot = jnp.where(one_hot, 1.0, 0.0).astype(jnp.bfloat16)
        return jnp.dot(one_hot, pages, preferred_element_type=jnp.float32).astype(jnp.bfloat16)

    @pl.when(pl.program_id(0) == 0)
    def _():
        vision_ref[...] = pick(all_ref[...])

    window = pick(pick_ref[0])
    keys_values = jnp.concatenate([prefix_ref[0], window, text_ref[0]], axis=0)
    text_rows = text_ref.shape[1]
    heads = keys_values.shape[1] // (2 * HD)
    query = query_ref[0]
    for head in range(heads):
        keys = keys_values[:, 2 * head * HD : (2 * head + 1) * HD]
        values = keys_values[:, (2 * head + 1) * HD : (2 * head + 2) * HD]
        stacked = jnp.concatenate(
            [
                query[:, (head * GROUP + a) * HD : (head * GROUP + a + 1) * HD]
                for a in range(GROUP)
            ],
            axis=0,
        )
        scores = lax.dot_general(
            stacked, keys, (((1,), (1,)), ((), ())), preferred_element_type=jnp.float32
        ) * (HD**-0.5)
        row = lax.broadcasted_iota(jnp.int32, scores.shape, 0) % text_rows
        column = lax.broadcasted_iota(jnp.int32, scores.shape, 1)
        text_column = column - (scores.shape[1] - text_rows)
        allowed = (text_column <= row) & (seen_ref[0] > 0)
        scores = jnp.where(allowed, scores, -1e30)
        best = jnp.max(scores, axis=1, keepdims=True)
        weights = jnp.exp(scores - best)
        total = jnp.sum(weights, axis=1, keepdims=True)
        result = jnp.dot(weights.astype(jnp.bfloat16), values, preferred_element_type=jnp.float32)
        result = (result / total).astype(jnp.bfloat16)
        for a in range(GROUP):
            out_ref[0, :, (head * GROUP + a) * HD : (head * GROUP + a + 1) * HD] = result[
                a * text_rows : (a + 1) * text_rows
            ]


def attend(place, queries, prefixes, text_kv, pages, picks, seen, all_rows):
    docs, rows, width = queries.shape
    kv_width = text_kv.shape[2]
    vision_rows = all_rows.shape[0]
    keys = seen.shape[2]
    return pl.pallas_call(
        attend_kernel,
        grid_spec=pltpu.PrefetchScalarGridSpec(
            num_scalar_prefetch=1,
            grid=(docs,),
            in_specs=[
                pl.BlockSpec((1, rows, width), lambda d, place: (d, 0, 0)),
                pl.BlockSpec((1,) + prefixes.shape[1:], lambda d, place: (place[d], 0, 0)),
                pl.BlockSpec((1, rows, kv_width), lambda d, place: (d, 0, 0)),
                pl.BlockSpec(pages.shape, lambda d, place: (0, 0)),
                pl.BlockSpec((1,) + picks.shape[1:], lambda d, place: (d, 0, 0)),
                pl.BlockSpec((1, 1, keys), lambda d, place: (d, 0, 0)),
                pl.BlockSpec(all_rows.shape, lambda d, place: (0, 0)),
            ],
            out_specs=[
                pl.BlockSpec((1, rows, width), lambda d, place: (d, 0, 0)),
                pl.BlockSpec((vision_rows, kv_width), lambda d, place: (0, 0)),
            ],
        ),
        out_shape=[
            jax.ShapeDtypeStruct(queries.shape, jnp.bfloat16),
            jax.ShapeDtypeStruct((vision_rows, kv_width), jnp.bfloat16),
        ],
        compiler_params=pltpu.CompilerParams(vmem_limit_bytes=VMEM),
        cost_estimate=pl.CostEstimate(
            flops=4 * docs * rows * width * keys,
            bytes_accessed=8 * docs * rows * width,
            transcendentals=docs * rows * keys * width // HD,
        ),
    )(place, queries, prefixes, text_kv, pages, picks, seen, all_rows)


def shards(
    panels,
    w_merge,
    ln_gain,
    w_kv,
    page_src,
    page_tile,
    doc_pages,
    prefix_id,
    prefix_cache,
    queries,
    text_kv,
):
    seq_count = lax.axis_size("seq")
    holder = lax.axis_index("seq")
    tile_count, panel_rows, _ = panels.shape
    page_count = page_src.shape[0]
    capacity = max(2, 2 * page_count // seq_count)
    sources = page_src[:, 0]

    kv, squares, small = merge_tiles(
        panels, w_merge, ln_gain, w_kv, pack_small(prefix_cache, sources, page_tile)
    )
    width = seq_count // lax.axis_size("tp")
    small = small.reshape(seq_count, SMALL_ROWS, -1)

    def place_of(index):
        group = (index // width) ^ (holder // width)
        return group * width + (index - holder) % width

    prefix_rows = prefix_cache.shape[1]
    prefixes = small[:, :prefix_rows]
    place = place_of(jnp.arange(seq_count, dtype=jnp.int32))
    asked_sources = small[:, prefix_rows, :page_count].astype(jnp.int32)[place]
    asked_tiles = small[:, prefix_rows + 1, :page_count].astype(jnp.int32)[place]
    asked = (asked_sources == holder).astype(jnp.int32)
    order = jnp.cumsum(asked, axis=1) - 1
    slots = jnp.arange(capacity, dtype=jnp.int32)
    picked = asked[:, None, :] * (order[:, None, :] == slots[None, :, None]).astype(jnp.int32)
    wanted = jnp.sum(picked * asked_tiles[:, None, :], axis=2)
    within = jnp.arange(panel_rows, dtype=jnp.int32)
    wanted_rows = (wanted.reshape(-1, 1) * panel_rows + within[None, :]).reshape(-1)
    chooser = wanted_rows[:, None] == jnp.arange(tile_count * panel_rows, dtype=jnp.int32)[None, :]
    chooser = chooser.astype(jnp.bfloat16)

    position = jnp.arange(page_count, dtype=jnp.int32)
    earlier = (sources[:, None] == sources[None, :]) & (position[None, :] < position[:, None])
    rank = jnp.sum(earlier.astype(jnp.int32), axis=1)
    arrival = sources * capacity + rank
    all_rows = (arrival[:, None] * panel_rows + within[None, :]).reshape(-1, 1)
    lengths = doc_pages[0]
    starts = jnp.cumsum(lengths) - lengths
    step = jnp.arange(MOST_PAGES, dtype=jnp.int32)
    inside = step[None, :] < lengths[:, None]
    page = jnp.minimum(starts[:, None] + step[None, :], page_count - 1)
    doc_rows = arrival[page][:, :, None] * panel_rows + within[None, None, :]
    doc_rows = jnp.where(inside[:, :, None], doc_rows, -1)
    doc_count, query_rows, _ = queries.shape
    picks = doc_rows.reshape(doc_count, -1, 1)
    seen = jnp.concatenate(
        [
            jnp.ones((doc_count, prefixes.shape[1]), jnp.int32),
            (doc_rows >= 0).reshape(doc_count, -1).astype(jnp.int32),
            jnp.ones((doc_count, query_rows), jnp.int32),
        ],
        axis=1,
    )[:, None, :]

    kv, squares = scatter_heads(kv, squares)
    row_scale = lax.rsqrt(squares / D + 1e-06)
    tile_kv = (kv * row_scale[:, None]).astype(jnp.bfloat16)
    outgoing = jnp.dot(chooser, tile_kv, preferred_element_type=jnp.float32).astype(jnp.bfloat16)
    pages = lax.all_to_all(outgoing, "seq", split_axis=0, concat_axis=0, tiled=True)
    attended, vision_kv = attend(
        place_of(prefix_id), queries, prefixes, text_kv, pages, picks, seen, all_rows
    )
    return (attended, vision_kv)


def solution(mesh):
    return jax.shard_map(
        shards,
        mesh=mesh,
        in_specs=(
            P("seq", None, "tp"),
            P("seq", "tp"),
            P("tp"),
            P("tp", None),
            P("seq", None),
            P("seq"),
            P("seq", None),
            P("seq"),
            P("seq", None, "tp"),
            P("seq", None, "tp"),
            P("seq", None, "tp"),
        ),
        out_specs=(P("seq", None, "tp"), P("seq", "tp")),
        check_vma=False,
    )
```

```python
import functools

import jax
import jax.numpy as jnp
from jax import lax
from jax.experimental import pallas as pl
from jax.experimental.pallas import tpu as pltpu
from jax.sharding import PartitionSpec as P

D = 8192
HD = 128
GROUP = 8
MOST_PAGES = 16
VMEM = 16 * 1024 * 1024


def bits_of(count):
    return [1 << bit for bit in range(count.bit_length() - 1)]


def flip(value, axis, bit):
    count = lax.axis_size(axis)
    return lax.ppermute(value, axis, [(i, i ^ bit) for i in range(count)])


def transpose_panels(local, swap):
    seq_count, tp_count = lax.axis_size("seq"), lax.axis_size("tp")
    width = seq_count // tp_count
    half = tp_count // 2
    pairs = []
    for origin in range(tp_count):
        for inner in range(width):
            for block in range(tp_count):
                source = (origin * width + inner) * tp_count + (block ^ swap)
                slot = ((origin ^ block) & 1) * half + origin // 2
                pairs.append((source, (block * width + inner) * tp_count + slot))
    return lax.ppermute(local, ("seq", "tp"), pairs)


def share_panels(moved):
    held = [moved]
    bits = bits_of(lax.axis_size("tp"))
    for bit in bits[-1:] + bits[:-1]:
        held = held + [flip(piece, "tp", bit) for piece in held]
    return held


def panel_base():
    group = lax.axis_index("seq") // (lax.axis_size("seq") // lax.axis_size("tp"))
    place = lax.axis_index("tp")
    half = lax.axis_size("tp") // 2
    return 2 * (place % half) + ((place // half) ^ (group & 1))


def order_kernel(share, scalars_ref, *refs):
    out_ref = refs[-1]
    rows, depth = refs[0].shape
    members = depth // share
    for place in range(4):
        at = pl.ds(pl.multiple_of(scalars_ref[place] * rows, rows), rows)
        for member in range(members):
            if members == 1:
                out_ref[at, :] = refs[place][...]
            else:
                source = lax.rem(scalars_ref[4] + member, members)
                columns = pl.ds(pl.multiple_of(source * share, share), share)
                out_ref[at, member * share : (member + 1) * share] = refs[place][:, columns]


def order_rows(scalars, held, share):
    rows, depth = held[0].shape
    return pl.pallas_call(
        functools.partial(order_kernel, share),
        grid_spec=pltpu.PrefetchScalarGridSpec(
            num_scalar_prefetch=1,
            grid=(1,),
            in_specs=[pl.BlockSpec((rows, depth), lambda i, scalars: (0, 0))] * 4,
            out_specs=pl.BlockSpec((4 * rows, depth), lambda i, scalars: (0, 0)),
        ),
        out_shape=jax.ShapeDtypeStruct((4 * rows, depth), jnp.bfloat16),
        compiler_params=pltpu.CompilerParams(vmem_limit_bytes=VMEM),
        cost_estimate=pl.CostEstimate(flops=0, bytes_accessed=2 * depth, transcendentals=0),
    )(scalars, *held)


def partial_kernel(halves, *refs):
    rows_refs, own_ref, others, out_refs = refs[:halves], refs[halves], refs[halves + 1 : -4], refs[-4:]

    def multiply(weights):
        for half, rows_ref in enumerate(rows_refs):
            total = jnp.dot(rows_ref[...], weights, preferred_element_type=jnp.float32)
            total = total.astype(jnp.bfloat16)
            rows = total.shape[0] // 4
            for k, out_ref in enumerate(out_refs):
                out_ref[half * rows : (half + 1) * rows] = total[k * rows : (k + 1) * rows]

    def joined(other):
        return multiply(jnp.concatenate([own_ref[...], other[...]], axis=0))

    if not others:
        multiply(own_ref[...])
    elif len(others) == 1:
        joined(others[0])
    else:
        for index, other in enumerate(others):
            pl.when(pl.program_id(0) == index)(functools.partial(joined, other))


def partial_products(held, operands, count):
    array, first, others = operands
    halves = len(held)
    rows, depth = held[0].shape
    tile = min(count, 512)
    used = depth // 2 if others else depth
    if len(others) > 1:
        assert all(other.shape[1] == tile for other in others)
    out = halves * rows // 4
    return pl.pallas_call(
        functools.partial(partial_kernel, halves),
        grid=(count // tile,),
        in_specs=[pl.BlockSpec((rows, depth), lambda i: (0, 0))] * halves
        + [pl.BlockSpec((used, tile), lambda i: (0, i + first // tile))]
        + [
            pl.BlockSpec((used, tile), (lambda i: (0, 0)) if len(others) > 1 else (lambda i: (0, i)))
            for _ in others
        ],
        out_specs=[pl.BlockSpec((out, tile), lambda i: (0, i))] * 4,
        out_shape=[jax.ShapeDtypeStruct((out, count), jnp.bfloat16)] * 4,
        compiler_params=pltpu.CompilerParams(vmem_limit_bytes=VMEM),
        cost_estimate=pl.CostEstimate(flops=0, bytes_accessed=2 * count, transcendentals=0),
    )(*held, array, *others)


def along(pairs):
    width = lax.axis_size("seq") // lax.axis_size("tp")
    return [(a * width + i, b * width + i) for a, b in pairs for i in range(width)]


def ride(value, extra):
    return jnp.concatenate([value] + extra, axis=0) if extra else value


def send_direct(parts, small):
    return [
        lax.ppermute(ride(part, small), "seq", along([(a, a ^ k) for a in range(4)]))
        for k, part in enumerate(parts[1:], 1)
    ]


def sum_direct(parts, arrived):
    rows = parts[0].shape[0]
    total = parts[0].astype(jnp.float32)
    for other in arrived:
        total = total + other[:rows]
    return total.astype(jnp.bfloat16)


PLAN = (((0,), 0, 2), ((0,), 2, 2), ((1,), 0, 4), ((0, 1), 4, 4))
RIDE = 3
WEIGHT_PARTS = (2, 2, 4)


def merge_tiles(panels, w_merge, ln_gain, w_kv, small):
    seq_count, tp_count = lax.axis_size("seq"), lax.axis_size("tp")
    assert tp_count == 4 and seq_count % 4 == 0
    width = seq_count // tp_count
    tiles, panel_rows, depth = panels.shape
    share = w_merge.shape[0]
    group = lax.axis_index("seq") // width
    member = lax.axis_index("seq") % width
    local = panels.reshape(tiles * panel_rows, depth)
    half = local.shape[0] // 2
    swapped = flip(local[half:], "tp", 2)
    moved = [transpose_panels(local[:half], 0), transpose_panels(swapped, 2)]
    eighth = w_merge.shape[1] // 8
    small = small.reshape(-1, WEIGHT_PARTS[-1] * eighth)
    extra = small.shape[0]
    received = []
    for index, part in enumerate(WEIGHT_PARTS):
        first = sum(WEIGHT_PARTS[:index]) * eighth
        own = w_merge[:, first : first + part * eighth]
        if index == len(WEIGHT_PARTS) - 1:
            own = jnp.concatenate([own, small], axis=0)
        if index:
            own, _ = lax.optimization_barrier((own, swapped))
        others = []
        for offset in range(1, width):
            pairs = [
                (g * width + (i + offset) % width, g * width + i)
                for g in range(tp_count)
                for i in range(width)
            ]
            others.append(lax.ppermute(own, "seq", pairs))
        received.append(others)
    aligned = width == 2 and share % 128 == 0
    if not aligned:
        share = depth
    places = panel_base() ^ jnp.arange(4, dtype=jnp.int32) ^ group
    scalars = jnp.concatenate([places, jnp.full((4,), member, jnp.int32)])
    early, _ = lax.optimization_barrier((moved[0], swapped))
    held = [order_rows(scalars, share_panels(early), share)]
    sent = []

    def finish(step):
        _, first, count = PLAN[step]
        merged = sum_direct(*sent[step]).astype(jnp.float32)
        at = slice(first * eighth, (first + count) * eighth)
        gained = (merged * ln_gain[at].astype(jnp.float32)[None, :]).astype(jnp.bfloat16)
        squared = jnp.sum(merged * merged, axis=1)
        return squared, jnp.dot(gained, w_kv[at], preferred_element_type=jnp.float32)

    for step, (halves, first, count) in enumerate(PLAN):
        if step == 2:
            late, _ = lax.optimization_barrier((moved[1], sent[0][0][0]))
            held.append(order_rows(scalars, share_panels(late), share))
        riding = []
        if step == RIDE:
            received[-1], _ = lax.optimization_barrier((received[-1], sent[step - 1][0][0]))
            small = [small] + [other[-extra:] for other in received[-1]]
            small_shape = (width,) + small[0].shape
            riding = [jnp.stack(small).reshape(-1, count * eighth)]
        others = []
        for index, part in enumerate(WEIGHT_PARTS):
            begin = sum(WEIGHT_PARTS[:index])
            if begin < first + count and begin + part > first:
                others.append(received[index])
        own = w_merge[:, first * eighth : (first + count) * eighth]
        if aligned:
            operands = (w_merge, first * eighth, [other[0] for other in others])
        else:
            rows = [own] + [
                jnp.concatenate([other[i][: own.shape[0]] for other in others], axis=1)
                for i in range(width - 1)
            ]
            rows = jnp.concatenate(rows, axis=0)
            operands = (jnp.roll(rows, member * own.shape[0], axis=0), 0, [])
        parts = partial_products([held[h] for h in halves], operands, count * eighth)
        if step:
            before = [sent[step - 1][1][1]] + ([sent[step - 2][1][2]] if step >= 2 else [])
            parts, _ = lax.optimization_barrier((parts, before))
        sent.append((parts, send_direct(parts, riding)))
    done = [finish(step) for step in range(len(PLAN))]
    squares, kv = [
        jnp.concatenate([done[0][i] + done[1][i], done[2][i]], axis=0) + done[3][i] for i in range(2)
    ]
    rows = sent[RIDE][0][0].shape[0]
    everyone = riding + [other[rows:] for other in sent[RIDE][1]]
    everyone = jnp.stack(everyone).reshape((4,) + small_shape)
    return kv, squares, everyone


def scatter_heads(kv, squares):
    tp_count = lax.axis_size("tp")
    place = lax.axis_index("tp")
    width = kv.shape[1] // tp_count
    blocks = None
    for bit in bits_of(tp_count):
        mine = (place // bit) % 2

        def half(which):
            if blocks is not None:
                paired = blocks.reshape((-1, 2) + blocks.shape[1:])
                return lax.dynamic_index_in_dim(paired, which, 1, keepdims=False)
            columns = [
                lax.dynamic_slice_in_dim(kv, (2 * i + which) * width, width, axis=1)
                for i in range(tp_count // 2)
            ]
            return jnp.stack(columns)

        arrived = flip(half(1 - mine).astype(jnp.bfloat16), "tp", bit)
        blocks = half(mine) + arrived.astype(jnp.float32)
        squares = squares + flip(squares, "tp", bit)
    return blocks[0], squares


SMALL_ROWS = 64


def pack_small(prefix_cache, sources, tiles):
    width = prefix_cache.shape[2]
    asks = jnp.stack([sources, tiles]).astype(jnp.bfloat16)
    rows = SMALL_ROWS - prefix_cache.shape[1]
    asks = jnp.pad(asks, ((0, rows - 2), (0, width - asks.shape[1])))
    return jnp.concatenate([prefix_cache[0], asks], axis=0)


def attend_kernel(
    place_ref, query_ref, prefix_ref, text_ref, pages_ref, pick_ref, all_ref, out_ref, vision_ref
):
    pages = pages_ref[...]
    count = pages.shape[0]

    def pick(index):
        one_hot = lax.broadcasted_iota(jnp.int32, (index.shape[0], count), 1) == index
        one_hot = jnp.where(one_hot, 1.0, 0.0).astype(jnp.bfloat16)
        return jnp.dot(one_hot, pages, preferred_element_type=jnp.float32).astype(jnp.bfloat16)

    @pl.when(pl.program_id(0) == 0)
    def _():
        vision_ref[...] = pick(all_ref[...])

    picked = pick_ref[0]
    window = pick(picked)
    text = text_ref[0]
    text_rows = text.shape[0]
    keys_values = jnp.concatenate([prefix_ref[0], window, text], axis=0)
    heads = keys_values.shape[1] // (2 * HD)
    query = query_ref[0]
    scale = HD**-0.5
    first = prefix_ref.shape[1]
    second = first + window.shape[0]
    for head in range(heads):
        keys = keys_values[:, 2 * head * HD : (2 * head + 1) * HD]
        values = keys_values[:, (2 * head + 1) * HD : (2 * head + 2) * HD]
        stacked = jnp.concatenate(
            [
                query[:, (head * GROUP + a) * HD : (head * GROUP + a + 1) * HD]
                for a in range(GROUP)
            ],
            axis=0,
        )
        scores = scale * lax.dot_general(
            keys, stacked, (((1,), (1,)), ((), ())), preferred_element_type=jnp.float32
        )
        shape = (text_rows, scores.shape[1])
        key_row = lax.broadcasted_iota(jnp.int32, shape, 0)
        query_row = lax.broadcasted_iota(jnp.int32, shape, 1) % text_rows
        scores = jnp.concatenate(
            [
                scores[:first],
                jnp.where(picked >= 0, scores[first:second], -1e30),
                jnp.where(key_row <= query_row, scores[second:], -1e30),
            ],
            axis=0,
        )
        weights = jnp.exp(scores - jnp.max(scores, axis=0, keepdims=True))
        total = jnp.sum(weights, axis=0, keepdims=True)
        result = lax.dot_general(
            values,
            weights.astype(jnp.bfloat16),
            (((0,), (0,)), ((), ())),
            preferred_element_type=jnp.float32,
        )
        result = result / total
        for a in range(GROUP):
            out_ref[0, :, (head * GROUP + a) * HD : (head * GROUP + a + 1) * HD] = (
                result[:, a * text_rows : (a + 1) * text_rows].T.astype(jnp.bfloat16)
            )


def attend(place, queries, prefixes, text_kv, pages, picks, all_rows):
    docs, rows, width = queries.shape
    kv_width = text_kv.shape[2]
    vision_rows = all_rows.shape[0]
    keys = prefixes.shape[1] + picks.shape[1] + rows
    return pl.pallas_call(
        attend_kernel,
        grid_spec=pltpu.PrefetchScalarGridSpec(
            num_scalar_prefetch=1,
            grid=(docs,),
            in_specs=[
                pl.BlockSpec((1, rows, width), lambda d, place: (d, 0, 0)),
                pl.BlockSpec((1,) + prefixes.shape[1:], lambda d, place: (place[d], 0, 0)),
                pl.BlockSpec((1, rows, kv_width), lambda d, place: (d, 0, 0)),
                pl.BlockSpec(pages.shape, lambda d, place: (0, 0)),
                pl.BlockSpec((1,) + picks.shape[1:], lambda d, place: (d, 0, 0)),
                pl.BlockSpec(all_rows.shape, lambda d, place: (0, 0)),
            ],
            out_specs=[
                pl.BlockSpec((1, rows, width), lambda d, place: (d, 0, 0)),
                pl.BlockSpec((vision_rows, kv_width), lambda d, place: (0, 0)),
            ],
        ),
        out_shape=[
            jax.ShapeDtypeStruct(queries.shape, jnp.bfloat16),
            jax.ShapeDtypeStruct((vision_rows, kv_width), jnp.bfloat16),
        ],
        compiler_params=pltpu.CompilerParams(vmem_limit_bytes=VMEM),
        cost_estimate=pl.CostEstimate(
            flops=4 * docs * rows * width * keys,
            bytes_accessed=8 * docs * rows * width,
            transcendentals=docs * rows * keys * width // HD,
        ),
    )(place, queries, prefixes, text_kv, pages, picks, all_rows)


def shards(
    panels,
    w_merge,
    ln_gain,
    w_kv,
    page_src,
    page_tile,
    doc_pages,
    prefix_id,
    prefix_cache,
    queries,
    text_kv,
):
    seq_count = lax.axis_size("seq")
    holder = lax.axis_index("seq")
    tile_count, panel_rows, _ = panels.shape
    page_count = page_src.shape[0]
    capacity = max(2, 2 * page_count // seq_count)
    sources = page_src[:, 0]

    kv, squares, small = merge_tiles(
        panels, w_merge, ln_gain, w_kv, pack_small(prefix_cache, sources, page_tile)
    )
    width = seq_count // lax.axis_size("tp")
    small = small.reshape(seq_count, SMALL_ROWS, -1)

    def place_of(index):
        group = (index // width) ^ (holder // width)
        return group * width + (index - holder) % width

    prefix_rows = prefix_cache.shape[1]
    prefixes = small[:, :prefix_rows]
    place = place_of(jnp.arange(seq_count, dtype=jnp.int32))
    asked_sources = small[:, prefix_rows, :page_count].astype(jnp.int32)[place]
    asked_tiles = small[:, prefix_rows + 1, :page_count].astype(jnp.int32)[place]
    asked = (asked_sources == holder).astype(jnp.int32)
    order = jnp.cumsum(asked, axis=1) - 1
    slots = jnp.arange(capacity, dtype=jnp.int32)
    picked = asked[:, None, :] * (order[:, None, :] == slots[None, :, None]).astype(jnp.int32)
    wanted = jnp.sum(picked * asked_tiles[:, None, :], axis=2)
    within = jnp.arange(panel_rows, dtype=jnp.int32)
    wanted_rows = (wanted.reshape(-1, 1) * panel_rows + within[None, :]).reshape(-1)
    chooser = wanted_rows[:, None] == jnp.arange(tile_count * panel_rows, dtype=jnp.int32)[None, :]
    chooser = chooser.astype(jnp.bfloat16)

    position = jnp.arange(page_count, dtype=jnp.int32)
    earlier = (sources[:, None] == sources[None, :]) & (position[None, :] < position[:, None])
    rank = jnp.sum(earlier.astype(jnp.int32), axis=1)
    arrival = sources * capacity + rank
    all_rows = (arrival[:, None] * panel_rows + within[None, :]).reshape(-1, 1)
    lengths = doc_pages[0]
    starts = jnp.cumsum(lengths) - lengths
    step = jnp.arange(MOST_PAGES, dtype=jnp.int32)
    inside = step[None, :] < lengths[:, None]
    page = jnp.minimum(starts[:, None] + step[None, :], page_count - 1)
    doc_rows = arrival[page][:, :, None] * panel_rows + within[None, None, :]
    doc_rows = jnp.where(inside[:, :, None], doc_rows, -1)
    doc_count, query_rows, _ = queries.shape
    picks = doc_rows.reshape(doc_count, -1, 1)
    kv, squares = scatter_heads(kv, squares)
    row_scale = lax.rsqrt(squares / D + 1e-06)
    tile_kv = (kv * row_scale[:, None]).astype(jnp.bfloat16)
    outgoing = jnp.dot(chooser, tile_kv, preferred_element_type=jnp.float32).astype(jnp.bfloat16)
    pages = lax.all_to_all(outgoing, "seq", split_axis=0, concat_axis=0, tiled=True)
    attended, vision_kv = attend(
        place_of(prefix_id), queries, prefixes, text_kv, pages, picks, all_rows
    )
    return (attended, vision_kv)


def solution(mesh):
    return jax.shard_map(
        shards,
        mesh=mesh,
        in_specs=(
            P("seq", None, "tp"),
            P("seq", "tp"),
            P("tp"),
            P("tp", None),
            P("seq", None),
            P("seq"),
            P("seq", None),
            P("seq"),
            P("seq", None, "tp"),
            P("seq", None, "tp"),
            P("seq", None, "tp"),
        ),
        out_specs=(P("seq", None, "tp"), P("seq", "tp")),
        check_vma=False,
    )
```

```python
import functools

import jax
import jax.numpy as jnp
from jax import lax
from jax.experimental import pallas as pl
from jax.experimental.pallas import tpu as pltpu
from jax.sharding import PartitionSpec as P

D = 8192
HD = 128
GROUP = 8
MOST_PAGES = 16
VMEM = 16 * 1024 * 1024


def bits_of(count):
    return [1 << bit for bit in range(count.bit_length() - 1)]


def flip(value, axis, bit):
    count = lax.axis_size(axis)
    return lax.ppermute(value, axis, [(i, i ^ bit) for i in range(count)])


def transpose_panels(local, swap):
    seq_count, tp_count = lax.axis_size("seq"), lax.axis_size("tp")
    width = seq_count // tp_count
    half = tp_count // 2
    pairs = []
    for origin in range(tp_count):
        for inner in range(width):
            for block in range(tp_count):
                source = (origin * width + inner) * tp_count + (block ^ swap)
                slot = ((origin ^ block) & 1) * half + origin // 2
                pairs.append((source, (block * width + inner) * tp_count + slot))
    return lax.ppermute(local, ("seq", "tp"), pairs)


def share_panels(moved):
    held = [moved]
    bits = bits_of(lax.axis_size("tp"))
    for bit in bits[-1:] + bits[:-1]:
        held = held + [flip(piece, "tp", bit) for piece in held]
    return held


def panel_base():
    group = lax.axis_index("seq") // (lax.axis_size("seq") // lax.axis_size("tp"))
    place = lax.axis_index("tp")
    half = lax.axis_size("tp") // 2
    return 2 * (place % half) + ((place // half) ^ (group & 1))


def order_kernel(share, scalars_ref, *refs):
    out_ref = refs[-1]
    rows, depth = refs[0].shape
    members = depth // share
    for place in range(4):
        at = pl.ds(pl.multiple_of(scalars_ref[place] * rows, rows), rows)
        for member in range(members):
            if members == 1:
                out_ref[at, :] = refs[place][...]
            else:
                source = lax.rem(scalars_ref[4] + member, members)
                columns = pl.ds(pl.multiple_of(source * share, share), share)
                out_ref[at, member * share : (member + 1) * share] = refs[place][:, columns]


def order_rows(scalars, held, share):
    rows, depth = held[0].shape
    return pl.pallas_call(
        functools.partial(order_kernel, share),
        grid_spec=pltpu.PrefetchScalarGridSpec(
            num_scalar_prefetch=1,
            grid=(1,),
            in_specs=[pl.BlockSpec((rows, depth), lambda i, scalars: (0, 0))] * 4,
            out_specs=pl.BlockSpec((4 * rows, depth), lambda i, scalars: (0, 0)),
        ),
        out_shape=jax.ShapeDtypeStruct((4 * rows, depth), jnp.bfloat16),
        compiler_params=pltpu.CompilerParams(vmem_limit_bytes=VMEM),
        cost_estimate=pl.CostEstimate(flops=0, bytes_accessed=2 * depth, transcendentals=0),
    )(scalars, *held)


def partial_kernel(halves, groups, *refs):
    inputs = len(refs) - len(groups)
    rows_refs, weights_refs, out_refs = refs[:halves], refs[halves:inputs], refs[inputs:]
    weights = jnp.concatenate([ref[...] for ref in weights_refs], axis=0)
    for half, rows_ref in enumerate(rows_refs):
        total = jnp.dot(rows_ref[...], weights, preferred_element_type=jnp.float32)
        total = total.astype(jnp.bfloat16)
        rows = total.shape[0] // 4
        for out_ref, members in zip(out_refs, groups):
            for i, k in enumerate(members):
                to = (i * halves + half) * rows
                out_ref[to : to + rows] = total[k * rows : (k + 1) * rows]


def partial_products(held, weights, count, groups):
    halves = len(held)
    rows, depth = held[0].shape
    tile = min(count, 512)

    def block(used, first):
        return pl.BlockSpec((used, tile), lambda i: (0, i + first // tile))

    outs = [len(members) * halves * rows // 4 for members in groups]
    return pl.pallas_call(
        functools.partial(partial_kernel, halves, groups),
        grid=(count // tile,),
        in_specs=[pl.BlockSpec((rows, depth), lambda i: (0, 0))] * halves
        + [block(used, first) for _, used, first in weights],
        out_specs=[pl.BlockSpec((out, tile), lambda i: (0, i)) for out in outs],
        out_shape=[jax.ShapeDtypeStruct((out, count), jnp.bfloat16) for out in outs],
        compiler_params=pltpu.CompilerParams(vmem_limit_bytes=VMEM),
        cost_estimate=pl.CostEstimate(flops=0, bytes_accessed=2 * count, transcendentals=0),
    )(*held, *[array for array, _, _ in weights])


def along(pairs):
    width = lax.axis_size("seq") // lax.axis_size("tp")
    return [(a * width + i, b * width + i) for a, b in pairs for i in range(width)]


INWARD = ((0, 1), (3, 2))
OUTWARD = ((1, 0), (2, 3))
ACROSS = ((1, 2), (2, 1))
BEYOND = ((1, 3), (2, 0))


def send_direct(parts):
    return [
        lax.ppermute(part, "seq", along([(a, a ^ k) for a in range(4)]))
        for k, part in enumerate(parts[1:], 1)
    ]


def sum_direct(parts, arrived):
    total = parts[0].astype(jnp.float32)
    for other in arrived:
        total = total + other
    return total.astype(jnp.bfloat16)


def ride(value, extra):
    return jnp.concatenate([value] + extra, axis=0) if extra else value


def send_sums(parts, small):
    _, others, first = parts
    inward = lax.ppermute(ride(others, small), "seq", along(INWARD))
    outward = lax.ppermute(ride(first, small), "seq", along(OUTWARD))
    return inward, outward


def finish_sums(parts, arrived, is_end, small):
    own, others, _ = parts
    inward, outward = arrived
    rows = own.shape[0]

    def add(mine, other):
        return (mine.astype(jnp.float32) + other.astype(jnp.float32)).astype(jnp.bfloat16)

    def part(value, first, index=0):
        count = small[0].shape[0]
        return value[first + index * count : first + (index + 1) * count]

    extra = [part(inward, 3 * rows)] + small if small else []
    beyond = add(others[rows : 2 * rows], inward[2 * rows : 3 * rows])
    beyond = lax.ppermute(ride(beyond, extra), "seq", along(BEYOND))
    across = add(others[2 * rows :], inward[rows : 2 * rows])
    across = lax.ppermute(ride(across, extra), "seq", along(ACROSS))
    mine = own.astype(jnp.float32)
    at_end = mine + outward[:rows] + beyond[:rows]
    at_middle = mine + inward[:rows] + across[:rows]
    shared = None
    if small:
        ends = [part(outward, rows), part(beyond, rows, 1), part(beyond, rows, 0)]
        middles = [part(inward, 3 * rows), part(across, rows, 0), part(across, rows, 1)]
        shared = small + [jnp.where(is_end, e, m) for e, m in zip(ends, middles)]
    return jnp.where(is_end, at_end, at_middle).astype(jnp.bfloat16), shared


PLAN = (((0,), 0, 4, True), ((1,), 0, 4, True), ((0, 1), 4, 2, False), ((0, 1), 6, 2, False))
RIDE = 2


def merge_tiles(panels, w_merge, ln_gain, w_kv, small):
    seq_count, tp_count = lax.axis_size("seq"), lax.axis_size("tp")
    assert tp_count == 4 and seq_count % 4 == 0
    width = seq_count // tp_count
    tiles, panel_rows, depth = panels.shape
    share = w_merge.shape[0]
    group = lax.axis_index("seq") // width
    member = lax.axis_index("seq") % width
    is_end = (group == 0) | (group == 3)
    local = panels.reshape(tiles * panel_rows, depth)
    half = local.shape[0] // 2
    swapped = flip(local[half:], "tp", 2)
    moved = [transpose_panels(local[:half], 0), transpose_panels(swapped, 2)]
    columns = w_merge.shape[1] // 2
    small = small.reshape(-1, columns)
    extra = small.shape[0]
    received = []
    for side in range(2):
        own = w_merge[:, side * columns : (side + 1) * columns]
        if side == 1:
            own = jnp.concatenate([own, small], axis=0)
            own, _ = lax.optimization_barrier((own, swapped))
        others = []
        for offset in range(1, width):
            pairs = [
                (g * width + (i + offset) % width, g * width + i)
                for g in range(tp_count)
                for i in range(width)
            ]
            others.append(lax.ppermute(own, "seq", pairs))
        received.append(others)
    aligned = width == 2 and share % 128 == 0
    if not aligned:
        share = depth
    places = panel_base() ^ jnp.arange(4, dtype=jnp.int32) ^ group
    scalars = jnp.concatenate([places, jnp.full((4,), member, jnp.int32)])
    early, _ = lax.optimization_barrier((moved[0], swapped))
    held = [order_rows(scalars, share_panels(early), share)]
    eighth = w_merge.shape[1] // 8
    sent = []

    def finish(step, merged):
        _, first, count, _ = PLAN[step]
        merged = merged.astype(jnp.float32)
        at = slice(first * eighth, (first + count) * eighth)
        gained = (merged * ln_gain[at].astype(jnp.float32)[None, :]).astype(jnp.bfloat16)
        squared = jnp.sum(merged * merged, axis=1)
        return squared, jnp.dot(gained, w_kv[at], preferred_element_type=jnp.float32)

    riding = []
    for step, (halves, first, count, direct) in enumerate(PLAN):
        first, count = first * eighth, count * eighth
        if step == 1:
            late, _ = lax.optimization_barrier((moved[1], sent[0][0][0]))
            held.append(order_rows(scalars, share_panels(late), share))
        if step == RIDE:
            received[1], _ = lax.optimization_barrier((received[1], sent[step - 1][1][0]))
            small = [small] + [other[-extra:] for other in received[1]]
            small_shape = (width,) + small[0].shape
            riding = [jnp.stack(small).reshape(-1, count)]
        side = first // columns
        inside = first - side * columns
        if aligned:
            operands = [(w_merge, share, first), (received[side][0], share, inside)]
        else:
            parts = [w_merge[:, side * columns : (side + 1) * columns]]
            parts += [other[: w_merge.shape[0]] for other in received[side]]
            parts = jnp.concatenate(parts, axis=0)
            operands = [(jnp.roll(parts, member * w_merge.shape[0], axis=0), depth, inside)]
        groups = ((0,), (1,), (2,), (3,)) if direct else ((0,), (1, 2, 3), (1,))
        parts = partial_products([held[h] for h in halves], operands, count, groups)
        if step == 1:
            parts, _ = lax.optimization_barrier((parts, sent[0][1][1]))
        elif step:
            parts, _ = lax.optimization_barrier((parts, sent[step - 2][1][-1 if step == 2 else 1]))
        if direct:
            sent.append((parts, send_direct(parts)))
        else:
            sent.append((parts, send_sums(parts, riding if step == RIDE else [])))
    done = []
    everyone = None
    for step, (_, _, _, direct) in enumerate(PLAN):
        parts, arrived = sent[step]
        if direct:
            merged = sum_direct(parts, arrived)
        else:
            merged, shared = finish_sums(parts, arrived, is_end, riding if step == RIDE else [])
            if shared is not None:
                everyone = jnp.stack(shared).reshape((4,) + small_shape)
        done.append(finish(step, merged))
    squares, kv = [
        jnp.concatenate([done[0][i], done[1][i]], axis=0) + done[2][i] + done[3][i] for i in range(2)
    ]
    return kv, squares, everyone


def scatter_heads(kv, squares):
    tp_count = lax.axis_size("tp")
    place = lax.axis_index("tp")
    width = kv.shape[1] // tp_count
    blocks = None
    for bit in bits_of(tp_count):
        mine = (place // bit) % 2

        def half(which):
            if blocks is not None:
                paired = blocks.reshape((-1, 2) + blocks.shape[1:])
                return lax.dynamic_index_in_dim(paired, which, 1, keepdims=False)
            columns = [
                lax.dynamic_slice_in_dim(kv, (2 * i + which) * width, width, axis=1)
                for i in range(tp_count // 2)
            ]
            return jnp.stack(columns)

        arrived = flip(half(1 - mine).astype(jnp.bfloat16), "tp", bit)
        blocks = half(mine) + arrived.astype(jnp.float32)
        squares = squares + flip(squares, "tp", bit)
    return blocks[0], squares


SMALL_ROWS = 48


def pack_small(prefix_cache, sources, tiles):
    width = prefix_cache.shape[2]
    asks = jnp.stack([sources, tiles]).astype(jnp.bfloat16)
    rows = SMALL_ROWS - prefix_cache.shape[1]
    asks = jnp.pad(asks, ((0, rows - 2), (0, width - asks.shape[1])))
    return jnp.concatenate([prefix_cache[0], asks], axis=0)


def attend_kernel(
    place_ref, query_ref, prefix_ref, text_ref, pages_ref, pick_ref, seen_ref, all_ref, out_ref, vision_ref
):
    pages = pages_ref[...]
    count = pages.shape[0]

    def pick(index):
        one_hot = lax.broadcasted_iota(jnp.int32, (index.shape[0], count), 1) == index
        one_hot = jnp.where(one_hot, 1.0, 0.0).astype(jnp.bfloat16)
        return jnp.dot(one_hot, pages, preferred_element_type=jnp.float32).astype(jnp.bfloat16)

    @pl.when(pl.program_id(0) == 0)
    def _():
        vision_ref[...] = pick(all_ref[...])

    window = pick(pick_ref[0])
    keys_values = jnp.concatenate([prefix_ref[0], window, text_ref[0]], axis=0)
    text_rows = text_ref.shape[1]
    heads = keys_values.shape[1] // (2 * HD)
    query = query_ref[0]
    for head in range(heads):
        keys = keys_values[:, 2 * head * HD : (2 * head + 1) * HD]
        values = keys_values[:, (2 * head + 1) * HD : (2 * head + 2) * HD]
        stacked = jnp.concatenate(
            [
                query[:, (head * GROUP + a) * HD : (head * GROUP + a + 1) * HD]
                for a in range(GROUP)
            ],
            axis=0,
        )
        scores = lax.dot_general(
            stacked, keys, (((1,), (1,)), ((), ())), preferred_element_type=jnp.float32
        ) * (HD**-0.5)
        row = lax.broadcasted_iota(jnp.int32, scores.shape, 0) % text_rows
        column = lax.broadcasted_iota(jnp.int32, scores.shape, 1)
        text_column = column - (scores.shape[1] - text_rows)
        allowed = (text_column <= row) & (seen_ref[0] > 0)
        scores = jnp.where(allowed, scores, -1e30)
        best = jnp.max(scores, axis=1, keepdims=True)
        weights = jnp.exp(scores - best)
        total = jnp.sum(weights, axis=1, keepdims=True)
        result = jnp.dot(weights.astype(jnp.bfloat16), values, preferred_element_type=jnp.float32)
        result = (result / total).astype(jnp.bfloat16)
        for a in range(GROUP):
            out_ref[0, :, (head * GROUP + a) * HD : (head * GROUP + a + 1) * HD] = result[
                a * text_rows : (a + 1) * text_rows
            ]


def attend(place, queries, prefixes, text_kv, pages, picks, seen, all_rows):
    docs, rows, width = queries.shape
    kv_width = text_kv.shape[2]
    vision_rows = all_rows.shape[0]
    keys = seen.shape[2]
    return pl.pallas_call(
        attend_kernel,
        grid_spec=pltpu.PrefetchScalarGridSpec(
            num_scalar_prefetch=1,
            grid=(docs,),
            in_specs=[
                pl.BlockSpec((1, rows, width), lambda d, place: (d, 0, 0)),
                pl.BlockSpec((1,) + prefixes.shape[1:], lambda d, place: (place[d], 0, 0)),
                pl.BlockSpec((1, rows, kv_width), lambda d, place: (d, 0, 0)),
                pl.BlockSpec(pages.shape, lambda d, place: (0, 0)),
                pl.BlockSpec((1,) + picks.shape[1:], lambda d, place: (d, 0, 0)),
                pl.BlockSpec((1, 1, keys), lambda d, place: (d, 0, 0)),
                pl.BlockSpec(all_rows.shape, lambda d, place: (0, 0)),
            ],
            out_specs=[
                pl.BlockSpec((1, rows, width), lambda d, place: (d, 0, 0)),
                pl.BlockSpec((vision_rows, kv_width), lambda d, place: (0, 0)),
            ],
        ),
        out_shape=[
            jax.ShapeDtypeStruct(queries.shape, jnp.bfloat16),
            jax.ShapeDtypeStruct((vision_rows, kv_width), jnp.bfloat16),
        ],
        compiler_params=pltpu.CompilerParams(vmem_limit_bytes=VMEM),
        cost_estimate=pl.CostEstimate(
            flops=4 * docs * rows * width * keys,
            bytes_accessed=8 * docs * rows * width,
            transcendentals=docs * rows * keys * width // HD,
        ),
    )(place, queries, prefixes, text_kv, pages, picks, seen, all_rows)


def shards(
    panels,
    w_merge,
    ln_gain,
    w_kv,
    page_src,
    page_tile,
    doc_pages,
    prefix_id,
    prefix_cache,
    queries,
    text_kv,
):
    seq_count = lax.axis_size("seq")
    holder = lax.axis_index("seq")
    tile_count, panel_rows, _ = panels.shape
    page_count = page_src.shape[0]
    capacity = max(2, 2 * page_count // seq_count)
    sources = page_src[:, 0]

    kv, squares, small = merge_tiles(
        panels, w_merge, ln_gain, w_kv, pack_small(prefix_cache, sources, page_tile)
    )
    width = seq_count // lax.axis_size("tp")
    small = small.reshape(seq_count, SMALL_ROWS, -1)

    def place_of(index):
        group = (index // width) ^ (holder // width)
        return group * width + (index - holder) % width

    prefix_rows = prefix_cache.shape[1]
    prefixes = small[:, :prefix_rows]
    place = place_of(jnp.arange(seq_count, dtype=jnp.int32))
    asked_sources = small[:, prefix_rows, :page_count].astype(jnp.int32)[place]
    asked_tiles = small[:, prefix_rows + 1, :page_count].astype(jnp.int32)[place]
    asked = (asked_sources == holder).astype(jnp.int32)
    order = jnp.cumsum(asked, axis=1) - 1
    slots = jnp.arange(capacity, dtype=jnp.int32)
    picked = asked[:, None, :] * (order[:, None, :] == slots[None, :, None]).astype(jnp.int32)
    wanted = jnp.sum(picked * asked_tiles[:, None, :], axis=2)
    within = jnp.arange(panel_rows, dtype=jnp.int32)
    wanted_rows = (wanted.reshape(-1, 1) * panel_rows + within[None, :]).reshape(-1)
    chooser = wanted_rows[:, None] == jnp.arange(tile_count * panel_rows, dtype=jnp.int32)[None, :]
    chooser = chooser.astype(jnp.bfloat16)

    position = jnp.arange(page_count, dtype=jnp.int32)
    earlier = (sources[:, None] == sources[None, :]) & (position[None, :] < position[:, None])
    rank = jnp.sum(earlier.astype(jnp.int32), axis=1)
    arrival = sources * capacity + rank
    all_rows = (arrival[:, None] * panel_rows + within[None, :]).reshape(-1, 1)
    lengths = doc_pages[0]
    starts = jnp.cumsum(lengths) - lengths
    step = jnp.arange(MOST_PAGES, dtype=jnp.int32)
    inside = step[None, :] < lengths[:, None]
    page = jnp.minimum(starts[:, None] + step[None, :], page_count - 1)
    doc_rows = arrival[page][:, :, None] * panel_rows + within[None, None, :]
    doc_rows = jnp.where(inside[:, :, None], doc_rows, -1)
    doc_count, query_rows, _ = queries.shape
    picks = doc_rows.reshape(doc_count, -1, 1)
    seen = jnp.concatenate(
        [
            jnp.ones((doc_count, prefixes.shape[1]), jnp.int32),
            (doc_rows >= 0).reshape(doc_count, -1).astype(jnp.int32),
            jnp.ones((doc_count, query_rows), jnp.int32),
        ],
        axis=1,
    )[:, None, :]

    kv, squares = scatter_heads(kv, squares)
    row_scale = lax.rsqrt(squares / D + 1e-06)
    tile_kv = (kv * row_scale[:, None]).astype(jnp.bfloat16)
    outgoing = jnp.dot(chooser, tile_kv, preferred_element_type=jnp.float32).astype(jnp.bfloat16)
    pages = lax.all_to_all(outgoing, "seq", split_axis=0, concat_axis=0, tiled=True)
    attended, vision_kv = attend(
        place_of(prefix_id), queries, prefixes, text_kv, pages, picks, seen, all_rows
    )
    return (attended, vision_kv)


def solution(mesh):
    return jax.shard_map(
        shards,
        mesh=mesh,
        in_specs=(
            P("seq", None, "tp"),
            P("seq", "tp"),
            P("tp"),
            P("tp", None),
            P("seq", None),
            P("seq"),
            P("seq", None),
            P("seq"),
            P("seq", None, "tp"),
            P("seq", None, "tp"),
            P("seq", None, "tp"),
        ),
        out_specs=(P("seq", None, "tp"), P("seq", "tp")),
        check_vma=False,
    )
```

```python
import functools

import jax
import jax.numpy as jnp
from jax import lax
from jax.experimental import pallas as pl
from jax.experimental.pallas import tpu as pltpu
from jax.sharding import PartitionSpec as P

D = 8192
HD = 128
GROUP = 8
MOST_PAGES = 16
VMEM = 16 * 1024 * 1024


def bits_of(count):
    return [1 << bit for bit in range(count.bit_length() - 1)]


def flip(value, axis, bit):
    count = lax.axis_size(axis)
    return lax.ppermute(value, axis, [(i, i ^ bit) for i in range(count)])


def transpose_panels(local, swap):
    seq_count, tp_count = lax.axis_size("seq"), lax.axis_size("tp")
    width = seq_count // tp_count
    half = tp_count // 2
    pairs = []
    for origin in range(tp_count):
        for inner in range(width):
            for block in range(tp_count):
                source = (origin * width + inner) * tp_count + (block ^ swap)
                slot = ((origin ^ block) & 1) * half + origin // 2
                pairs.append((source, (block * width + inner) * tp_count + slot))
    return lax.ppermute(local, ("seq", "tp"), pairs)


def share_panels(moved):
    held = [moved]
    bits = bits_of(lax.axis_size("tp"))
    for bit in bits[-1:] + bits[:-1]:
        held = held + [flip(piece, "tp", bit) for piece in held]
    return held


def panel_base():
    group = lax.axis_index("seq") // (lax.axis_size("seq") // lax.axis_size("tp"))
    place = lax.axis_index("tp")
    half = lax.axis_size("tp") // 2
    return 2 * (place % half) + ((place // half) ^ (group & 1))


def order_kernel(share, scalars_ref, *refs):
    out_ref = refs[-1]
    rows, depth = refs[0].shape
    members = depth // share
    for place in range(4):
        at = pl.ds(pl.multiple_of(scalars_ref[place] * rows, rows), rows)
        for member in range(members):
            if members == 1:
                out_ref[at, :] = refs[place][...]
            else:
                source = lax.rem(scalars_ref[4] + member, members)
                columns = pl.ds(pl.multiple_of(source * share, share), share)
                out_ref[at, member * share : (member + 1) * share] = refs[place][:, columns]


def order_rows(scalars, held, share):
    rows, depth = held[0].shape
    return pl.pallas_call(
        functools.partial(order_kernel, share),
        grid_spec=pltpu.PrefetchScalarGridSpec(
            num_scalar_prefetch=1,
            grid=(1,),
            in_specs=[pl.BlockSpec((rows, depth), lambda i, scalars: (0, 0))] * 4,
            out_specs=pl.BlockSpec((4 * rows, depth), lambda i, scalars: (0, 0)),
        ),
        out_shape=jax.ShapeDtypeStruct((4 * rows, depth), jnp.bfloat16),
        compiler_params=pltpu.CompilerParams(vmem_limit_bytes=VMEM),
        cost_estimate=pl.CostEstimate(flops=0, bytes_accessed=2 * depth, transcendentals=0),
    )(scalars, *held)


def partial_kernel(halves, *refs):
    rows_refs, weights_refs, out_refs = refs[:halves], refs[halves:-4], refs[-4:]
    weights = jnp.concatenate([ref[...] for ref in weights_refs], axis=0)
    for half, rows_ref in enumerate(rows_refs):
        total = jnp.dot(rows_ref[...], weights, preferred_element_type=jnp.float32)
        total = total.astype(jnp.bfloat16)
        rows = total.shape[0] // 4
        for k, out_ref in enumerate(out_refs):
            out_ref[half * rows : (half + 1) * rows] = total[k * rows : (k + 1) * rows]


def partial_products(held, weights, count):
    halves = len(held)
    rows, depth = held[0].shape
    tile = min(count, 512)

    def block(used, first):
        return pl.BlockSpec((used, tile), lambda i: (0, i + first // tile))

    out = halves * rows // 4
    return pl.pallas_call(
        functools.partial(partial_kernel, halves),
        grid=(count // tile,),
        in_specs=[pl.BlockSpec((rows, depth), lambda i: (0, 0))] * halves
        + [block(used, first) for _, used, first in weights],
        out_specs=[pl.BlockSpec((out, tile), lambda i: (0, i))] * 4,
        out_shape=[jax.ShapeDtypeStruct((out, count), jnp.bfloat16)] * 4,
        compiler_params=pltpu.CompilerParams(vmem_limit_bytes=VMEM),
        cost_estimate=pl.CostEstimate(flops=0, bytes_accessed=2 * count, transcendentals=0),
    )(*held, *[array for array, _, _ in weights])


def along(pairs):
    width = lax.axis_size("seq") // lax.axis_size("tp")
    return [(a * width + i, b * width + i) for a, b in pairs for i in range(width)]


def ride(value, extra):
    return jnp.concatenate([value] + extra, axis=0) if extra else value


def send_direct(parts, small, kinds=(1, 2, 3)):
    return [
        lax.ppermute(ride(parts[k], small), "seq", along([(a, a ^ k) for a in range(4)]))
        for k in kinds
    ]


def sum_direct(parts, arrived):
    rows = parts[0].shape[0]
    total = parts[0].astype(jnp.float32)
    for other in arrived:
        total = total + other[:rows]
    return total.astype(jnp.bfloat16)


PLAN = (((0,), 0, 4), ((1,), 0, 4), ((0, 1), 4, 2), ((0, 1), 6, 2))
RIDE = 2


def merge_tiles(panels, w_merge, ln_gain, w_kv, small):
    seq_count, tp_count = lax.axis_size("seq"), lax.axis_size("tp")
    assert tp_count == 4 and seq_count % 4 == 0
    width = seq_count // tp_count
    tiles, panel_rows, depth = panels.shape
    share = w_merge.shape[0]
    group = lax.axis_index("seq") // width
    member = lax.axis_index("seq") % width
    local = panels.reshape(tiles * panel_rows, depth)
    half = local.shape[0] // 2
    swapped = flip(local[half:], "tp", 2)
    moved = [transpose_panels(local[:half], 0), transpose_panels(swapped, 2)]
    columns = w_merge.shape[1] // 2
    small = small.reshape(-1, columns)
    extra = small.shape[0]
    received = []
    for side in range(2):
        if side == 0:
            own = w_merge[:, :columns]
        else:
            source, _ = lax.optimization_barrier((w_merge, swapped))
            own = jnp.concatenate([source[:, columns:], small], axis=0)
        others = []
        for offset in range(1, width):
            pairs = [
                (g * width + (i + offset) % width, g * width + i)
                for g in range(tp_count)
                for i in range(width)
            ]
            others.append(lax.ppermute(own, "seq", pairs))
        received.append(others)
    aligned = width == 2 and share % 128 == 0
    if not aligned:
        share = depth
    places = panel_base() ^ jnp.arange(4, dtype=jnp.int32) ^ group
    scalars = jnp.concatenate([places, jnp.full((4,), member, jnp.int32)])
    early, _ = lax.optimization_barrier((moved[0], swapped))
    held = [order_rows(scalars, share_panels(early), share)]
    eighth = w_merge.shape[1] // 8
    sent = []

    def finish(step):
        _, first, count = PLAN[step]
        merged = sum_direct(*sent[step]).astype(jnp.float32)
        at = slice(first * eighth, (first + count) * eighth)
        gained = (merged * ln_gain[at].astype(jnp.float32)[None, :]).astype(jnp.bfloat16)
        squared = jnp.sum(merged * merged, axis=1)
        return squared, jnp.dot(gained, w_kv[at], preferred_element_type=jnp.float32)

    riding = []
    for step, (halves, first, count) in enumerate(PLAN):
        first, count = first * eighth, count * eighth
        if step == 1:
            late, _ = lax.optimization_barrier((moved[1], sent[0][0][0]))
            held.append(order_rows(scalars, share_panels(late), share))
        if step == RIDE:
            received[1], _ = lax.optimization_barrier((received[1], sent[step - 1][0][0]))
            small = [small] + [other[-extra:] for other in received[1]]
            small_shape = (width,) + small[0].shape
            riding = [jnp.stack(small).reshape(-1, count)]
        side = first // columns
        inside = first - side * columns
        if aligned:
            operands = [(w_merge, share, first), (received[side][0], share, inside)]
        else:
            parts = [w_merge[:, side * columns : (side + 1) * columns]]
            parts += [other[: w_merge.shape[0]] for other in received[side]]
            parts = jnp.concatenate(parts, axis=0)
            operands = [(jnp.roll(parts, member * w_merge.shape[0], axis=0), depth, inside)]
        parts = partial_products([held[h] for h in halves], operands, count)
        if step == 0:
            sent.append((parts, send_direct(parts, [], (2, 3))))
        elif step == 1:
            parts, _ = lax.optimization_barrier((parts, sent[0][1]))
            joined = jnp.concatenate([sent[0][0][1], parts[1]], axis=0)
            far = send_direct(parts, [], (2, 3))
            near = send_direct([None, joined], [], (1,))[0]
            sent[0][1].append(near[:half])
            sent.append((parts, far + [near[half:]]))
        elif step == 2:
            parts, _ = lax.optimization_barrier((parts, sent[1][1][0]))
            sent.append((parts, send_direct(parts, riding)))
        else:
            parts, _ = lax.optimization_barrier((parts, (sent[1][1][1], sent[2][1][0])))
            sent.append((parts, send_direct(parts, [])))
    done = [finish(step) for step in range(len(PLAN) - 1)]

    def complete(after):
        parts, arrived = sent[-1]
        arrived, after = lax.optimization_barrier((arrived, after))
        sent[-1] = (parts, arrived)
        done.append(finish(len(PLAN) - 1))
        squares, kv = [
            jnp.concatenate([done[0][i], done[1][i]], axis=0) + done[2][i] + done[3][i]
            for i in range(2)
        ]
        return kv, squares, after

    rows = sent[RIDE][0][0].shape[0]
    everyone = riding + [other[rows:] for other in sent[RIDE][1]]
    everyone = jnp.stack(everyone).reshape((4,) + small_shape)
    return complete, everyone


def scatter_heads(kv, squares):
    tp_count = lax.axis_size("tp")
    place = lax.axis_index("tp")
    width = kv.shape[1] // tp_count
    blocks = None
    for bit in bits_of(tp_count):
        mine = (place // bit) % 2

        def half(which):
            if blocks is not None:
                paired = blocks.reshape((-1, 2) + blocks.shape[1:])
                return lax.dynamic_index_in_dim(paired, which, 1, keepdims=False)
            columns = [
                lax.dynamic_slice_in_dim(kv, (2 * i + which) * width, width, axis=1)
                for i in range(tp_count // 2)
            ]
            return jnp.stack(columns)

        arrived = flip(half(1 - mine).astype(jnp.bfloat16), "tp", bit)
        blocks = half(mine) + arrived.astype(jnp.float32)
        squares = squares + flip(squares, "tp", bit)
    return blocks[0], squares


SMALL_ROWS = 48


def pack_small(prefix_cache, sources, tiles):
    width = prefix_cache.shape[2]
    asks = jnp.stack([sources, tiles]).astype(jnp.bfloat16)
    rows = SMALL_ROWS - prefix_cache.shape[1]
    asks = jnp.pad(asks, ((0, rows - 2), (0, width - asks.shape[1])))
    return jnp.concatenate([prefix_cache[0], asks], axis=0)


def stack_heads(query, head):
    return jnp.concatenate(
        [query[:, (head * GROUP + a) * HD : (head * GROUP + a + 1) * HD] for a in range(GROUP)], axis=0
    )


def score(stacked, keys):
    return lax.dot_general(
        stacked, keys, (((1,), (1,)), ((), ())), preferred_element_type=jnp.float32
    ) * (HD**-0.5)


def weigh(scores, values):
    best = jnp.max(scores, axis=1, keepdims=True)
    weights = jnp.exp(scores - best)
    total = jnp.sum(weights, axis=1, keepdims=True)
    return (
        best,
        total,
        jnp.dot(weights.astype(jnp.bfloat16), values, preferred_element_type=jnp.float32),
    )


def text_kernel(place_ref, query_ref, prefix_ref, text_ref, result_ref, state_ref):
    text = text_ref[0]
    text_rows = text.shape[0]
    keys_values = jnp.concatenate([prefix_ref[0], text], axis=0)
    first = prefix_ref.shape[1]
    for head in range(keys_values.shape[1] // (2 * HD)):
        at = 2 * head * HD
        scores = score(stack_heads(query_ref[0], head), keys_values[:, at : at + HD])
        row = lax.broadcasted_iota(jnp.int32, scores.shape, 0) % text_rows
        column = lax.broadcasted_iota(jnp.int32, scores.shape, 1) - first
        scores = jnp.where(column <= row, scores, -1e30)
        best, total, result = weigh(scores, keys_values[:, at + HD : at + 2 * HD])
        result_ref[0, head] = result
        lane = lax.broadcasted_iota(jnp.int32, result.shape, 1)
        state_ref[0, head] = jnp.where(lane < HD // 2, best, total)


def attend_text(place, queries, prefixes, text_kv):
    docs, rows, width = queries.shape
    kv_width = text_kv.shape[2]
    shape = (docs, kv_width // (2 * HD), GROUP * rows, HD)
    out = pl.BlockSpec((1,) + shape[1:], lambda d, place: (d, 0, 0, 0))
    return pl.pallas_call(
        text_kernel,
        grid_spec=pltpu.PrefetchScalarGridSpec(
            num_scalar_prefetch=1,
            grid=(docs,),
            in_specs=[
                pl.BlockSpec((1, rows, width), lambda d, place: (d, 0, 0)),
                pl.BlockSpec((1,) + prefixes.shape[1:], lambda d, place: (place[d], 0, 0)),
                pl.BlockSpec((1, rows, kv_width), lambda d, place: (d, 0, 0)),
            ],
            out_specs=[out, out],
        ),
        out_shape=[jax.ShapeDtypeStruct(shape, jnp.float32)] * 2,
        compiler_params=pltpu.CompilerParams(vmem_limit_bytes=VMEM),
        cost_estimate=pl.CostEstimate(flops=0, bytes_accessed=width, transcendentals=0),
    )(place, queries, prefixes, text_kv)


def vision_kernel(
    query_ref, pages_ref, pick_ref, seen_ref, all_ref, result_ref, state_ref, out_ref, vision_ref
):
    pages = pages_ref[...]
    count = pages.shape[0]

    def pick(index):
        one_hot = lax.broadcasted_iota(jnp.int32, (index.shape[0], count), 1) == index
        one_hot = jnp.where(one_hot, 1.0, 0.0).astype(jnp.bfloat16)
        return jnp.dot(one_hot, pages, preferred_element_type=jnp.float32).astype(jnp.bfloat16)

    @pl.when(pl.program_id(0) == 0)
    def _():
        vision_ref[...] = pick(all_ref[...])

    window = pick(pick_ref[0])
    rows = out_ref.shape[1]
    for head in range(window.shape[1] // (2 * HD)):
        at = 2 * head * HD
        scores = score(stack_heads(query_ref[0], head), window[:, at : at + HD])
        scores = jnp.where(seen_ref[0] > 0, scores, -1e30)
        best, total, result = weigh(scores, window[:, at + HD : at + 2 * HD])
        state = state_ref[0, head]
        other_best, other_total = state[:, :1], state[:, HD // 2 : HD // 2 + 1]
        top = jnp.maximum(best, other_best)
        mine, other = jnp.exp(best - top), jnp.exp(other_best - top)
        scale = 1.0 / (total * mine + other_total * other)
        result = result * (mine * scale) + result_ref[0, head] * (other * scale)
        result = result.astype(jnp.bfloat16)
        for a in range(GROUP):
            out_ref[0, :, (head * GROUP + a) * HD : (head * GROUP + a + 1) * HD] = result[
                a * rows : (a + 1) * rows
            ]


def attend_vision(queries, pages, picks, seen, all_rows, result, state):
    docs, rows, width = queries.shape
    vision_rows = all_rows.shape[0]
    partial = pl.BlockSpec((1,) + result.shape[1:], lambda d: (d, 0, 0, 0))
    return pl.pallas_call(
        vision_kernel,
        grid=(docs,),
        in_specs=[
            pl.BlockSpec((1, rows, width), lambda d: (d, 0, 0)),
            pl.BlockSpec(pages.shape, lambda d: (0, 0)),
            pl.BlockSpec((1,) + picks.shape[1:], lambda d: (d, 0, 0)),
            pl.BlockSpec((1,) + seen.shape[1:], lambda d: (d, 0, 0)),
            pl.BlockSpec(all_rows.shape, lambda d: (0, 0)),
            partial,
            partial,
        ],
        out_specs=[
            pl.BlockSpec((1, rows, width), lambda d: (d, 0, 0)),
            pl.BlockSpec((vision_rows, pages.shape[1]), lambda d: (0, 0)),
        ],
        out_shape=[
            jax.ShapeDtypeStruct(queries.shape, jnp.bfloat16),
            jax.ShapeDtypeStruct((vision_rows, pages.shape[1]), jnp.bfloat16),
        ],
        compiler_params=pltpu.CompilerParams(vmem_limit_bytes=VMEM),
        cost_estimate=pl.CostEstimate(flops=0, bytes_accessed=width, transcendentals=0),
    )(queries, pages, picks, seen, all_rows, result, state)


def shards(
    panels,
    w_merge,
    ln_gain,
    w_kv,
    page_src,
    page_tile,
    doc_pages,
    prefix_id,
    prefix_cache,
    queries,
    text_kv,
):
    seq_count = lax.axis_size("seq")
    holder = lax.axis_index("seq")
    tile_count, panel_rows, _ = panels.shape
    page_count = page_src.shape[0]
    capacity = max(2, 2 * page_count // seq_count)
    sources = page_src[:, 0]

    complete, small = merge_tiles(
        panels, w_merge, ln_gain, w_kv, pack_small(prefix_cache, sources, page_tile)
    )
    width = seq_count // lax.axis_size("tp")
    small = small.reshape(seq_count, SMALL_ROWS, -1)

    def place_of(index):
        group = (index // width) ^ (holder // width)
        return group * width + (index - holder) % width

    prefix_rows = prefix_cache.shape[1]
    prefixes = small[:, :prefix_rows]
    place = place_of(jnp.arange(seq_count, dtype=jnp.int32))
    asked_sources = small[:, prefix_rows, :page_count].astype(jnp.int32)[place]
    asked_tiles = small[:, prefix_rows + 1, :page_count].astype(jnp.int32)[place]
    asked = (asked_sources == holder).astype(jnp.int32)
    order = jnp.cumsum(asked, axis=1) - 1
    slots = jnp.arange(capacity, dtype=jnp.int32)
    picked = asked[:, None, :] * (order[:, None, :] == slots[None, :, None]).astype(jnp.int32)
    wanted = jnp.sum(picked * asked_tiles[:, None, :], axis=2)
    within = jnp.arange(panel_rows, dtype=jnp.int32)
    wanted_rows = (wanted.reshape(-1, 1) * panel_rows + within[None, :]).reshape(-1)
    chooser = wanted_rows[:, None] == jnp.arange(tile_count * panel_rows, dtype=jnp.int32)[None, :]
    chooser = chooser.astype(jnp.bfloat16)

    position = jnp.arange(page_count, dtype=jnp.int32)
    earlier = (sources[:, None] == sources[None, :]) & (position[None, :] < position[:, None])
    rank = jnp.sum(earlier.astype(jnp.int32), axis=1)
    arrival = sources * capacity + rank
    all_rows = (arrival[:, None] * panel_rows + within[None, :]).reshape(-1, 1)
    lengths = doc_pages[0]
    starts = jnp.cumsum(lengths) - lengths
    step = jnp.arange(MOST_PAGES, dtype=jnp.int32)
    inside = step[None, :] < lengths[:, None]
    page = jnp.minimum(starts[:, None] + step[None, :], page_count - 1)
    doc_rows = arrival[page][:, :, None] * panel_rows + within[None, None, :]
    doc_rows = jnp.where(inside[:, :, None], doc_rows, -1)
    doc_count = queries.shape[0]
    picks = doc_rows.reshape(doc_count, -1, 1)
    seen = (doc_rows >= 0).reshape(doc_count, 1, -1).astype(jnp.int32)
    early = attend_text(place_of(prefix_id), queries, prefixes, text_kv)
    kv, squares, (early, chooser) = complete((early, chooser))
    kv, squares = scatter_heads(kv, squares)
    row_scale = lax.rsqrt(squares / D + 1e-06)
    tile_kv = (kv * row_scale[:, None]).astype(jnp.bfloat16)
    outgoing = jnp.dot(chooser, tile_kv, preferred_element_type=jnp.float32).astype(jnp.bfloat16)
    pages = lax.all_to_all(outgoing, "seq", split_axis=0, concat_axis=0, tiled=True)
    attended, vision_kv = attend_vision(queries, pages, picks, seen, all_rows, *early)
    return (attended, vision_kv)


def solution(mesh):
    return jax.shard_map(
        shards,
        mesh=mesh,
        in_specs=(
            P("seq", None, "tp"),
            P("seq", "tp"),
            P("tp"),
            P("tp", None),
            P("seq", None),
            P("seq"),
            P("seq", None),
            P("seq"),
            P("seq", None, "tp"),
            P("seq", None, "tp"),
            P("seq", None, "tp"),
        ),
        out_specs=(P("seq", None, "tp"), P("seq", "tp")),
        check_vma=False,
    )
```

```python
import functools

import jax
import jax.numpy as jnp
from jax import lax
from jax.experimental import pallas as pl
from jax.experimental.pallas import tpu as pltpu
from jax.sharding import PartitionSpec as P

D = 8192
HD = 128
GROUP = 8
MOST_PAGES = 16
VMEM = 16 * 1024 * 1024


def bits_of(count):
    return [1 << bit for bit in range(count.bit_length() - 1)]


def flip(value, axis, bit):
    count = lax.axis_size(axis)
    return lax.ppermute(value, axis, [(i, i ^ bit) for i in range(count)])


def transpose_panels(local, swap):
    seq_count, tp_count = lax.axis_size("seq"), lax.axis_size("tp")
    width = seq_count // tp_count
    half = tp_count // 2
    pairs = []
    for origin in range(tp_count):
        for inner in range(width):
            for block in range(tp_count):
                source = (origin * width + inner) * tp_count + (block ^ swap)
                slot = ((origin ^ block) & 1) * half + origin // 2
                pairs.append((source, (block * width + inner) * tp_count + slot))
    return lax.ppermute(local, ("seq", "tp"), pairs)


def share_panels(moved):
    held = [moved]
    bits = bits_of(lax.axis_size("tp"))
    for bit in bits[-1:] + bits[:-1]:
        held = held + [flip(piece, "tp", bit) for piece in held]
    return held


def panel_base():
    group = lax.axis_index("seq") // (lax.axis_size("seq") // lax.axis_size("tp"))
    place = lax.axis_index("tp")
    half = lax.axis_size("tp") // 2
    return 2 * (place % half) + ((place // half) ^ (group & 1))


def order_kernel(share, scalars_ref, *refs):
    out_ref = refs[-1]
    rows, depth = refs[0].shape
    members = depth // share
    for place in range(4):
        at = pl.ds(pl.multiple_of(scalars_ref[place] * rows, rows), rows)
        for member in range(members):
            if members == 1:
                out_ref[at, :] = refs[place][...]
            else:
                source = lax.rem(scalars_ref[4] + member, members)
                columns = pl.ds(pl.multiple_of(source * share, share), share)
                out_ref[at, member * share : (member + 1) * share] = refs[place][:, columns]


def order_rows(scalars, held, share):
    rows, depth = held[0].shape
    return pl.pallas_call(
        functools.partial(order_kernel, share),
        grid_spec=pltpu.PrefetchScalarGridSpec(
            num_scalar_prefetch=1,
            grid=(1,),
            in_specs=[pl.BlockSpec((rows, depth), lambda i, scalars: (0, 0))] * 4,
            out_specs=pl.BlockSpec((4 * rows, depth), lambda i, scalars: (0, 0)),
        ),
        out_shape=jax.ShapeDtypeStruct((4 * rows, depth), jnp.bfloat16),
        compiler_params=pltpu.CompilerParams(vmem_limit_bytes=VMEM),
        cost_estimate=pl.CostEstimate(flops=0, bytes_accessed=2 * depth, transcendentals=0),
    )(scalars, *held)


def partial_kernel(halves, groups, *refs):
    inputs = len(refs) - len(groups)
    rows_refs, weights_refs, out_refs = refs[:halves], refs[halves:inputs], refs[inputs:]
    weights = jnp.concatenate([ref[...] for ref in weights_refs], axis=0)
    for half, rows_ref in enumerate(rows_refs):
        total = jnp.dot(rows_ref[...], weights, preferred_element_type=jnp.float32)
        total = total.astype(jnp.bfloat16)
        rows = total.shape[0] // 4
        for out_ref, members in zip(out_refs, groups):
            for i, k in enumerate(members):
                to = (i * halves + half) * rows
                out_ref[to : to + rows] = total[k * rows : (k + 1) * rows]


def partial_products(held, weights, count, groups):
    halves = len(held)
    rows, depth = held[0].shape
    tile = min(count, 512)

    def block(used, first):
        return pl.BlockSpec((used, tile), lambda i: (0, i + first // tile))

    outs = [len(members) * halves * rows // 4 for members in groups]
    return pl.pallas_call(
        functools.partial(partial_kernel, halves, groups),
        grid=(count // tile,),
        in_specs=[pl.BlockSpec((rows, depth), lambda i: (0, 0))] * halves
        + [block(used, first) for _, used, first in weights],
        out_specs=[pl.BlockSpec((out, tile), lambda i: (0, i)) for out in outs],
        out_shape=[jax.ShapeDtypeStruct((out, count), jnp.bfloat16) for out in outs],
        compiler_params=pltpu.CompilerParams(vmem_limit_bytes=VMEM),
        cost_estimate=pl.CostEstimate(flops=0, bytes_accessed=2 * count, transcendentals=0),
    )(*held, *[array for array, _, _ in weights])


def along(pairs):
    width = lax.axis_size("seq") // lax.axis_size("tp")
    return [(a * width + i, b * width + i) for a, b in pairs for i in range(width)]


INWARD = ((0, 1), (3, 2))
OUTWARD = ((1, 0), (2, 3))
ACROSS = ((1, 2), (2, 1))
BEYOND = ((1, 3), (2, 0))


def send_direct(parts, kinds):
    return [
        lax.ppermute(parts[k], "seq", along([(a, a ^ k) for a in range(4)])) for k in kinds
    ]


def sum_direct(parts, arrived):
    total = parts[0].astype(jnp.float32)
    for other in arrived:
        total = total + other
    return total.astype(jnp.bfloat16)


def ride(value, extra):
    return jnp.concatenate([value] + extra, axis=0) if extra else value


def send_sums(parts, small):
    _, others, first = parts
    inward = lax.ppermute(ride(others, small), "seq", along(INWARD))
    outward = lax.ppermute(ride(first, small), "seq", along(OUTWARD))
    return inward, outward


def finish_sums(parts, arrived, is_end, small):
    own, others, _ = parts
    inward, outward = arrived
    rows = own.shape[0]

    def add(mine, other):
        return (mine.astype(jnp.float32) + other.astype(jnp.float32)).astype(jnp.bfloat16)

    def part(value, first, index=0):
        count = small[0].shape[0]
        return value[first + index * count : first + (index + 1) * count]

    extra = [part(inward, 3 * rows)] + small if small else []
    beyond = add(others[rows : 2 * rows], inward[2 * rows : 3 * rows])
    beyond = lax.ppermute(ride(beyond, extra), "seq", along(BEYOND))
    across = add(others[2 * rows :], inward[rows : 2 * rows])
    across = lax.ppermute(ride(across, extra), "seq", along(ACROSS))
    mine = own.astype(jnp.float32)
    at_end = mine + outward[:rows] + beyond[:rows]
    at_middle = mine + inward[:rows] + across[:rows]
    shared = None
    if small:
        ends = [part(outward, rows), part(beyond, rows, 1), part(beyond, rows, 0)]
        middles = [part(inward, 3 * rows), part(across, rows, 0), part(across, rows, 1)]
        shared = small + [jnp.where(is_end, e, m) for e, m in zip(ends, middles)]
    return jnp.where(is_end, at_end, at_middle).astype(jnp.bfloat16), shared


PLAN = (((0,), 0, 4, True), ((1,), 0, 4, True), ((0, 1), 4, 2, False), ((0, 1), 6, 2, False))
RIDE = 2


def merge_tiles(panels, w_merge, ln_gain, w_kv, small):
    seq_count, tp_count = lax.axis_size("seq"), lax.axis_size("tp")
    assert tp_count == 4 and seq_count % 4 == 0
    width = seq_count // tp_count
    tiles, panel_rows, depth = panels.shape
    share = w_merge.shape[0]
    group = lax.axis_index("seq") // width
    member = lax.axis_index("seq") % width
    is_end = (group == 0) | (group == 3)
    local = panels.reshape(tiles * panel_rows, depth)
    half = local.shape[0] // 2
    swapped = flip(local[half:], "tp", 2)
    moved = [transpose_panels(local[:half], 0), transpose_panels(swapped, 2)]
    columns = w_merge.shape[1] // 2
    small = small.reshape(-1, columns)
    extra = small.shape[0]
    received = []
    for side in range(2):
        own = w_merge[:, side * columns : (side + 1) * columns]
        if side == 1:
            own = jnp.concatenate([own, small], axis=0)
            own, _ = lax.optimization_barrier((own, swapped))
        others = []
        for offset in range(1, width):
            pairs = [
                (g * width + (i + offset) % width, g * width + i)
                for g in range(tp_count)
                for i in range(width)
            ]
            others.append(lax.ppermute(own, "seq", pairs))
        received.append(others)
    aligned = width == 2 and share % 128 == 0
    if not aligned:
        share = depth
    places = panel_base() ^ jnp.arange(4, dtype=jnp.int32) ^ group
    scalars = jnp.concatenate([places, jnp.full((4,), member, jnp.int32)])
    early, _ = lax.optimization_barrier((moved[0], swapped))
    held = [order_rows(scalars, share_panels(early), share)]
    eighth = w_merge.shape[1] // 8
    sent = []

    def finish(step, merged):
        _, first, count, _ = PLAN[step]
        merged = merged.astype(jnp.float32)
        at = slice(first * eighth, (first + count) * eighth)
        gained = (merged * ln_gain[at].astype(jnp.float32)[None, :]).astype(jnp.bfloat16)
        squared = jnp.sum(merged * merged, axis=1)
        return squared, jnp.dot(gained, w_kv[at], preferred_element_type=jnp.float32)

    riding = []
    for step, (halves, first, count, direct) in enumerate(PLAN):
        first, count = first * eighth, count * eighth
        if step == 1:
            late, _ = lax.optimization_barrier((moved[1], sent[0][0][0]))
            held.append(order_rows(scalars, share_panels(late), share))
        if step == RIDE:
            received[1], _ = lax.optimization_barrier((received[1], sent[step - 1][0][0]))
            small = [small] + [other[-extra:] for other in received[1]]
            small_shape = (width,) + small[0].shape
            riding = [jnp.stack(small).reshape(-1, count)]
        side = first // columns
        inside = first - side * columns
        if aligned:
            operands = [(w_merge, share, first), (received[side][0], share, inside)]
        else:
            parts = [w_merge[:, side * columns : (side + 1) * columns]]
            parts += [other[: w_merge.shape[0]] for other in received[side]]
            parts = jnp.concatenate(parts, axis=0)
            operands = [(jnp.roll(parts, member * w_merge.shape[0], axis=0), depth, inside)]
        groups = ((0,), (1,), (2,), (3,)) if direct else ((0,), (1, 2, 3), (1,))
        parts = partial_products([held[h] for h in halves], operands, count, groups)
        if step == 0:
            sent.append((parts, send_direct(parts, (2, 3))))
        elif step == 1:
            parts, _ = lax.optimization_barrier((parts, sent[0][1][0]))
            joined = jnp.concatenate([sent[0][0][1], parts[1]], axis=0)
            far = send_direct(parts, (2, 3))
            near = send_direct([None, joined], (1,))[0]
            sent[0][1].append(near[:half])
            sent.append((parts, far + [near[half:]]))
        else:
            parts, _ = lax.optimization_barrier((parts, sent[0][1][1]))
            sent.append((parts, send_sums(parts, riding if step == RIDE else [])))
    done = []
    everyone = None
    for step, (_, _, _, direct) in enumerate(PLAN):
        parts, arrived = sent[step]
        if direct:
            merged = sum_direct(parts, arrived)
        else:
            merged, shared = finish_sums(parts, arrived, is_end, riding if step == RIDE else [])
            if shared is not None:
                everyone = jnp.stack(shared).reshape((4,) + small_shape)
        done.append(finish(step, merged))
    squares, kv = [
        jnp.concatenate([done[0][i], done[1][i]], axis=0) + done[2][i] + done[3][i] for i in range(2)
    ]
    return kv, squares, everyone


def scatter_heads(kv, squares):
    tp_count = lax.axis_size("tp")
    place = lax.axis_index("tp")
    width = kv.shape[1] // tp_count
    blocks = None
    for bit in bits_of(tp_count):
        mine = (place // bit) % 2

        def half(which):
            if blocks is not None:
                paired = blocks.reshape((-1, 2) + blocks.shape[1:])
                return lax.dynamic_index_in_dim(paired, which, 1, keepdims=False)
            columns = [
                lax.dynamic_slice_in_dim(kv, (2 * i + which) * width, width, axis=1)
                for i in range(tp_count // 2)
            ]
            return jnp.stack(columns)

        arrived = flip(half(1 - mine).astype(jnp.bfloat16), "tp", bit)
        blocks = half(mine) + arrived.astype(jnp.float32)
        squares = squares + flip(squares, "tp", bit)
    return blocks[0], squares


SMALL_ROWS = 48


def pack_small(prefix_cache, sources, tiles):
    width = prefix_cache.shape[2]
    asks = jnp.stack([sources, tiles]).astype(jnp.bfloat16)
    rows = SMALL_ROWS - prefix_cache.shape[1]
    asks = jnp.pad(asks, ((0, rows - 2), (0, width - asks.shape[1])))
    return jnp.concatenate([prefix_cache[0], asks], axis=0)


def attend_kernel(
    place_ref, query_ref, prefix_ref, text_ref, pages_ref, pick_ref, seen_ref, all_ref, out_ref, vision_ref
):
    pages = pages_ref[...]
    count = pages.shape[0]

    def pick(index):
        one_hot = lax.broadcasted_iota(jnp.int32, (index.shape[0], count), 1) == index
        one_hot = jnp.where(one_hot, 1.0, 0.0).astype(jnp.bfloat16)
        return jnp.dot(one_hot, pages, preferred_element_type=jnp.float32).astype(jnp.bfloat16)

    @pl.when(pl.program_id(0) == 0)
    def _():
        vision_ref[...] = pick(all_ref[...])

    window = pick(pick_ref[0])
    keys_values = jnp.concatenate([prefix_ref[0], window, text_ref[0]], axis=0)
    text_rows = text_ref.shape[1]
    heads = keys_values.shape[1] // (2 * HD)
    query = query_ref[0]
    for head in range(heads):
        keys = keys_values[:, 2 * head * HD : (2 * head + 1) * HD]
        values = keys_values[:, (2 * head + 1) * HD : (2 * head + 2) * HD]
        stacked = jnp.concatenate(
            [
                query[:, (head * GROUP + a) * HD : (head * GROUP + a + 1) * HD]
                for a in range(GROUP)
            ],
            axis=0,
        )
        scores = lax.dot_general(
            stacked, keys, (((1,), (1,)), ((), ())), preferred_element_type=jnp.float32
        ) * (HD**-0.5)
        row = lax.broadcasted_iota(jnp.int32, scores.shape, 0) % text_rows
        column = lax.broadcasted_iota(jnp.int32, scores.shape, 1)
        text_column = column - (scores.shape[1] - text_rows)
        allowed = (text_column <= row) & (seen_ref[0] > 0)
        scores = jnp.where(allowed, scores, -1e30)
        best = jnp.max(scores, axis=1, keepdims=True)
        weights = jnp.exp(scores - best)
        total = jnp.sum(weights, axis=1, keepdims=True)
        result = jnp.dot(weights.astype(jnp.bfloat16), values, preferred_element_type=jnp.float32)
        result = (result / total).astype(jnp.bfloat16)
        for a in range(GROUP):
            out_ref[0, :, (head * GROUP + a) * HD : (head * GROUP + a + 1) * HD] = result[
                a * text_rows : (a + 1) * text_rows
            ]


def attend(place, queries, prefixes, text_kv, pages, picks, seen, all_rows):
    docs, rows, width = queries.shape
    kv_width = text_kv.shape[2]
    vision_rows = all_rows.shape[0]
    keys = seen.shape[2]
    return pl.pallas_call(
        attend_kernel,
        grid_spec=pltpu.PrefetchScalarGridSpec(
            num_scalar_prefetch=1,
            grid=(docs,),
            in_specs=[
                pl.BlockSpec((1, rows, width), lambda d, place: (d, 0, 0)),
                pl.BlockSpec((1,) + prefixes.shape[1:], lambda d, place: (place[d], 0, 0)),
                pl.BlockSpec((1, rows, kv_width), lambda d, place: (d, 0, 0)),
                pl.BlockSpec(pages.shape, lambda d, place: (0, 0)),
                pl.BlockSpec((1,) + picks.shape[1:], lambda d, place: (d, 0, 0)),
                pl.BlockSpec((1, 1, keys), lambda d, place: (d, 0, 0)),
                pl.BlockSpec(all_rows.shape, lambda d, place: (0, 0)),
            ],
            out_specs=[
                pl.BlockSpec((1, rows, width), lambda d, place: (d, 0, 0)),
                pl.BlockSpec((vision_rows, kv_width), lambda d, place: (0, 0)),
            ],
        ),
        out_shape=[
            jax.ShapeDtypeStruct(queries.shape, jnp.bfloat16),
            jax.ShapeDtypeStruct((vision_rows, kv_width), jnp.bfloat16),
        ],
        compiler_params=pltpu.CompilerParams(vmem_limit_bytes=VMEM),
        cost_estimate=pl.CostEstimate(
            flops=4 * docs * rows * width * keys,
            bytes_accessed=8 * docs * rows * width,
            transcendentals=docs * rows * keys * width // HD,
        ),
    )(place, queries, prefixes, text_kv, pages, picks, seen, all_rows)


def shards(
    panels,
    w_merge,
    ln_gain,
    w_kv,
    page_src,
    page_tile,
    doc_pages,
    prefix_id,
    prefix_cache,
    queries,
    text_kv,
):
    seq_count = lax.axis_size("seq")
    holder = lax.axis_index("seq")
    tile_count, panel_rows, _ = panels.shape
    page_count = page_src.shape[0]
    capacity = max(2, 2 * page_count // seq_count)
    sources = page_src[:, 0]

    kv, squares, small = merge_tiles(
        panels, w_merge, ln_gain, w_kv, pack_small(prefix_cache, sources, page_tile)
    )
    width = seq_count // lax.axis_size("tp")
    small = small.reshape(seq_count, SMALL_ROWS, -1)

    def place_of(index):
        group = (index // width) ^ (holder // width)
        return group * width + (index - holder) % width

    prefix_rows = prefix_cache.shape[1]
    prefixes = small[:, :prefix_rows]
    place = place_of(jnp.arange(seq_count, dtype=jnp.int32))
    asked_sources = small[:, prefix_rows, :page_count].astype(jnp.int32)[place]
    asked_tiles = small[:, prefix_rows + 1, :page_count].astype(jnp.int32)[place]
    asked = (asked_sources == holder).astype(jnp.int32)
    order = jnp.cumsum(asked, axis=1) - 1
    slots = jnp.arange(capacity, dtype=jnp.int32)
    picked = asked[:, None, :] * (order[:, None, :] == slots[None, :, None]).astype(jnp.int32)
    wanted = jnp.sum(picked * asked_tiles[:, None, :], axis=2)
    within = jnp.arange(panel_rows, dtype=jnp.int32)
    wanted_rows = (wanted.reshape(-1, 1) * panel_rows + within[None, :]).reshape(-1)
    chooser = wanted_rows[:, None] == jnp.arange(tile_count * panel_rows, dtype=jnp.int32)[None, :]
    chooser = chooser.astype(jnp.bfloat16)

    position = jnp.arange(page_count, dtype=jnp.int32)
    earlier = (sources[:, None] == sources[None, :]) & (position[None, :] < position[:, None])
    rank = jnp.sum(earlier.astype(jnp.int32), axis=1)
    arrival = sources * capacity + rank
    all_rows = (arrival[:, None] * panel_rows + within[None, :]).reshape(-1, 1)
    lengths = doc_pages[0]
    starts = jnp.cumsum(lengths) - lengths
    step = jnp.arange(MOST_PAGES, dtype=jnp.int32)
    inside = step[None, :] < lengths[:, None]
    page = jnp.minimum(starts[:, None] + step[None, :], page_count - 1)
    doc_rows = arrival[page][:, :, None] * panel_rows + within[None, None, :]
    doc_rows = jnp.where(inside[:, :, None], doc_rows, -1)
    doc_count, query_rows, _ = queries.shape
    picks = doc_rows.reshape(doc_count, -1, 1)
    seen = jnp.concatenate(
        [
            jnp.ones((doc_count, prefixes.shape[1]), jnp.int32),
            (doc_rows >= 0).reshape(doc_count, -1).astype(jnp.int32),
            jnp.ones((doc_count, query_rows), jnp.int32),
        ],
        axis=1,
    )[:, None, :]

    kv, squares = scatter_heads(kv, squares)
    row_scale = lax.rsqrt(squares / D + 1e-06)
    tile_kv = (kv * row_scale[:, None]).astype(jnp.bfloat16)
    outgoing = jnp.dot(chooser, tile_kv, preferred_element_type=jnp.float32).astype(jnp.bfloat16)
    pages = lax.all_to_all(outgoing, "seq", split_axis=0, concat_axis=0, tiled=True)
    attended, vision_kv = attend(
        place_of(prefix_id), queries, prefixes, text_kv, pages, picks, seen, all_rows
    )
    return (attended, vision_kv)


def solution(mesh):
    return jax.shard_map(
        shards,
        mesh=mesh,
        in_specs=(
            P("seq", None, "tp"),
            P("seq", "tp"),
            P("tp"),
            P("tp", None),
            P("seq", None),
            P("seq"),
            P("seq", None),
            P("seq"),
            P("seq", None, "tp"),
            P("seq", None, "tp"),
            P("seq", None, "tp"),
        ),
        out_specs=(P("seq", None, "tp"), P("seq", "tp")),
        check_vma=False,
    )
```

```python
import functools

import jax
import jax.numpy as jnp
from jax import lax
from jax.experimental import pallas as pl
from jax.experimental.pallas import tpu as pltpu
from jax.sharding import PartitionSpec as P

D = 8192
HD = 128
GROUP = 8
MOST_PAGES = 16
VMEM = 16 * 1024 * 1024


def bits_of(count):
    return [1 << bit for bit in range(count.bit_length() - 1)]


def flip(value, axis, bit):
    count = lax.axis_size(axis)
    return lax.ppermute(value, axis, [(i, i ^ bit) for i in range(count)])


def transpose_panels(local, swap):
    seq_count, tp_count = lax.axis_size("seq"), lax.axis_size("tp")
    width = seq_count // tp_count
    half = tp_count // 2
    pairs = []
    for origin in range(tp_count):
        for inner in range(width):
            for block in range(tp_count):
                source = (origin * width + inner) * tp_count + (block ^ swap)
                slot = ((origin ^ block) & 1) * half + origin // 2
                pairs.append((source, (block * width + inner) * tp_count + slot))
    return lax.ppermute(local, ("seq", "tp"), pairs)


def share_panels(moved):
    held = [moved]
    bits = bits_of(lax.axis_size("tp"))
    for bit in bits[-1:] + bits[:-1]:
        held = held + [flip(piece, "tp", bit) for piece in held]
    return held


def panel_base():
    group = lax.axis_index("seq") // (lax.axis_size("seq") // lax.axis_size("tp"))
    place = lax.axis_index("tp")
    half = lax.axis_size("tp") // 2
    return 2 * (place % half) + ((place // half) ^ (group & 1))


def order_kernel(share, scalars_ref, *refs):
    out_ref = refs[-1]
    rows, depth = refs[0].shape
    members = depth // share
    for place in range(4):
        at = pl.ds(pl.multiple_of(scalars_ref[place] * rows, rows), rows)
        for member in range(members):
            if members == 1:
                out_ref[at, :] = refs[place][...]
            else:
                source = lax.rem(scalars_ref[4] + member, members)
                columns = pl.ds(pl.multiple_of(source * share, share), share)
                out_ref[at, member * share : (member + 1) * share] = refs[place][:, columns]


def order_rows(scalars, held, share):
    rows, depth = held[0].shape
    return pl.pallas_call(
        functools.partial(order_kernel, share),
        grid_spec=pltpu.PrefetchScalarGridSpec(
            num_scalar_prefetch=1,
            grid=(1,),
            in_specs=[pl.BlockSpec((rows, depth), lambda i, scalars: (0, 0))] * 4,
            out_specs=pl.BlockSpec((4 * rows, depth), lambda i, scalars: (0, 0)),
        ),
        out_shape=jax.ShapeDtypeStruct((4 * rows, depth), jnp.bfloat16),
        compiler_params=pltpu.CompilerParams(vmem_limit_bytes=VMEM),
        cost_estimate=pl.CostEstimate(flops=0, bytes_accessed=2 * depth, transcendentals=0),
    )(scalars, *held)


def partial_kernel(halves, riding, *refs):
    rows_refs, weights_refs, out_refs = refs[:halves], refs[halves : -4 - riding], refs[-4:]
    weights = jnp.concatenate([ref[...] for ref in weights_refs], axis=0)
    for half, rows_ref in enumerate(rows_refs):
        total = jnp.dot(rows_ref[...], weights, preferred_element_type=jnp.float32)
        total = total.astype(jnp.bfloat16)
        rows = total.shape[0] // 4
        for k, out_ref in enumerate(out_refs):
            out_ref[half * rows : (half + 1) * rows] = total[k * rows : (k + 1) * rows]
    if riding:
        for out_ref in out_refs[1:]:
            out_ref[halves * rows :] = refs[-5][...]


def partial_products(held, weights, count, riding):
    halves = len(held)
    rows, depth = held[0].shape
    tile = min(count, 512)

    def block(used, first):
        return pl.BlockSpec((used, tile), lambda i: (0, i + first // tile))

    outs = [halves * rows // 4 + (sum(r.shape[0] for r in riding) if k else 0) for k in range(4)]
    return pl.pallas_call(
        functools.partial(partial_kernel, halves, len(riding)),
        grid=(count // tile,),
        in_specs=[pl.BlockSpec((rows, depth), lambda i: (0, 0))] * halves
        + [block(used, first) for _, used, first in weights]
        + [block(r.shape[0], 0) for r in riding],
        out_specs=[pl.BlockSpec((out, tile), lambda i: (0, i)) for out in outs],
        out_shape=[jax.ShapeDtypeStruct((out, count), jnp.bfloat16) for out in outs],
        compiler_params=pltpu.CompilerParams(vmem_limit_bytes=VMEM),
        cost_estimate=pl.CostEstimate(flops=0, bytes_accessed=2 * count, transcendentals=0),
    )(*held, *[array for array, _, _ in weights], *riding)


def along(pairs):
    width = lax.axis_size("seq") // lax.axis_size("tp")
    return [(a * width + i, b * width + i) for a, b in pairs for i in range(width)]


def send_direct(parts):
    return [
        lax.ppermute(part, "seq", along([(a, a ^ k) for a in range(4)]))
        for k, part in enumerate(parts[1:], 1)
    ]


def sum_direct(parts, arrived):
    rows = parts[0].shape[0]
    total = parts[0].astype(jnp.float32)
    for other in arrived:
        total = total + other[:rows]
    return total.astype(jnp.bfloat16)


PLAN = (((0,), 0, 4), ((1,), 0, 4), ((0, 1), 4, 4))
RIDE = 2


def merge_tiles(panels, w_merge, ln_gain, w_kv, small):
    seq_count, tp_count = lax.axis_size("seq"), lax.axis_size("tp")
    assert tp_count == 4 and seq_count % 4 == 0
    width = seq_count // tp_count
    tiles, panel_rows, depth = panels.shape
    share = w_merge.shape[0]
    group = lax.axis_index("seq") // width
    member = lax.axis_index("seq") % width
    local = panels.reshape(tiles * panel_rows, depth)
    half = local.shape[0] // 2
    swapped = flip(local[half:], "tp", 2)
    moved = [transpose_panels(local[:half], 0), transpose_panels(swapped, 2)]
    columns = w_merge.shape[1] // 2
    small = small.reshape(-1, columns)
    extra = small.shape[0]
    received = []
    for side in range(2):
        own = w_merge[:, side * columns : (side + 1) * columns]
        if side == 1:
            own = jnp.concatenate([own, small], axis=0)
            own, _ = lax.optimization_barrier((own, swapped))
        others = []
        for offset in range(1, width):
            pairs = [
                (g * width + (i + offset) % width, g * width + i)
                for g in range(tp_count)
                for i in range(width)
            ]
            others.append(lax.ppermute(own, "seq", pairs))
        received.append(others)
    aligned = width == 2 and share % 128 == 0
    if not aligned:
        share = depth
    places = panel_base() ^ jnp.arange(4, dtype=jnp.int32) ^ group
    scalars = jnp.concatenate([places, jnp.full((4,), member, jnp.int32)])
    early, _ = lax.optimization_barrier((moved[0], swapped))
    held = [order_rows(scalars, share_panels(early), share)]
    kv = [0.0, 0.0]
    squares = [0.0, 0.0]
    everyone = None
    eighth = w_merge.shape[1] // 8
    sent = []

    def finish(step):
        halves, first, count = PLAN[step]
        merged = sum_direct(*sent[step]).astype(jnp.float32)
        at = slice(first * eighth, (first + count) * eighth)
        gained = (merged * ln_gain[at].astype(jnp.float32)[None, :]).astype(jnp.bfloat16)
        squared = jnp.sum(merged * merged, axis=1)
        product = jnp.dot(gained, w_kv[at], preferred_element_type=jnp.float32)
        for i, h in enumerate(halves):
            squares[h] = squares[h] + squared[i * half : (i + 1) * half]
            kv[h] = kv[h] + product[i * half : (i + 1) * half]

    for step, (halves, first, count) in enumerate(PLAN):
        first, count = first * eighth, count * eighth
        if step == 1:
            late, _ = lax.optimization_barrier((moved[1], sent[0][0][0]))
            held.append(order_rows(scalars, share_panels(late), share))
        riding = []
        if step == RIDE:
            received[1], _ = lax.optimization_barrier((received[1], sent[step - 1][0][0]))
            small = [small] + [other[-extra:] for other in received[1]]
            small_shape = (width,) + small[0].shape
            riding = [jnp.stack(small).reshape(-1, count)]
        side = first // columns
        inside = first - side * columns
        if aligned:
            operands = [(w_merge, share, first), (received[side][0], share, inside)]
        else:
            parts = [w_merge[:, side * columns : (side + 1) * columns]]
            parts += [other[: w_merge.shape[0]] for other in received[side]]
            parts = jnp.concatenate(parts, axis=0)
            operands = [(jnp.roll(parts, member * w_merge.shape[0], axis=0), depth, inside)]
        parts = partial_products([held[h] for h in halves], operands, count, riding)
        if step:
            before = [sent[step - 1][1][1]] + ([sent[step - 2][1][2]] if step >= 2 else [])
            parts, _ = lax.optimization_barrier((parts, before))
        sent.append((parts, send_direct(parts)))
    for step in range(len(PLAN)):
        finish(step)
    rows = sent[RIDE][0][0].shape[0]
    everyone = riding + [other[rows:] for other in sent[RIDE][1]]
    everyone = jnp.stack(everyone).reshape((4,) + small_shape)
    return jnp.concatenate(kv), jnp.concatenate(squares), everyone


def scatter_heads(kv, squares):
    tp_count = lax.axis_size("tp")
    place = lax.axis_index("tp")
    width = kv.shape[1] // tp_count
    blocks = None
    for bit in bits_of(tp_count):
        mine = (place // bit) % 2

        def half(which):
            if blocks is not None:
                paired = blocks.reshape((-1, 2) + blocks.shape[1:])
                return lax.dynamic_index_in_dim(paired, which, 1, keepdims=False)
            columns = [
                lax.dynamic_slice_in_dim(kv, (2 * i + which) * width, width, axis=1)
                for i in range(tp_count // 2)
            ]
            return jnp.stack(columns)

        arrived = flip(half(1 - mine).astype(jnp.bfloat16), "tp", bit)
        blocks = half(mine) + arrived.astype(jnp.float32)
        squares = squares + flip(squares, "tp", bit)
    return blocks[0], squares


SMALL_ROWS = 64


def pack_small(prefix_cache, sources, tiles):
    width = prefix_cache.shape[2]
    asks = jnp.stack([sources, tiles]).astype(jnp.bfloat16)
    rows = SMALL_ROWS - prefix_cache.shape[1]
    asks = jnp.pad(asks, ((0, rows - 2), (0, width - asks.shape[1])))
    return jnp.concatenate([prefix_cache[0], asks], axis=0)


def attend_kernel(
    place_ref, query_ref, prefix_ref, text_ref, pages_ref, pick_ref, seen_ref, all_ref, out_ref, vision_ref
):
    pages = pages_ref[...]
    count = pages.shape[0]

    def pick(index):
        one_hot = lax.broadcasted_iota(jnp.int32, (index.shape[0], count), 1) == index
        one_hot = jnp.where(one_hot, 1.0, 0.0).astype(jnp.bfloat16)
        return jnp.dot(one_hot, pages, preferred_element_type=jnp.float32).astype(jnp.bfloat16)

    @pl.when(pl.program_id(0) == 0)
    def _():
        vision_ref[...] = pick(all_ref[...])

    window = pick(pick_ref[0])
    keys_values = jnp.concatenate([prefix_ref[0], window, text_ref[0]], axis=0)
    text_rows = text_ref.shape[1]
    heads = keys_values.shape[1] // (2 * HD)
    query = query_ref[0]
    for head in range(heads):
        keys = keys_values[:, 2 * head * HD : (2 * head + 1) * HD]
        values = keys_values[:, (2 * head + 1) * HD : (2 * head + 2) * HD]
        stacked = jnp.concatenate(
            [
                query[:, (head * GROUP + a) * HD : (head * GROUP + a + 1) * HD]
                for a in range(GROUP)
            ],
            axis=0,
        )
        scores = lax.dot_general(
            stacked, keys, (((1,), (1,)), ((), ())), preferred_element_type=jnp.float32
        ) * (HD**-0.5)
        row = lax.broadcasted_iota(jnp.int32, scores.shape, 0) % text_rows
        column = lax.broadcasted_iota(jnp.int32, scores.shape, 1)
        text_column = column - (scores.shape[1] - text_rows)
        allowed = (text_column <= row) & (seen_ref[0] > 0)
        scores = jnp.where(allowed, scores, -1e30)
        best = jnp.max(scores, axis=1, keepdims=True)
        weights = jnp.exp(scores - best)
        total = jnp.sum(weights, axis=1, keepdims=True)
        result = jnp.dot(weights.astype(jnp.bfloat16), values, preferred_element_type=jnp.float32)
        result = (result / total).astype(jnp.bfloat16)
        for a in range(GROUP):
            out_ref[0, :, (head * GROUP + a) * HD : (head * GROUP + a + 1) * HD] = result[
                a * text_rows : (a + 1) * text_rows
            ]


def attend(place, queries, prefixes, text_kv, pages, picks, seen, all_rows):
    docs, rows, width = queries.shape
    kv_width = text_kv.shape[2]
    vision_rows = all_rows.shape[0]
    keys = seen.shape[2]
    return pl.pallas_call(
        attend_kernel,
        grid_spec=pltpu.PrefetchScalarGridSpec(
            num_scalar_prefetch=1,
            grid=(docs,),
            in_specs=[
                pl.BlockSpec((1, rows, width), lambda d, place: (d, 0, 0)),
                pl.BlockSpec((1,) + prefixes.shape[1:], lambda d, place: (place[d], 0, 0)),
                pl.BlockSpec((1, rows, kv_width), lambda d, place: (d, 0, 0)),
                pl.BlockSpec(pages.shape, lambda d, place: (0, 0)),
                pl.BlockSpec((1,) + picks.shape[1:], lambda d, place: (d, 0, 0)),
                pl.BlockSpec((1, 1, keys), lambda d, place: (d, 0, 0)),
                pl.BlockSpec(all_rows.shape, lambda d, place: (0, 0)),
            ],
            out_specs=[
                pl.BlockSpec((1, rows, width), lambda d, place: (d, 0, 0)),
                pl.BlockSpec((vision_rows, kv_width), lambda d, place: (0, 0)),
            ],
        ),
        out_shape=[
            jax.ShapeDtypeStruct(queries.shape, jnp.bfloat16),
            jax.ShapeDtypeStruct((vision_rows, kv_width), jnp.bfloat16),
        ],
        compiler_params=pltpu.CompilerParams(vmem_limit_bytes=VMEM),
        cost_estimate=pl.CostEstimate(
            flops=4 * docs * rows * width * keys,
            bytes_accessed=8 * docs * rows * width,
            transcendentals=docs * rows * keys * width // HD,
        ),
    )(place, queries, prefixes, text_kv, pages, picks, seen, all_rows)


def shards(
    panels,
    w_merge,
    ln_gain,
    w_kv,
    page_src,
    page_tile,
    doc_pages,
    prefix_id,
    prefix_cache,
    queries,
    text_kv,
):
    seq_count = lax.axis_size("seq")
    holder = lax.axis_index("seq")
    tile_count, panel_rows, _ = panels.shape
    page_count = page_src.shape[0]
    capacity = max(2, 2 * page_count // seq_count)
    sources = page_src[:, 0]

    kv, squares, small = merge_tiles(
        panels, w_merge, ln_gain, w_kv, pack_small(prefix_cache, sources, page_tile)
    )
    width = seq_count // lax.axis_size("tp")
    small = small.reshape(seq_count, SMALL_ROWS, -1)

    def place_of(index):
        group = (index // width) ^ (holder // width)
        return group * width + (index - holder) % width

    prefix_rows = prefix_cache.shape[1]
    prefixes = small[:, :prefix_rows]
    place = place_of(jnp.arange(seq_count, dtype=jnp.int32))
    asked_sources = small[:, prefix_rows, :page_count].astype(jnp.int32)[place]
    asked_tiles = small[:, prefix_rows + 1, :page_count].astype(jnp.int32)[place]
    asked = (asked_sources == holder).astype(jnp.int32)
    order = jnp.cumsum(asked, axis=1) - 1
    slots = jnp.arange(capacity, dtype=jnp.int32)
    picked = asked[:, None, :] * (order[:, None, :] == slots[None, :, None]).astype(jnp.int32)
    wanted = jnp.sum(picked * asked_tiles[:, None, :], axis=2)
    within = jnp.arange(panel_rows, dtype=jnp.int32)
    wanted_rows = (wanted.reshape(-1, 1) * panel_rows + within[None, :]).reshape(-1)
    chooser = wanted_rows[:, None] == jnp.arange(tile_count * panel_rows, dtype=jnp.int32)[None, :]
    chooser = chooser.astype(jnp.bfloat16)

    position = jnp.arange(page_count, dtype=jnp.int32)
    earlier = (sources[:, None] == sources[None, :]) & (position[None, :] < position[:, None])
    rank = jnp.sum(earlier.astype(jnp.int32), axis=1)
    arrival = sources * capacity + rank
    all_rows = (arrival[:, None] * panel_rows + within[None, :]).reshape(-1, 1)
    lengths = doc_pages[0]
    starts = jnp.cumsum(lengths) - lengths
    step = jnp.arange(MOST_PAGES, dtype=jnp.int32)
    inside = step[None, :] < lengths[:, None]
    page = jnp.minimum(starts[:, None] + step[None, :], page_count - 1)
    doc_rows = arrival[page][:, :, None] * panel_rows + within[None, None, :]
    doc_rows = jnp.where(inside[:, :, None], doc_rows, -1)
    doc_count, query_rows, _ = queries.shape
    picks = doc_rows.reshape(doc_count, -1, 1)
    seen = jnp.concatenate(
        [
            jnp.ones((doc_count, prefixes.shape[1]), jnp.int32),
            (doc_rows >= 0).reshape(doc_count, -1).astype(jnp.int32),
            jnp.ones((doc_count, query_rows), jnp.int32),
        ],
        axis=1,
    )[:, None, :]

    kv, squares = scatter_heads(kv, squares)
    row_scale = lax.rsqrt(squares / D + 1e-06)
    tile_kv = (kv * row_scale[:, None]).astype(jnp.bfloat16)
    outgoing = jnp.dot(chooser, tile_kv, preferred_element_type=jnp.float32).astype(jnp.bfloat16)
    pages = lax.all_to_all(outgoing, "seq", split_axis=0, concat_axis=0, tiled=True)
    attended, vision_kv = attend(
        place_of(prefix_id), queries, prefixes, text_kv, pages, picks, seen, all_rows
    )
    return (attended, vision_kv)


def solution(mesh):
    return jax.shard_map(
        shards,
        mesh=mesh,
        in_specs=(
            P("seq", None, "tp"),
            P("seq", "tp"),
            P("tp"),
            P("tp", None),
            P("seq", None),
            P("seq"),
            P("seq", None),
            P("seq"),
            P("seq", None, "tp"),
            P("seq", None, "tp"),
            P("seq", None, "tp"),
        ),
        out_specs=(P("seq", None, "tp"), P("seq", "tp")),
        check_vma=False,
    )
```

```python
import functools

import jax
import jax.numpy as jnp
from jax import lax
from jax.experimental import pallas as pl
from jax.experimental.pallas import tpu as pltpu
from jax.sharding import PartitionSpec as P

D = 8192
HD = 128
GROUP = 8
MOST_PAGES = 16
VMEM = 16 * 1024 * 1024


def bits_of(count):
    return [1 << bit for bit in range(count.bit_length() - 1)]


def flip(value, axis, bit):
    count = lax.axis_size(axis)
    return lax.ppermute(value, axis, [(i, i ^ bit) for i in range(count)])


def transpose_panels(local, swap):
    seq_count, tp_count = lax.axis_size("seq"), lax.axis_size("tp")
    width = seq_count // tp_count
    half = tp_count // 2
    pairs = []
    for origin in range(tp_count):
        for inner in range(width):
            for block in range(tp_count):
                source = (origin * width + inner) * tp_count + (block ^ swap)
                slot = ((origin ^ block) & 1) * half + origin // 2
                pairs.append((source, (block * width + inner) * tp_count + slot))
    return lax.ppermute(local, ("seq", "tp"), pairs)


def share_panels(moved):
    held = [moved]
    bits = bits_of(lax.axis_size("tp"))
    for bit in bits[-1:] + bits[:-1]:
        held = held + [flip(piece, "tp", bit) for piece in held]
    return held


def panel_base():
    group = lax.axis_index("seq") // (lax.axis_size("seq") // lax.axis_size("tp"))
    place = lax.axis_index("tp")
    half = lax.axis_size("tp") // 2
    return 2 * (place % half) + ((place // half) ^ (group & 1))


def order_kernel(share, scalars_ref, *refs):
    out_ref = refs[-1]
    rows, depth = refs[0].shape
    members = depth // share
    for place in range(4):
        at = pl.ds(pl.multiple_of(scalars_ref[place] * rows, rows), rows)
        for member in range(members):
            if members == 1:
                out_ref[at, :] = refs[place][...]
            else:
                source = lax.rem(scalars_ref[4] + member, members)
                columns = pl.ds(pl.multiple_of(source * share, share), share)
                out_ref[at, member * share : (member + 1) * share] = refs[place][:, columns]


def order_rows(scalars, held, share):
    rows, depth = held[0].shape
    return pl.pallas_call(
        functools.partial(order_kernel, share),
        grid_spec=pltpu.PrefetchScalarGridSpec(
            num_scalar_prefetch=1,
            grid=(1,),
            in_specs=[pl.BlockSpec((rows, depth), lambda i, scalars: (0, 0))] * 4,
            out_specs=pl.BlockSpec((4 * rows, depth), lambda i, scalars: (0, 0)),
        ),
        out_shape=jax.ShapeDtypeStruct((4 * rows, depth), jnp.bfloat16),
        compiler_params=pltpu.CompilerParams(vmem_limit_bytes=VMEM),
        cost_estimate=pl.CostEstimate(flops=0, bytes_accessed=2 * depth, transcendentals=0),
    )(scalars, *held)


def partial_kernel(halves, riding, *refs):
    rows_refs, weights_refs, out_refs = refs[:halves], refs[halves : -4 - riding], refs[-4:]
    weights = jnp.concatenate([ref[...] for ref in weights_refs], axis=0)
    for half, rows_ref in enumerate(rows_refs):
        total = jnp.dot(rows_ref[...], weights, preferred_element_type=jnp.float32)
        total = total.astype(jnp.bfloat16)
        rows = total.shape[0] // 4
        for k, out_ref in enumerate(out_refs):
            out_ref[half * rows : (half + 1) * rows] = total[k * rows : (k + 1) * rows]
    if riding:
        for out_ref in out_refs[1:]:
            out_ref[halves * rows :] = refs[-5][...]


def partial_products(held, weights, count, riding):
    halves = len(held)
    rows, depth = held[0].shape
    tile = min(count, 512)

    def block(used, first):
        return pl.BlockSpec((used, tile), lambda i: (0, i + first // tile))

    outs = [halves * rows // 4 + (sum(r.shape[0] for r in riding) if k else 0) for k in range(4)]
    return pl.pallas_call(
        functools.partial(partial_kernel, halves, len(riding)),
        grid=(count // tile,),
        in_specs=[pl.BlockSpec((rows, depth), lambda i: (0, 0))] * halves
        + [block(used, first) for _, used, first in weights]
        + [block(r.shape[0], 0) for r in riding],
        out_specs=[pl.BlockSpec((out, tile), lambda i: (0, i)) for out in outs],
        out_shape=[jax.ShapeDtypeStruct((out, count), jnp.bfloat16) for out in outs],
        compiler_params=pltpu.CompilerParams(vmem_limit_bytes=VMEM),
        cost_estimate=pl.CostEstimate(flops=0, bytes_accessed=2 * count, transcendentals=0),
    )(*held, *[array for array, _, _ in weights], *riding)


def along(pairs):
    width = lax.axis_size("seq") // lax.axis_size("tp")
    return [(a * width + i, b * width + i) for a, b in pairs for i in range(width)]


def send_direct(parts):
    return [
        lax.ppermute(part, "seq", along([(a, a ^ k) for a in range(4)]))
        for k, part in enumerate(parts[1:], 1)
    ]


def sum_direct(parts, arrived):
    rows = parts[0].shape[0]
    total = parts[0].astype(jnp.float32)
    for other in arrived:
        total = total + other[:rows]
    return total.astype(jnp.bfloat16)


PLAN = (((0,), 0, 4), ((1,), 0, 4), ((0, 1), 4, 4))
RIDE = 2


def merge_tiles(panels, w_merge, ln_gain, w_kv, small):
    seq_count, tp_count = lax.axis_size("seq"), lax.axis_size("tp")
    assert tp_count == 4 and seq_count % 4 == 0
    width = seq_count // tp_count
    tiles, panel_rows, depth = panels.shape
    share = w_merge.shape[0]
    group = lax.axis_index("seq") // width
    member = lax.axis_index("seq") % width
    local = panels.reshape(tiles * panel_rows, depth)
    half = local.shape[0] // 2
    swapped = flip(local[half:], "tp", 2)
    moved = [transpose_panels(local[:half], 0), transpose_panels(swapped, 2)]
    columns = w_merge.shape[1] // 2
    small = small.reshape(-1, columns)
    extra = small.shape[0]
    received = []
    for side in range(2):
        own = w_merge[:, side * columns : (side + 1) * columns]
        if side == 1:
            own = jnp.concatenate([own, small], axis=0)
            own, _ = lax.optimization_barrier((own, swapped))
        others = []
        for offset in range(1, width):
            pairs = [
                (g * width + (i + offset) % width, g * width + i)
                for g in range(tp_count)
                for i in range(width)
            ]
            others.append(lax.ppermute(own, "seq", pairs))
        received.append(others)
    aligned = width == 2 and share % 128 == 0
    if not aligned:
        share = depth
    places = panel_base() ^ jnp.arange(4, dtype=jnp.int32) ^ group
    scalars = jnp.concatenate([places, jnp.full((4,), member, jnp.int32)])
    early, _ = lax.optimization_barrier((moved[0], swapped))
    held = [order_rows(scalars, share_panels(early), share)]
    kv = [0.0, 0.0]
    squares = [0.0, 0.0]
    everyone = None
    eighth = w_merge.shape[1] // 8
    sent = []

    def finish(step):
        halves, first, count = PLAN[step]
        merged = sum_direct(*sent[step]).astype(jnp.float32)
        at = slice(first * eighth, (first + count) * eighth)
        gained = (merged * ln_gain[at].astype(jnp.float32)[None, :]).astype(jnp.bfloat16)
        squared = jnp.sum(merged * merged, axis=1)
        product = jnp.dot(gained, w_kv[at], preferred_element_type=jnp.float32)
        for i, h in enumerate(halves):
            squares[h] = squares[h] + squared[i * half : (i + 1) * half]
            kv[h] = kv[h] + product[i * half : (i + 1) * half]

    for step, (halves, first, count) in enumerate(PLAN):
        first, count = first * eighth, count * eighth
        if step == 1:
            late, _ = lax.optimization_barrier((moved[1], sent[0][0][0]))
            held.append(order_rows(scalars, share_panels(late), share))
        riding = []
        if step == RIDE:
            received[1], _ = lax.optimization_barrier((received[1], sent[step - 1][0][0]))
            small = [small] + [other[-extra:] for other in received[1]]
            small_shape = (width,) + small[0].shape
            riding = [jnp.stack(small).reshape(-1, count)]
        side = first // columns
        inside = first - side * columns
        if aligned:
            operands = [(w_merge, share, first), (received[side][0], share, inside)]
        else:
            parts = [w_merge[:, side * columns : (side + 1) * columns]]
            parts += [other[: w_merge.shape[0]] for other in received[side]]
            parts = jnp.concatenate(parts, axis=0)
            operands = [(jnp.roll(parts, member * w_merge.shape[0], axis=0), depth, inside)]
        parts = partial_products([held[h] for h in halves], operands, count, riding)
        if step:
            before = [sent[step - 1][1][1 if step == 1 else 0]]
            before += [sent[step - 2][1][2]] if step >= 2 else []
            parts, _ = lax.optimization_barrier((parts, before))
        sent.append((parts, send_direct(parts)))
    for step in range(len(PLAN)):
        finish(step)
    rows = sent[RIDE][0][0].shape[0]
    everyone = riding + [other[rows:] for other in sent[RIDE][1]]
    everyone = jnp.stack(everyone).reshape((4,) + small_shape)
    return jnp.concatenate(kv), jnp.concatenate(squares), everyone


def scatter_heads(kv, squares):
    tp_count = lax.axis_size("tp")
    place = lax.axis_index("tp")
    width = kv.shape[1] // tp_count
    blocks = None
    for bit in bits_of(tp_count):
        mine = (place // bit) % 2

        def half(which):
            if blocks is not None:
                paired = blocks.reshape((-1, 2) + blocks.shape[1:])
                return lax.dynamic_index_in_dim(paired, which, 1, keepdims=False)
            columns = [
                lax.dynamic_slice_in_dim(kv, (2 * i + which) * width, width, axis=1)
                for i in range(tp_count // 2)
            ]
            return jnp.stack(columns)

        arrived = flip(half(1 - mine).astype(jnp.bfloat16), "tp", bit)
        blocks = half(mine) + arrived.astype(jnp.float32)
        squares = squares + flip(squares, "tp", bit)
    return blocks[0], squares


SMALL_ROWS = 48


def pack_small(prefix_cache, sources, tiles):
    width = prefix_cache.shape[2]
    asks = jnp.stack([sources, tiles]).astype(jnp.bfloat16)
    rows = SMALL_ROWS - prefix_cache.shape[1]
    asks = jnp.pad(asks, ((0, rows - 2), (0, width - asks.shape[1])))
    return jnp.concatenate([prefix_cache[0], asks], axis=0)


def attend_kernel(
    place_ref, query_ref, prefix_ref, text_ref, pages_ref, pick_ref, seen_ref, all_ref, out_ref, vision_ref
):
    pages = pages_ref[...]
    count = pages.shape[0]

    def pick(index):
        one_hot = lax.broadcasted_iota(jnp.int32, (index.shape[0], count), 1) == index
        one_hot = jnp.where(one_hot, 1.0, 0.0).astype(jnp.bfloat16)
        return jnp.dot(one_hot, pages, preferred_element_type=jnp.float32).astype(jnp.bfloat16)

    @pl.when(pl.program_id(0) == 0)
    def _():
        vision_ref[...] = pick(all_ref[...])

    window = pick(pick_ref[0])
    keys_values = jnp.concatenate([prefix_ref[0], window, text_ref[0]], axis=0)
    text_rows = text_ref.shape[1]
    heads = keys_values.shape[1] // (2 * HD)
    query = query_ref[0]
    for head in range(heads):
        keys = keys_values[:, 2 * head * HD : (2 * head + 1) * HD]
        values = keys_values[:, (2 * head + 1) * HD : (2 * head + 2) * HD]
        stacked = jnp.concatenate(
            [
                query[:, (head * GROUP + a) * HD : (head * GROUP + a + 1) * HD]
                for a in range(GROUP)
            ],
            axis=0,
        )
        scores = lax.dot_general(
            stacked, keys, (((1,), (1,)), ((), ())), preferred_element_type=jnp.float32
        ) * (HD**-0.5)
        row = lax.broadcasted_iota(jnp.int32, scores.shape, 0) % text_rows
        column = lax.broadcasted_iota(jnp.int32, scores.shape, 1)
        text_column = column - (scores.shape[1] - text_rows)
        allowed = (text_column <= row) & (seen_ref[0] > 0)
        scores = jnp.where(allowed, scores, -1e30)
        best = jnp.max(scores, axis=1, keepdims=True)
        weights = jnp.exp(scores - best)
        total = jnp.sum(weights, axis=1, keepdims=True)
        result = jnp.dot(weights.astype(jnp.bfloat16), values, preferred_element_type=jnp.float32)
        result = (result / total).astype(jnp.bfloat16)
        for a in range(GROUP):
            out_ref[0, :, (head * GROUP + a) * HD : (head * GROUP + a + 1) * HD] = result[
                a * text_rows : (a + 1) * text_rows
            ]


def attend(place, queries, prefixes, text_kv, pages, picks, seen, all_rows):
    docs, rows, width = queries.shape
    kv_width = text_kv.shape[2]
    vision_rows = all_rows.shape[0]
    keys = seen.shape[2]
    return pl.pallas_call(
        attend_kernel,
        grid_spec=pltpu.PrefetchScalarGridSpec(
            num_scalar_prefetch=1,
            grid=(docs,),
            in_specs=[
                pl.BlockSpec((1, rows, width), lambda d, place: (d, 0, 0)),
                pl.BlockSpec((1,) + prefixes.shape[1:], lambda d, place: (place[d], 0, 0)),
                pl.BlockSpec((1, rows, kv_width), lambda d, place: (d, 0, 0)),
                pl.BlockSpec(pages.shape, lambda d, place: (0, 0)),
                pl.BlockSpec((1,) + picks.shape[1:], lambda d, place: (d, 0, 0)),
                pl.BlockSpec((1, 1, keys), lambda d, place: (d, 0, 0)),
                pl.BlockSpec(all_rows.shape, lambda d, place: (0, 0)),
            ],
            out_specs=[
                pl.BlockSpec((1, rows, width), lambda d, place: (d, 0, 0)),
                pl.BlockSpec((vision_rows, kv_width), lambda d, place: (0, 0)),
            ],
        ),
        out_shape=[
            jax.ShapeDtypeStruct(queries.shape, jnp.bfloat16),
            jax.ShapeDtypeStruct((vision_rows, kv_width), jnp.bfloat16),
        ],
        compiler_params=pltpu.CompilerParams(vmem_limit_bytes=VMEM),
        cost_estimate=pl.CostEstimate(
            flops=4 * docs * rows * width * keys,
            bytes_accessed=8 * docs * rows * width,
            transcendentals=docs * rows * keys * width // HD,
        ),
    )(place, queries, prefixes, text_kv, pages, picks, seen, all_rows)


def shards(
    panels,
    w_merge,
    ln_gain,
    w_kv,
    page_src,
    page_tile,
    doc_pages,
    prefix_id,
    prefix_cache,
    queries,
    text_kv,
):
    seq_count = lax.axis_size("seq")
    holder = lax.axis_index("seq")
    tile_count, panel_rows, _ = panels.shape
    page_count = page_src.shape[0]
    capacity = max(2, 2 * page_count // seq_count)
    sources = page_src[:, 0]

    kv, squares, small = merge_tiles(
        panels, w_merge, ln_gain, w_kv, pack_small(prefix_cache, sources, page_tile)
    )
    width = seq_count // lax.axis_size("tp")
    small = small.reshape(seq_count, SMALL_ROWS, -1)

    def place_of(index):
        group = (index // width) ^ (holder // width)
        return group * width + (index - holder) % width

    prefix_rows = prefix_cache.shape[1]
    prefixes = small[:, :prefix_rows]
    place = place_of(jnp.arange(seq_count, dtype=jnp.int32))
    asked_sources = small[:, prefix_rows, :page_count].astype(jnp.int32)[place]
    asked_tiles = small[:, prefix_rows + 1, :page_count].astype(jnp.int32)[place]
    asked = (asked_sources == holder).astype(jnp.int32)
    order = jnp.cumsum(asked, axis=1) - 1
    slots = jnp.arange(capacity, dtype=jnp.int32)
    picked = asked[:, None, :] * (order[:, None, :] == slots[None, :, None]).astype(jnp.int32)
    wanted = jnp.sum(picked * asked_tiles[:, None, :], axis=2)
    within = jnp.arange(panel_rows, dtype=jnp.int32)
    wanted_rows = (wanted.reshape(-1, 1) * panel_rows + within[None, :]).reshape(-1)
    chooser = wanted_rows[:, None] == jnp.arange(tile_count * panel_rows, dtype=jnp.int32)[None, :]
    chooser = chooser.astype(jnp.bfloat16)

    position = jnp.arange(page_count, dtype=jnp.int32)
    earlier = (sources[:, None] == sources[None, :]) & (position[None, :] < position[:, None])
    rank = jnp.sum(earlier.astype(jnp.int32), axis=1)
    arrival = sources * capacity + rank
    all_rows = (arrival[:, None] * panel_rows + within[None, :]).reshape(-1, 1)
    lengths = doc_pages[0]
    starts = jnp.cumsum(lengths) - lengths
    step = jnp.arange(MOST_PAGES, dtype=jnp.int32)
    inside = step[None, :] < lengths[:, None]
    page = jnp.minimum(starts[:, None] + step[None, :], page_count - 1)
    doc_rows = arrival[page][:, :, None] * panel_rows + within[None, None, :]
    doc_rows = jnp.where(inside[:, :, None], doc_rows, -1)
    doc_count, query_rows, _ = queries.shape
    picks = doc_rows.reshape(doc_count, -1, 1)
    seen = jnp.concatenate(
        [
            jnp.ones((doc_count, prefixes.shape[1]), jnp.int32),
            (doc_rows >= 0).reshape(doc_count, -1).astype(jnp.int32),
            jnp.ones((doc_count, query_rows), jnp.int32),
        ],
        axis=1,
    )[:, None, :]

    kv, squares = scatter_heads(kv, squares)
    row_scale = lax.rsqrt(squares / D + 1e-06)
    tile_kv = (kv * row_scale[:, None]).astype(jnp.bfloat16)
    outgoing = jnp.dot(chooser, tile_kv, preferred_element_type=jnp.float32).astype(jnp.bfloat16)
    pages = lax.all_to_all(outgoing, "seq", split_axis=0, concat_axis=0, tiled=True)
    attended, vision_kv = attend(
        place_of(prefix_id), queries, prefixes, text_kv, pages, picks, seen, all_rows
    )
    return (attended, vision_kv)


def solution(mesh):
    return jax.shard_map(
        shards,
        mesh=mesh,
        in_specs=(
            P("seq", None, "tp"),
            P("seq", "tp"),
            P("tp"),
            P("tp", None),
            P("seq", None),
            P("seq"),
            P("seq", None),
            P("seq"),
            P("seq", None, "tp"),
            P("seq", None, "tp"),
            P("seq", None, "tp"),
        ),
        out_specs=(P("seq", None, "tp"), P("seq", "tp")),
        check_vma=False,
    )
```

```python
import functools

import jax
import jax.numpy as jnp
from jax import lax
from jax.experimental import pallas as pl
from jax.experimental.pallas import tpu as pltpu
from jax.sharding import PartitionSpec as P

D = 8192
HD = 128
GROUP = 8
MOST_PAGES = 16
VMEM = 16 * 1024 * 1024


def bits_of(count):
    return [1 << bit for bit in range(count.bit_length() - 1)]


def flip(value, axis, bit):
    count = lax.axis_size(axis)
    return lax.ppermute(value, axis, [(i, i ^ bit) for i in range(count)])


def transpose_panels(local, swap):
    seq_count, tp_count = lax.axis_size("seq"), lax.axis_size("tp")
    width = seq_count // tp_count
    half = tp_count // 2
    pairs = []
    for origin in range(tp_count):
        for inner in range(width):
            for block in range(tp_count):
                source = (origin * width + inner) * tp_count + (block ^ swap)
                slot = ((origin ^ block) & 1) * half + origin // 2
                pairs.append((source, (block * width + inner) * tp_count + slot))
    return lax.ppermute(local, ("seq", "tp"), pairs)


def share_panels(moved):
    held = [moved]
    bits = bits_of(lax.axis_size("tp"))
    for bit in bits[-1:] + bits[:-1]:
        held = held + [flip(piece, "tp", bit) for piece in held]
    return held


def panel_base():
    group = lax.axis_index("seq") // (lax.axis_size("seq") // lax.axis_size("tp"))
    place = lax.axis_index("tp")
    half = lax.axis_size("tp") // 2
    return 2 * (place % half) + ((place // half) ^ (group & 1))


def order_kernel(share, scalars_ref, *refs):
    out_ref = refs[-1]
    rows, depth = refs[0].shape
    members = depth // share
    for place in range(4):
        at = pl.ds(pl.multiple_of(scalars_ref[place] * rows, rows), rows)
        for member in range(members):
            if members == 1:
                out_ref[at, :] = refs[place][...]
            else:
                source = lax.rem(scalars_ref[4] + member, members)
                columns = pl.ds(pl.multiple_of(source * share, share), share)
                out_ref[at, member * share : (member + 1) * share] = refs[place][:, columns]


def order_rows(scalars, held, share):
    rows, depth = held[0].shape
    return pl.pallas_call(
        functools.partial(order_kernel, share),
        grid_spec=pltpu.PrefetchScalarGridSpec(
            num_scalar_prefetch=1,
            grid=(1,),
            in_specs=[pl.BlockSpec((rows, depth), lambda i, scalars: (0, 0))] * 4,
            out_specs=pl.BlockSpec((4 * rows, depth), lambda i, scalars: (0, 0)),
        ),
        out_shape=jax.ShapeDtypeStruct((4 * rows, depth), jnp.bfloat16),
        compiler_params=pltpu.CompilerParams(vmem_limit_bytes=VMEM),
        cost_estimate=pl.CostEstimate(flops=0, bytes_accessed=2 * depth, transcendentals=0),
    )(scalars, *held)


def partial_kernel(halves, riding, *refs):
    rows_refs, weights_refs, out_refs = refs[:halves], refs[halves : -4 - riding], refs[-4:]
    weights = jnp.concatenate([ref[...] for ref in weights_refs], axis=0)
    for half, rows_ref in enumerate(rows_refs):
        total = jnp.dot(rows_ref[...], weights, preferred_element_type=jnp.float32)
        total = total.astype(jnp.bfloat16)
        rows = total.shape[0] // 4
        for k, out_ref in enumerate(out_refs):
            out_ref[half * rows : (half + 1) * rows] = total[k * rows : (k + 1) * rows]
    if riding:
        for out_ref in out_refs[1:]:
            out_ref[halves * rows :] = refs[-5][...]


def partial_products(held, weights, count, riding):
    halves = len(held)
    rows, depth = held[0].shape
    tile = min(count, 512)

    def block(used, first):
        return pl.BlockSpec((used, tile), lambda i: (0, i + first // tile))

    outs = [halves * rows // 4 + (sum(r.shape[0] for r in riding) if k else 0) for k in range(4)]
    return pl.pallas_call(
        functools.partial(partial_kernel, halves, len(riding)),
        grid=(count // tile,),
        in_specs=[pl.BlockSpec((rows, depth), lambda i: (0, 0))] * halves
        + [block(used, first) for _, used, first in weights]
        + [block(r.shape[0], 0) for r in riding],
        out_specs=[pl.BlockSpec((out, tile), lambda i: (0, i)) for out in outs],
        out_shape=[jax.ShapeDtypeStruct((out, count), jnp.bfloat16) for out in outs],
        compiler_params=pltpu.CompilerParams(vmem_limit_bytes=VMEM),
        cost_estimate=pl.CostEstimate(flops=0, bytes_accessed=2 * count, transcendentals=0),
    )(*held, *[array for array, _, _ in weights], *riding)


def along(pairs):
    width = lax.axis_size("seq") // lax.axis_size("tp")
    return [(a * width + i, b * width + i) for a, b in pairs for i in range(width)]


def send_direct(parts):
    return [
        lax.ppermute(part, "seq", along([(a, a ^ k) for a in range(4)]))
        for k, part in enumerate(parts[1:], 1)
    ]


def sum_direct(parts, arrived):
    rows = parts[0].shape[0]
    total = parts[0].astype(jnp.float32)
    for other in arrived:
        total = total + other[:rows]
    return total.astype(jnp.bfloat16)


PLAN = (((0,), 0, 4), ((1,), 0, 4), ((0, 1), 4, 4))
RIDE = 2


def merge_tiles(panels, w_merge, ln_gain, w_kv, small):
    seq_count, tp_count = lax.axis_size("seq"), lax.axis_size("tp")
    assert tp_count == 4 and seq_count % 4 == 0
    width = seq_count // tp_count
    tiles, panel_rows, depth = panels.shape
    share = w_merge.shape[0]
    group = lax.axis_index("seq") // width
    member = lax.axis_index("seq") % width
    local = panels.reshape(tiles * panel_rows, depth)
    half = local.shape[0] // 2
    swapped = flip(local[half:], "tp", 2)
    moved = [transpose_panels(local[:half], 0), transpose_panels(swapped, 2)]
    columns = w_merge.shape[1] // 2
    small = small.reshape(-1, columns)
    extra = small.shape[0]
    received = []
    for side in range(2):
        own = w_merge[:, side * columns : (side + 1) * columns]
        if side == 1:
            own = jnp.concatenate([own, small], axis=0)
            own, _ = lax.optimization_barrier((own, swapped))
        others = []
        for offset in range(1, width):
            pairs = [
                (g * width + (i + offset) % width, g * width + i)
                for g in range(tp_count)
                for i in range(width)
            ]
            others.append(lax.ppermute(own, "seq", pairs))
        received.append(others)
    aligned = width == 2 and share % 128 == 0
    if not aligned:
        share = depth
    places = panel_base() ^ jnp.arange(4, dtype=jnp.int32) ^ group
    scalars = jnp.concatenate([places, jnp.full((4,), member, jnp.int32)])
    early, _ = lax.optimization_barrier((moved[0], swapped))
    held = [order_rows(scalars, share_panels(early), share)]
    eighth = w_merge.shape[1] // 8
    sent = []

    def finish(step):
        _, first, count = PLAN[step]
        merged = sum_direct(*sent[step]).astype(jnp.float32)
        at = slice(first * eighth, (first + count) * eighth)
        gained = (merged * ln_gain[at].astype(jnp.float32)[None, :]).astype(jnp.bfloat16)
        squared = jnp.sum(merged * merged, axis=1)
        return squared, jnp.dot(gained, w_kv[at], preferred_element_type=jnp.float32)

    for step, (halves, first, count) in enumerate(PLAN):
        first, count = first * eighth, count * eighth
        if step == 1:
            late, _ = lax.optimization_barrier((moved[1], sent[0][0][0]))
            held.append(order_rows(scalars, share_panels(late), share))
        riding = []
        if step == RIDE:
            received[1], _ = lax.optimization_barrier((received[1], sent[step - 1][0][0]))
            small = [small] + [other[-extra:] for other in received[1]]
            small_shape = (width,) + small[0].shape
            riding = [jnp.stack(small).reshape(-1, count)]
        side = first // columns
        inside = first - side * columns
        if aligned:
            operands = [(w_merge, share, first), (received[side][0], share, inside)]
        else:
            parts = [w_merge[:, side * columns : (side + 1) * columns]]
            parts += [other[: w_merge.shape[0]] for other in received[side]]
            parts = jnp.concatenate(parts, axis=0)
            operands = [(jnp.roll(parts, member * w_merge.shape[0], axis=0), depth, inside)]
        parts = partial_products([held[h] for h in halves], operands, count, riding)
        if step:
            before = [sent[step - 1][1][1 if step == 1 else 0]]
            before += [sent[step - 2][1][2]] if step >= 2 else []
            parts, _ = lax.optimization_barrier((parts, before))
        sent.append((parts, send_direct(parts)))
    done = [finish(step) for step in range(len(PLAN))]
    squares, kv = [jnp.concatenate([done[0][i], done[1][i]], axis=0) + done[2][i] for i in range(2)]
    rows = sent[RIDE][0][0].shape[0]
    everyone = riding + [other[rows:] for other in sent[RIDE][1]]
    everyone = jnp.stack(everyone).reshape((4,) + small_shape)
    return kv, squares, everyone


def scatter_heads(kv, squares):
    tp_count = lax.axis_size("tp")
    place = lax.axis_index("tp")
    width = kv.shape[1] // tp_count
    blocks = None
    for bit in bits_of(tp_count):
        mine = (place // bit) % 2

        def half(which):
            if blocks is not None:
                paired = blocks.reshape((-1, 2) + blocks.shape[1:])
                return lax.dynamic_index_in_dim(paired, which, 1, keepdims=False)
            columns = [
                lax.dynamic_slice_in_dim(kv, (2 * i + which) * width, width, axis=1)
                for i in range(tp_count // 2)
            ]
            return jnp.stack(columns)

        arrived = flip(half(1 - mine).astype(jnp.bfloat16), "tp", bit)
        blocks = half(mine) + arrived.astype(jnp.float32)
        squares = squares + flip(squares, "tp", bit)
    return blocks[0], squares


SMALL_ROWS = 48


def pack_small(prefix_cache, sources, tiles):
    width = prefix_cache.shape[2]
    asks = jnp.stack([sources, tiles]).astype(jnp.bfloat16)
    rows = SMALL_ROWS - prefix_cache.shape[1]
    asks = jnp.pad(asks, ((0, rows - 2), (0, width - asks.shape[1])))
    return jnp.concatenate([prefix_cache[0], asks], axis=0)


def attend_kernel(
    place_ref, query_ref, prefix_ref, text_ref, pages_ref, pick_ref, seen_ref, all_ref, out_ref, vision_ref
):
    pages = pages_ref[...]
    count = pages.shape[0]

    def pick(index):
        one_hot = lax.broadcasted_iota(jnp.int32, (index.shape[0], count), 1) == index
        one_hot = jnp.where(one_hot, 1.0, 0.0).astype(jnp.bfloat16)
        return jnp.dot(one_hot, pages, preferred_element_type=jnp.float32).astype(jnp.bfloat16)

    @pl.when(pl.program_id(0) == 0)
    def _():
        vision_ref[...] = pick(all_ref[...])

    window = pick(pick_ref[0])
    keys_values = jnp.concatenate([prefix_ref[0], window, text_ref[0]], axis=0)
    text_rows = text_ref.shape[1]
    heads = keys_values.shape[1] // (2 * HD)
    query = query_ref[0]
    for head in range(heads):
        keys = keys_values[:, 2 * head * HD : (2 * head + 1) * HD]
        values = keys_values[:, (2 * head + 1) * HD : (2 * head + 2) * HD]
        stacked = jnp.concatenate(
            [
                query[:, (head * GROUP + a) * HD : (head * GROUP + a + 1) * HD]
                for a in range(GROUP)
            ],
            axis=0,
        )
        scores = lax.dot_general(
            stacked, keys, (((1,), (1,)), ((), ())), preferred_element_type=jnp.float32
        ) * (HD**-0.5)
        row = lax.broadcasted_iota(jnp.int32, scores.shape, 0) % text_rows
        column = lax.broadcasted_iota(jnp.int32, scores.shape, 1)
        text_column = column - (scores.shape[1] - text_rows)
        allowed = (text_column <= row) & (seen_ref[0] > 0)
        scores = jnp.where(allowed, scores, -1e30)
        best = jnp.max(scores, axis=1, keepdims=True)
        weights = jnp.exp(scores - best)
        total = jnp.sum(weights, axis=1, keepdims=True)
        result = jnp.dot(weights.astype(jnp.bfloat16), values, preferred_element_type=jnp.float32)
        result = (result / total).astype(jnp.bfloat16)
        for a in range(GROUP):
            out_ref[0, :, (head * GROUP + a) * HD : (head * GROUP + a + 1) * HD] = result[
                a * text_rows : (a + 1) * text_rows
            ]


def attend(place, queries, prefixes, text_kv, pages, picks, seen, all_rows):
    docs, rows, width = queries.shape
    kv_width = text_kv.shape[2]
    vision_rows = all_rows.shape[0]
    keys = seen.shape[2]
    return pl.pallas_call(
        attend_kernel,
        grid_spec=pltpu.PrefetchScalarGridSpec(
            num_scalar_prefetch=1,
            grid=(docs,),
            in_specs=[
                pl.BlockSpec((1, rows, width), lambda d, place: (d, 0, 0)),
                pl.BlockSpec((1,) + prefixes.shape[1:], lambda d, place: (place[d], 0, 0)),
                pl.BlockSpec((1, rows, kv_width), lambda d, place: (d, 0, 0)),
                pl.BlockSpec(pages.shape, lambda d, place: (0, 0)),
                pl.BlockSpec((1,) + picks.shape[1:], lambda d, place: (d, 0, 0)),
                pl.BlockSpec((1, 1, keys), lambda d, place: (d, 0, 0)),
                pl.BlockSpec(all_rows.shape, lambda d, place: (0, 0)),
            ],
            out_specs=[
                pl.BlockSpec((1, rows, width), lambda d, place: (d, 0, 0)),
                pl.BlockSpec((vision_rows, kv_width), lambda d, place: (0, 0)),
            ],
        ),
        out_shape=[
            jax.ShapeDtypeStruct(queries.shape, jnp.bfloat16),
            jax.ShapeDtypeStruct((vision_rows, kv_width), jnp.bfloat16),
        ],
        compiler_params=pltpu.CompilerParams(vmem_limit_bytes=VMEM),
        cost_estimate=pl.CostEstimate(
            flops=4 * docs * rows * width * keys,
            bytes_accessed=8 * docs * rows * width,
            transcendentals=docs * rows * keys * width // HD,
        ),
    )(place, queries, prefixes, text_kv, pages, picks, seen, all_rows)


def shards(
    panels,
    w_merge,
    ln_gain,
    w_kv,
    page_src,
    page_tile,
    doc_pages,
    prefix_id,
    prefix_cache,
    queries,
    text_kv,
):
    seq_count = lax.axis_size("seq")
    holder = lax.axis_index("seq")
    tile_count, panel_rows, _ = panels.shape
    page_count = page_src.shape[0]
    capacity = max(2, 2 * page_count // seq_count)
    sources = page_src[:, 0]

    kv, squares, small = merge_tiles(
        panels, w_merge, ln_gain, w_kv, pack_small(prefix_cache, sources, page_tile)
    )
    width = seq_count // lax.axis_size("tp")
    small = small.reshape(seq_count, SMALL_ROWS, -1)

    def place_of(index):
        group = (index // width) ^ (holder // width)
        return group * width + (index - holder) % width

    prefix_rows = prefix_cache.shape[1]
    prefixes = small[:, :prefix_rows]
    place = place_of(jnp.arange(seq_count, dtype=jnp.int32))
    asked_sources = small[:, prefix_rows, :page_count].astype(jnp.int32)[place]
    asked_tiles = small[:, prefix_rows + 1, :page_count].astype(jnp.int32)[place]
    asked = (asked_sources == holder).astype(jnp.int32)
    order = jnp.cumsum(asked, axis=1) - 1
    slots = jnp.arange(capacity, dtype=jnp.int32)
    picked = asked[:, None, :] * (order[:, None, :] == slots[None, :, None]).astype(jnp.int32)
    wanted = jnp.sum(picked * asked_tiles[:, None, :], axis=2)
    within = jnp.arange(panel_rows, dtype=jnp.int32)
    wanted_rows = (wanted.reshape(-1, 1) * panel_rows + within[None, :]).reshape(-1)
    chooser = wanted_rows[:, None] == jnp.arange(tile_count * panel_rows, dtype=jnp.int32)[None, :]
    chooser = chooser.astype(jnp.bfloat16)

    position = jnp.arange(page_count, dtype=jnp.int32)
    earlier = (sources[:, None] == sources[None, :]) & (position[None, :] < position[:, None])
    rank = jnp.sum(earlier.astype(jnp.int32), axis=1)
    arrival = sources * capacity + rank
    all_rows = (arrival[:, None] * panel_rows + within[None, :]).reshape(-1, 1)
    lengths = doc_pages[0]
    starts = jnp.cumsum(lengths) - lengths
    step = jnp.arange(MOST_PAGES, dtype=jnp.int32)
    inside = step[None, :] < lengths[:, None]
    page = jnp.minimum(starts[:, None] + step[None, :], page_count - 1)
    doc_rows = arrival[page][:, :, None] * panel_rows + within[None, None, :]
    doc_rows = jnp.where(inside[:, :, None], doc_rows, -1)
    doc_count, query_rows, _ = queries.shape
    picks = doc_rows.reshape(doc_count, -1, 1)
    seen = jnp.concatenate(
        [
            jnp.ones((doc_count, prefixes.shape[1]), jnp.int32),
            (doc_rows >= 0).reshape(doc_count, -1).astype(jnp.int32),
            jnp.ones((doc_count, query_rows), jnp.int32),
        ],
        axis=1,
    )[:, None, :]

    kv, squares = scatter_heads(kv, squares)
    row_scale = lax.rsqrt(squares / D + 1e-06)
    tile_kv = (kv * row_scale[:, None]).astype(jnp.bfloat16)
    outgoing = jnp.dot(chooser, tile_kv, preferred_element_type=jnp.float32).astype(jnp.bfloat16)
    pages = lax.all_to_all(outgoing, "seq", split_axis=0, concat_axis=0, tiled=True)
    attended, vision_kv = attend(
        place_of(prefix_id), queries, prefixes, text_kv, pages, picks, seen, all_rows
    )
    return (attended, vision_kv)


def solution(mesh):
    return jax.shard_map(
        shards,
        mesh=mesh,
        in_specs=(
            P("seq", None, "tp"),
            P("seq", "tp"),
            P("tp"),
            P("tp", None),
            P("seq", None),
            P("seq"),
            P("seq", None),
            P("seq"),
            P("seq", None, "tp"),
            P("seq", None, "tp"),
            P("seq", None, "tp"),
        ),
        out_specs=(P("seq", None, "tp"), P("seq", "tp")),
        check_vma=False,
    )
```
